128 devices in a mesh: dp: 16 (over z, x_hi, core), tensor: 8 (over y, x_lo).
Axes of the slice: x: 4 (x_hi: 2, x_lo: 2; x = x_hi * 2 + x_lo), y: 4, z: 4, core: 2. Of those that a mesh axis runs over, the one named last changes fastest.
Arguments:
- tokens: bfloat16 [32768, 1024], P(('dp', 'tensor')), may hold values from -6 to 6
- attn_gain: bfloat16 [1024], replicated, may hold values from 0.099609375 to 1.8984375
- w_query: bfloat16 [1024, 2048], P('dp', 'tensor'), may hold values from -0.1875 to 0.1875
- key_weight: bfloat16 [1024, 1024], P('dp', 'tensor'), may hold values from -0.1875 to 0.1875
- value_weight: bfloat16 [1024, 1024], P('dp', 'tensor'), may hold values from -0.1875 to 0.1875
- query_gain: bfloat16 [128], replicated, may hold values from 0.099609375 to 1.8984375
- key_gain: bfloat16 [128], replicated, may hold values from 0.099609375 to 1.8984375
- w_out: bfloat16 [2048, 1024], P('tensor', 'dp'), may hold values from -0.5 to 0.5
- mlp_gain: bfloat16 [1024], replicated, may hold values from 0.099609375 to 1.8984375
- w_gate: bfloat16 [1024, 3072], P('dp', 'tensor'), may hold values from -0.1875 to 0.1875
- w_up: bfloat16 [1024, 3072], P('dp', 'tensor'), may hold values from -0.1875 to 0.1875
- w_down: bfloat16 [3072, 1024], P('tensor', 'dp'), may hold values from -0.109375 to 0.109375
- out_cotangent: bfloat16 [32768, 1024], P(('dp', 'tensor')), may hold values from -6 to 6
Outputs:
- layer_out: bfloat16 [32768, 1024], P(('dp', 'tensor'))
- input_grad: float32 [32768, 1024], P(('dp', 'tensor'))
- attn_gain_grad: float32 [1024], replicated
- w_query_grad: float32 [1024, 2048], P('dp', 'tensor')
- w_key_grad: float32 [1024, 1024], P('dp', 'tensor')
- w_value_grad: float32 [1024, 1024], P('dp', 'tensor')
- query_gain_grad: float32 [128], replicated
- key_gain_grad: float32 [128], replicated
- w_out_grad: float32 [2048, 1024], P('tensor', 'dp')
- mlp_gain_grad: float32 [1024], replicated
- w_gate_grad: float32 [1024, 3072], P('dp', 'tensor')
- w_up_grad: float32 [1024, 3072], P('dp', 'tensor')
- w_down_grad: float32 [3072, 1024], P('tensor', 'dp')
The draws below stay inside these ranges and needn't reach their ends.
All inputs are finite; a program needn't handle non-finite values.
Results may differ from the reference program's by a relative error of at most 0.025.
Values may be sent and summed in bfloat16 or wider, within the bound.
A program may use at most 128 MiB of HBM per device.

```python
import math
import jax
import jax.numpy as jnp
from jax import lax

MODEL_WIDTH = 1024
FF = 3072
QUERY_HEADS = 16
KEY_VALUE_HEADS = 8
HEAD_SIZE = 128
SEQUENCE_LENGTH = 1024
TOKENS = 32768


def levels(key, shape, split, smallest, high):
    gain, own = 1.0, jax.random.fold_in(key, 6)
    for axis_at, shards_of in split:
        draws = jnp.exp(jax.random.uniform(jax.random.fold_in(own, axis_at), (shards_of,), jnp.float32, smallest / len(split), high / len(split)))
        gain = gain * jnp.repeat(draws, shape[axis_at] // shards_of).reshape([-1 if axis == axis_at else 1 for axis in range(len(shape))])
    return gain


def gaussian(rng, extent, width, most, pieces=(), kind=jnp.bfloat16):
    array = jax.random.normal(rng, extent, jnp.float32) * width
    if len(pieces) > 0:
        array = levels(rng, extent, pieces, -0.22, 0.18) * array
    return jnp.clip(array, min=-most, max=most).astype(kind)


def setup_inputs(seed: int = 0) -> dict:
    streams_of = jax.random.split(jax.random.key(seed), 14)
    tokens = gaussian(streams_of[0], (TOKENS, MODEL_WIDTH), 1.0, 6.0, ((0, 128),))
    attn_gain = jnp.clip(1.0 + 0.18 * jax.random.normal(streams_of[1], (MODEL_WIDTH,), jnp.float32), 0.099609375, 1.8984375).astype(jnp.bfloat16)
    w_query = gaussian(streams_of[2], (MODEL_WIDTH, QUERY_HEADS * HEAD_SIZE), MODEL_WIDTH ** -0.5, 0.1875, ((0, 16), (1, 8)))
    key_weight = gaussian(streams_of[3], (MODEL_WIDTH, KEY_VALUE_HEADS * HEAD_SIZE), MODEL_WIDTH ** -0.5, 0.1875, ((0, 16), (1, 8)))
    value_weight = gaussian(streams_of[4], (MODEL_WIDTH, KEY_VALUE_HEADS * HEAD_SIZE), MODEL_WIDTH ** -0.5, 0.1875, ((0, 16), (1, 8)))
    query_gain = jnp.clip(1.0 + 0.18 * jax.random.normal(streams_of[5], (HEAD_SIZE,), jnp.float32), 0.099609375, 1.8984375).astype(jnp.bfloat16)
    key_gain = jnp.clip(1.0 + 0.18 * jax.random.normal(streams_of[6], (HEAD_SIZE,), jnp.float32), 0.099609375, 1.8984375).astype(jnp.bfloat16)
    w_out = gaussian(streams_of[7], (QUERY_HEADS * HEAD_SIZE, MODEL_WIDTH), (QUERY_HEADS * HEAD_SIZE // 16) ** -0.5, 0.5, ((0, 8), (1, 16)))
    mlp_gain = jnp.clip(1.0 + 0.18 * jax.random.normal(streams_of[8], (MODEL_WIDTH,), jnp.float32), 0.099609375, 1.8984375).astype(jnp.bfloat16)
    w_gate = gaussian(streams_of[9], (MODEL_WIDTH, FF), MODEL_WIDTH ** -0.5, 0.1875, ((0, 16), (1, 8)))
    w_up = gaussian(streams_of[10], (MODEL_WIDTH, FF), MODEL_WIDTH ** -0.5, 0.1875, ((0, 16), (1, 8)))
    w_down = gaussian(streams_of[11], (FF, MODEL_WIDTH), FF ** -0.5, 0.109375, ((0, 8), (1, 16)))
    out_cotangent = gaussian(streams_of[12], (TOKENS, MODEL_WIDTH), 1.0, 6.0, ((0, 128),))
    return {"tokens": tokens, "attn_gain": attn_gain, "w_query": w_query, "key_weight": key_weight, "value_weight": value_weight, "query_gain": query_gain, "key_gain": key_gain, "w_out": w_out, "mlp_gain": mlp_gain, "w_gate": w_gate, "w_up": w_up, "w_down": w_down, "out_cotangent": out_cotangent}


eps_norm = 1e-06
rope_base = 1000000.0

@jax.custom_vjp
def low(v):
    return lax.optimization_barrier(v.astype(jnp.bfloat16)).astype(jnp.float32)

@jax.custom_vjp
def reduced_backward(v):
    return v

def low_keep(v):
    return (low(v), None)

def low_pass(kept, grad):
    return (grad,)

def back_keep(v):
    return (v, None)

def back_low(kept, grad):
    return (low(grad),)
low.defvjp(low_keep, low_pass)
reduced_backward.defvjp(back_keep, back_low)

def precise_product(first_op, second_op):
    return jnp.dot(first_op, second_op, precision=lax.Precision.HIGHEST, preferred_element_type=jnp.float32)

def rms_scale(values):
    return lax.rsqrt(lax.optimization_barrier(jnp.mean(values * values, axis=-1, keepdims=True)) + eps_norm)

def rope_tables(token_length, head_dim):
    half_dim = head_dim // 2
    position = lax.broadcasted_iota(jnp.float32, (token_length, half_dim), 0)
    channel = lax.broadcasted_iota(jnp.float32, (token_length, half_dim), 1)
    angle_rad = position * jnp.exp(channel * (-2.0 * math.log(rope_base) / head_dim))
    return (jnp.cos(angle_rad)[:, None, :], jnp.sin(angle_rad)[:, None, :])

def rotate(values, cos_table, sin_table):
    half_dim = values.shape[-1] // 2
    first_part = values[..., :half_dim]
    second_part = values[..., half_dim:]
    return jnp.concatenate([first_part * cos_table - second_part * sin_table, second_part * cos_table + first_part * sin_table], axis=-1)

def attend_sequence(operands):
    query_sequence, key_seq, value_seq = operands
    token_length = query_sequence.shape[0]
    grouped_heads = query_sequence.reshape(token_length, KEY_VALUE_HEADS, QUERY_HEADS // KEY_VALUE_HEADS, HEAD_SIZE)
    scores = jnp.einsum('ikgd,jkd->kgij', grouped_heads, key_seq, precision=lax.Precision.HIGHEST) * (1.0 / math.sqrt(HEAD_SIZE))
    scores = reduced_backward(scores)
    row_pos = lax.broadcasted_iota(jnp.int32, (token_length, token_length), 0)
    col_pos = lax.broadcasted_iota(jnp.int32, (token_length, token_length), 1)
    scores = jnp.where(col_pos <= row_pos, scores, -1e+30)
    top_score = lax.optimization_barrier(jnp.max(scores, axis=-1, keepdims=True))
    exp_scores = jnp.exp(scores - top_score)
    prob_rows = exp_scores / lax.optimization_barrier(jnp.sum(exp_scores, axis=-1, keepdims=True))
    mixed_rows = jnp.einsum('kgij,jkd->ikgd', low(prob_rows), value_seq, precision=lax.Precision.HIGHEST)
    return mixed_rows.reshape(token_length, QUERY_HEADS * HEAD_SIZE)

def layer_forward(rows_x, params):
    attn_gain, w_query, key_weight, value_weight, query_gain, key_gain, w_out, mlp_gain, w_gate, w_up, w_down = params
    row_count = rows_x.shape[0]
    sequence_count = row_count // SEQUENCE_LENGTH
    attention_input = low(rows_x * rms_scale(rows_x) * attn_gain)
    query_pre = reduced_backward(precise_product(attention_input, w_query)).reshape(sequence_count, SEQUENCE_LENGTH, QUERY_HEADS, HEAD_SIZE)
    key_before_norm = reduced_backward(precise_product(attention_input, key_weight)).reshape(sequence_count, SEQUENCE_LENGTH, KEY_VALUE_HEADS, HEAD_SIZE)
    value_before_norm = reduced_backward(precise_product(attention_input, value_weight)).reshape(sequence_count, SEQUENCE_LENGTH, KEY_VALUE_HEADS, HEAD_SIZE)
    query_norm = query_pre * rms_scale(query_pre) * query_gain
    key_norm = key_before_norm * rms_scale(key_before_norm) * key_gain
    cos_table, sin_table = rope_tables(SEQUENCE_LENGTH, HEAD_SIZE)
    query_rot = low(rotate(query_norm, cos_table, sin_table))
    key_rot = low(rotate(key_norm, cos_table, sin_table))
    value_rot = low(value_before_norm)
    mixed_all = lax.map(jax.checkpoint(attend_sequence), (query_rot, key_rot, value_rot))
    mixed_all = low(reduced_backward(mixed_all.reshape(row_count, QUERY_HEADS * HEAD_SIZE)))
    resid = rows_x + reduced_backward(precise_product(mixed_all, w_out))
    mlp_in = low(resid * rms_scale(resid) * mlp_gain)
    gate_pre = reduced_backward(precise_product(mlp_in, w_gate))
    up_pre = reduced_backward(precise_product(mlp_in, w_up))
    hidden_act = low(jax.nn.sigmoid(gate_pre) * gate_pre * up_pre)
    return resid + precise_product(hidden_act, w_down)

def reference(tokens, attn_gain, w_query, key_weight, value_weight, query_gain, key_gain, w_out, mlp_gain, w_gate, w_up, w_down, out_cotangent):
    params = tuple((item.astype(jnp.float32) for item in (attn_gain, w_query, key_weight, value_weight, query_gain, key_gain, w_out, mlp_gain, w_gate, w_up, w_down)))
    total_seqs = tokens.shape[0] // SEQUENCE_LENGTH
    seq_per_span = math.gcd(total_seqs, max(1, 4096 // SEQUENCE_LENGTH))
    span_count = total_seqs // seq_per_span
    span_rows = seq_per_span * SEQUENCE_LENGTH
    token_spans = tokens.astype(jnp.float32).reshape(span_count, span_rows, tokens.shape[1])
    cot_spans = out_cotangent.astype(jnp.float32).reshape(span_count, span_rows, tokens.shape[1])

    def one_span(running, span_pair):
        rows_x, rows_cot = span_pair
        out_span, pullback = jax.vjp(layer_forward, rows_x, params)
        input_part, param_part = pullback(rows_cot)
        running = tuple((total + part for total, part in zip(running, param_part)))
        return (running, (out_span.astype(jnp.bfloat16), input_part))
    start_sums = tuple((jnp.zeros(item.shape, jnp.float32) for item in params))
    grad_sums, (out_rows, input_rows) = lax.scan(one_span, start_sums, (token_spans, cot_spans))
    layer_out = out_rows.reshape(tokens.shape)
    input_grad = input_rows.reshape(tokens.shape)
    return (layer_out, input_grad, grad_sums[0], grad_sums[1], grad_sums[2], grad_sums[3], grad_sums[4], grad_sums[5], grad_sums[6], grad_sums[7], grad_sums[8], grad_sums[9], grad_sums[10])
```

```python
import math

import jax
import jax.numpy as jnp
import numpy as np
from jax import lax
from jax.experimental import pallas as pl
from jax.experimental.pallas import tpu as pltpu
from jax.sharding import PartitionSpec as P

HEAD = 128
SEQ = 1024
WIDTH = 1024
ROWS = 256
QKV = 512
AW = 768
HID = 384
MW = 3 * HID
EPS = 1e-06
ROPE_BASE = 1000000.0
EXP_SCALE = math.log2(math.e) / math.sqrt(HEAD)
SCORE_SCALE = 1.0 / math.sqrt(HEAD)
MESH = pl.DeviceIdType.MESH
F32 = jnp.float32
BF16 = jnp.bfloat16


def dot_nn(a, b):
    return jnp.dot(a, b, preferred_element_type=F32)


def dot_nt(a, b):
    return lax.dot_general(a, b, (((1,), (1,)), ((), ())), preferred_element_type=F32)


def dot_tn(a, b):
    return lax.dot_general(a, b, (((0,), (0,)), ((), ())), preferred_element_type=F32)


def reorder(v):
    return jnp.concatenate([v[:, :512], v[:, 768:], v[:, 512:768]], axis=1)


def row_scale(v):
    return lax.rsqrt(jnp.mean(v * v, axis=-1, keepdims=True) + EPS)


def flip(bit):
    return 1 - bit


SCRATCH = {
    "w_attn": ((2, 2, 2, 2, 2, 64, AW), BF16),
    "w_mlp": ((2, 2, 2, 2, 2, 64, MW), BF16),
    "a_full": ((4, ROWS, WIDTH), BF16),
    "m_full": ((4, ROWS, WIDTH), BF16),
    "c_full": ((4, ROWS, WIDTH), BF16),
    "d_full": ((4, ROWS, WIDTH), BF16),
    "qkp": ((2, 4, ROWS, 384), F32),
    "qs": ((2, 4, 512, HEAD), BF16),
    "ks": ((2, 4, ROWS, HEAD), BF16),
    "kt": ((2, 4, HEAD, ROWS), BF16),
    "vs": ((2, 4, ROWS, HEAD), BF16),
    "vt": ((2, 4, HEAD, ROWS), BF16),
    "os": ((2, 4, 512, HEAD), BF16),
    "linv": ((2, 4, 8, 512), F32),
    "delta": ((2, 4, 8, 512), F32),
    "dos": ((2, 4, 512, HEAD), BF16),
    "dk": ((2, 4, ROWS, HEAD), F32),
    "dv": ((2, 4, ROWS, HEAD), F32),
    "hid": ((2, 4, ROWS, HID), BF16),
    "dgu": ((2, 4, ROWS, 2 * HID), BF16),
    "own": ((ROWS, WIDTH), F32),
    "own_down": ((ROWS, WIDTH), F32),
    "resid": ((ROWS, WIDTH), F32),
    "stage": ((3, ROWS, WIDTH), BF16),
    "stage_down": ((3, ROWS, WIDTH), BF16),
    "rs_q_d": ((2, 128, WIDTH), BF16),
    "rs_q_n": ((2, ROWS, WIDTH), BF16),
    "rs_m": ((3, ROWS, WIDTH), BF16),
    "rs_d": ((3, ROWS, WIDTH), BF16),
    "gains": ((8, WIDTH), F32),
    "gain_in": ((7, 8, WIDTH), F32),
    "core_in": ((2, 2, 2, 2, 1, 64, AW), BF16),
    "mlp_x": ((2, 64, MW), BF16),
    "mlp_c": ((64, MW), F32),
    "attn_x": ((64, AW), F32),
    "attn_sum": ((64, AW), F32),
    "mlp_sum": ((2, 64, MW), F32),
}
AXES = {"xo": 3, "yo": 0, "za": 2, "zb": 1}
ORDER = ["xo", "yo", "za", "zb"]


def part_axes(part):
    return [ORDER[(part + step) % 4] for step in range(4)]


def cube_shape(part, step, cores, width):
    shape = [1, 1, 1, 1]
    for axis in part_axes(part)[:step]:
        shape[AXES[axis]] = 2
    return (*shape, cores, 16, width)


for _part in range(4):
    for _step in range(4):
        SCRATCH[f"ra_{_part}_{_step}"] = (cube_shape(_part, _step, 1, AW), BF16)
        SCRATCH[f"rm_{_part}_{_step}"] = (cube_shape(_part, _step, 2, MW), BF16)

NAMES = list(SCRATCH)
N_SEM = 200
INPUTS = ["tok", "cot", "pa", "pm", "ag", "mg", "qg", "kg", "cosf", "sinf"]
OUTPUTS = ["layer_out", "input_grad", "d_attn", "d_mlp", "d_gain"]


class Refs:
    pass


def kernel(*refs):
    r = Refs()
    names = INPUTS + OUTPUTS + NAMES
    for name, ref in zip(names, refs):
        setattr(r, name, ref)
    ssem, rsem = refs[len(names)], refs[len(names) + 1]

    dp = lax.axis_index("dp")
    tn = lax.axis_index("tensor")
    z = dp // 4
    x_hi = (dp // 2) % 2
    core = dp % 2
    y = tn // 2
    x_lo = tn % 2
    y_lo = y % 2
    y_hi = y // 2
    gz = jnp.where(z < 2, z, 5 - z)
    own_bit = {"xo": x_hi, "yo": y_hi, "za": gz % 2, "zb": gz // 2}
    nbr = {
        "c": (dp + 1 - 2 * core, tn),
        "x": (dp, tn + 1 - 2 * x_lo),
        "y": (dp, tn + 2 - 4 * y_lo),
        "xo": (dp + 2 - 4 * x_hi, tn + 1 - 2 * x_lo),
        "yo": (dp, (3 - y) * 2 + x_lo),
        "za": (dp + 4 - 8 * (z % 2), tn),
        "zb": (dp + 4 * (3 - 2 * z), tn),
    }
    b_own = y_lo * 2 + x_lo
    b_x = y_lo * 2 + flip(x_lo)
    b_y = flip(y_lo) * 2 + x_lo
    b_d = flip(y_lo) * 2 + flip(x_lo)
    i_own = y_lo * 2 + core
    i_c = y_lo * 2 + flip(core)
    i_y = flip(y_lo) * 2 + core
    i_yc = flip(y_lo) * 2 + flip(core)

    counter = [0]
    unsent = []

    def rcopy(src, dst, to):
        i = counter[0]
        counter[0] += 1
        return pltpu.make_async_remote_copy(
            src_ref=src,
            dst_ref=dst,
            send_sem=ssem.at[i],
            recv_sem=rsem.at[i],
            device_id=nbr[to],
            device_id_type=MESH,
        )

    def send(src, dst, to):
        copy = rcopy(src, dst, to)
        copy.start()
        unsent.append(copy)
        return copy

    def flush():
        while unsent:
            unsent.pop().wait_send()

    def own_slot(cores):
        return (
            pl.ds(own_bit["yo"], 1),
            pl.ds(own_bit["zb"], 1),
            pl.ds(own_bit["za"], 1),
            pl.ds(own_bit["xo"], 1),
            cores,
        )

    def slots(full, current, cores):
        index = [None] * 4
        for axis in ORDER:
            if axis in full:
                index[AXES[axis]] = pl.ds(0, 2)
            else:
                bit = own_bit[axis]
                if current is not None and current == axis:
                    bit = flip(bit)
                index[AXES[axis]] = pl.ds(bit, 1)
        return (*index, cores)

    both = pl.ds(0, 2)
    lane = pl.ds(core, 1)

    def gather_step(w, step, cores):
        copies = []
        for part in range(4):
            axes = part_axes(part)
            rows = pl.ds(16 * part, 16)
            view = w.at[(*slots(axes[:step], None, cores), rows)]
            copies.append(send(view, view, axes[step]))
        return copies

    def wait_recv(copies):
        for copy in copies:
            copy.wait_recv()

    def core_send(w, late):
        copies = []
        for part in range(4):
            axes = part_axes(part)
            rows = pl.ds(16 * part, 16)
            current = axes[3] if late else None
            view = w.at[(*slots(axes[:3], current, lane), rows)]
            copies.append(send(view, view, "c"))
        return copies

    def reduce_send(w, bufs, step, cores):
        copies = []
        for part in range(4):
            axes = part_axes(part)
            rows = pl.ds(16 * part, 16)
            view = w.at[(*slots(axes[:step], axes[step], cores), rows)]
            copies.append(send(view, getattr(r, f"{bufs}_{part}_{step}"), axes[step]))
        return copies

    def reduce_add(w, bufs, step, cores, copies):
        for part in range(4):
            axes = part_axes(part)
            rows = pl.ds(16 * part, 16)
            index = (*slots(axes[:step], None, cores), rows)
            copies[part].wait_recv()
            total = w[index].astype(F32) + getattr(r, f"{bufs}_{part}_{step}")[...].astype(F32)
            w[index] = total.astype(BF16)

    barrier = pltpu.get_barrier_semaphore()
    for to in nbr:
        pl.semaphore_signal(barrier, inc=1, device_id=nbr[to], device_id_type=MESH)
    pl.semaphore_wait(barrier, len(nbr))

    swap = rcopy(r.pa, r.w_attn.at[(own_bit["yo"], own_bit["zb"], own_bit["za"], own_bit["xo"], core)], "x")
    mlp_own = r.w_mlp.at[(own_bit["yo"], own_bit["zb"], own_bit["za"], own_bit["xo"], core)]
    mlp_pair = r.w_mlp.at[(own_bit["yo"], own_bit["zb"], own_bit["za"], own_bit["xo"])]
    mlp_to_core = rcopy(r.pm, mlp_own, "c")
    mlp_to_x = rcopy(mlp_pair, mlp_pair, "x")
    carries = core == x_lo
    lends = core != x_lo

    @pl.when(x_hi == 1)
    def _():
        swap.start()

    @pl.when(lends)
    def _():
        mlp_to_core.start()

    @pl.when(x_hi == 0)
    def _():
        r.w_attn[own_slot(lane)] = r.pa[...].reshape(1, 1, 1, 1, 1, 64, AW)

    @pl.when(carries)
    def _():
        r.w_mlp[own_slot(lane)] = r.pm[...].reshape(1, 1, 1, 1, 1, 64, MW)

    attn_gain = reorder(r.ag[...].astype(F32))
    mlp_gain = reorder(r.mg[...].astype(F32))
    query_gain = r.qg[...].astype(F32)
    key_gain = r.kg[...].astype(F32)
    rows_x = reorder(r.tok[...].astype(F32))
    r.a_full[b_own] = (rows_x * row_scale(rows_x) * attn_gain).astype(BF16)

    def square_gather(buf):
        def half(block, n):
            return buf.at[block, pl.ds(128 * n, 128)]

        x0 = send(half(b_own, 0), half(b_own, 0), "x")
        y1 = send(half(b_own, 1), half(b_own, 1), "y")
        x1 = send(half(b_own, 1), half(b_own, 1), "x")
        y0 = send(half(b_own, 0), half(b_own, 0), "y")

        def forward():
            x0.wait_recv()
            fy = send(half(b_x, 0), half(b_x, 0), "y")
            y1.wait_recv()
            fx = send(half(b_y, 1), half(b_y, 1), "x")
            return [x1, y0, fx, fy]

        return forward

    a_forward = square_gather(r.a_full)

    @pl.when(x_hi == 1)
    def _():
        swap.wait_recv()

    step_a = gather_step(r.w_attn, 0, lane)

    @pl.when(carries)
    def _():
        mlp_to_core.wait_recv()
        mlp_to_x.start()

    r.c_full[i_own] = reorder(r.cot[...])
    c_core = send(r.c_full.at[i_own], r.c_full.at[i_own], "c")
    c_y = send(r.c_full.at[i_own], r.c_full.at[i_own], "y")

    wait_recv(step_a)
    step_a = gather_step(r.w_attn, 1, lane)
    a_rest = a_forward()
    wait_recv(step_a)
    step_a = gather_step(r.w_attn, 2, lane)

    @pl.when(lends)
    def _():
        mlp_to_x.wait_recv()

    wait_recv(step_a)
    step_a = gather_step(r.w_attn, 3, lane)
    early = core_send(r.w_attn, False)
    step_m = gather_step(r.w_mlp, 0, both)
    wait_recv(step_a)
    late = core_send(r.w_attn, True)
    wait_recv(a_rest)
    wait_recv(early)
    wait_recv(late)
    wait_recv(step_m)
    step_m = gather_step(r.w_mlp, 1, both)

    def w_qkv(g):
        return r.w_attn[g, :, :, :, :, :, 0:QKV].reshape(WIDTH, QKV)

    def w_o(g):
        return r.w_attn[g, :, :, :, :, :, QKV:AW].reshape(WIDTH, 256)

    def w_gu(g):
        return r.w_mlp[g, :, :, :, :, :, 0 : 2 * HID].reshape(WIDTH, 2 * HID)

    def w_dn(g):
        return r.w_mlp[g, :, :, :, :, :, 2 * HID : MW].reshape(WIDTH, HID)

    def qkv_block(blk, carry):
        rows = r.a_full[blk]
        cos = r.cosf[blk]
        sin = r.sinf[blk]
        for g in range(2):
            acc = dot_nn(rows, w_qkv(g))
            r.qkp[g, blk] = acc[:, :384]
            for h in range(3):
                pre = acc[:, h * HEAD : (h + 1) * HEAD]
                normed = pre * row_scale(pre) * (key_gain if h == 2 else query_gain)
                turned = normed * cos + pltpu.roll(normed, 64, 1) * sin
                if h == 2:
                    r.ks[g, blk] = turned.astype(BF16)
                    r.kt[g, blk] = turned.T.astype(BF16)
                else:
                    r.qs[g, blk, h * ROWS : (h + 1) * ROWS] = turned.astype(BF16)
            value = acc[:, 384:]
            r.vs[g, blk] = value.astype(BF16)
            r.vt[g, blk] = value.T.astype(BF16)
        return carry

    lax.fori_loop(0, 4, qkv_block, 0)
    wait_recv(step_m)
    step_m = gather_step(r.w_mlp, 2, both)

    key_at = lax.broadcasted_iota(jnp.int32, (ROWS, 512), 0)
    query_at = lax.broadcasted_iota(jnp.int32, (ROWS, 512), 1) % ROWS
    visible = key_at <= query_at

    def weights_t(g, i, j, diagonal):
        scores = dot_nt(r.ks[g, j], r.qs[g, i])
        exps = jnp.exp2(scores * EXP_SCALE)
        if diagonal:
            exps = jnp.where(visible, exps, 0.0)
        return exps

    def attend_step(i, j, carry, diagonal):
        out = []
        for g in range(2):
            total, acc = carry[g]
            exps = weights_t(g, i, j, diagonal)
            total = total + jnp.sum(exps, axis=0, keepdims=True)
            acc = acc + dot_nn(r.vt[g, j], exps.astype(BF16))
            out.append((total, acc))
        return tuple(out)

    def attend_block(i, carry):
        zero = (jnp.zeros((1, 512), F32), jnp.zeros((HEAD, 512), F32))
        state = lax.fori_loop(0, i, lambda j, s: attend_step(i, j, s, False), (zero, zero))
        state = attend_step(i, i, state, True)
        for g in range(2):
            total, acc = state[g]
            inv = 1.0 / total
            r.linv[g, i] = jnp.broadcast_to(inv, (8, 512))
            mixed = acc * inv
            r.os[g, i] = mixed.T.astype(BF16)
        return carry

    lax.fori_loop(0, 4, attend_block, 0)
    wait_recv(step_m)
    step_m = gather_step(r.w_mlp, 3, both)

    def square_sum(part_of, near, far, finish_own):
        flush()
        r.stage[2] = part_of(b_d).astype(BF16)
        d0 = send(r.stage.at[2, pl.ds(0, 128)], far.at[0], "x")
        d1 = send(r.stage.at[2, pl.ds(128, 128)], far.at[1], "y")
        r.stage[0] = part_of(b_x).astype(BF16)
        x0 = send(r.stage.at[0, pl.ds(0, 128)], near.at[0, pl.ds(0, 128)], "x")
        r.stage[1] = part_of(b_y).astype(BF16)
        y1 = send(r.stage.at[1, pl.ds(128, 128)], near.at[1, pl.ds(128, 128)], "y")
        d1.wait_recv()
        r.stage[0, 128:256] = (r.stage[0, 128:256].astype(F32) + far[1].astype(F32)).astype(BF16)
        x1 = send(r.stage.at[0, pl.ds(128, 128)], near.at[0, pl.ds(128, 128)], "x")
        d0.wait_recv()
        r.stage[1, 0:128] = (r.stage[1, 0:128].astype(F32) + far[0].astype(F32)).astype(BF16)
        y0 = send(r.stage.at[1, pl.ds(0, 128)], near.at[1, pl.ds(0, 128)], "y")
        r.own[...] = part_of(b_own)
        finish_own()
        wait_recv([x0, y1, x1, y0])
        return r.own[...] + near[0].astype(F32) + near[1].astype(F32)

    def part_o(blk):
        acc = jnp.zeros((ROWS, WIDTH), F32)
        for g in range(2):
            heads = r.os[g, blk]
            acc = acc + dot_nt(jnp.concatenate([heads[:ROWS], heads[ROWS:]], axis=1), w_o(g))
        return acc

    def forward_cot():
        c_y.wait_recv()
        forwards.append(send(r.c_full.at[i_y], r.c_full.at[i_y], "c"))

    forwards = []
    resid = rows_x_again(r) + square_sum(part_o, r.rs_q_n, r.rs_q_d, forward_cot)
    r.resid[...] = resid

    r.m_full[i_own] = (resid * row_scale(resid) * mlp_gain).astype(BF16)
    m_core = send(r.m_full.at[i_own], r.m_full.at[i_own], "c")
    m_y = []
    for n in range(2):
        view = r.m_full.at[i_own, pl.ds(128 * n, 128)]
        m_y.append(send(view, view, "y"))
    wait_recv(step_m)
    c_core.wait_recv()
    wait_recv(forwards)

    def mlp_block(i):
        rows = r.m_full[i]
        cots = r.c_full[i]
        for g in range(2):
            pre = dot_nn(rows, w_gu(g))
            grad = dot_nn(cots, w_dn(g))
            gate = pre[:, :HID]
            up = pre[:, HID:]
            sig = 1.0 / (1.0 + jnp.exp(-gate))
            act = gate * sig
            r.hid[g, i] = (act * up).astype(BF16)
            r.dgu[g, i, :, 0:HID] = (grad * up * sig * (1.0 + gate * (1.0 - sig))).astype(BF16)
            r.dgu[g, i, :, HID : 2 * HID] = (grad * act).astype(BF16)

    mlp_block(i_own)
    m_core.wait_recv()
    mlp_block(i_c)
    m_f = []
    for n in range(2):
        view = r.m_full.at[i_y, pl.ds(128 * n, 128)]
        m_y[n].wait_recv()
        m_f.append(send(view, view, "c"))
    mlp_block(i_y)
    wait_recv(m_f)
    mlp_block(i_yc)

    def pair_sum(part_of, stage, recv, own):
        stage[2] = part_of(i_yc).astype(BF16)
        s3 = send(stage.at[2], recv.at[0], "c")
        stage[0] = part_of(i_c).astype(BF16)
        s1 = send(stage.at[0], recv.at[1], "c")
        near = part_of(i_y)
        s3.wait_recv()
        stage[1] = (near + recv[0].astype(F32)).astype(BF16)
        s2 = send(stage.at[1], recv.at[2], "y")
        own[...] = part_of(i_own)

        def finish():
            wait_recv([s1, s2])
            return own[...] + recv[1].astype(F32) + recv[2].astype(F32)

        return finish

    def part_dm(i):
        return dot_nt(r.dgu[0, i], w_gu(0)) + dot_nt(r.dgu[1, i], w_gu(1))

    def part_down(i):
        return dot_nt(r.hid[0, i], w_dn(0)) + dot_nt(r.hid[1, i], w_dn(1))

    flush()
    dm_finish = pair_sum(part_dm, r.stage, r.rs_m, r.own)
    down_finish = pair_sum(part_down, r.stage_down, r.rs_d, r.own_down)
    r.own_down[...] += r.resid[...]

    @pl.when(carries)
    def _():
        mlp_to_x.wait_send()

    for p in range(4):
        cols = pl.ds(256 * p, 256)
        rows_t = r.m_full[:, :, cols].reshape(SEQ, 256)
        cots_t = r.c_full[:, :, cols].reshape(SEQ, 256)
        for g in range(2):
            grad_gu = dot_tn(rows_t, r.dgu[g].reshape(SEQ, 2 * HID))
            grad_dn = dot_tn(cots_t, r.hid[g].reshape(SEQ, HID))
            r.w_mlp[g, p // 2, p % 2, :, :, :, 0 : 2 * HID] = grad_gu.reshape(2, 2, 64, 2 * HID).astype(BF16)
            r.w_mlp[g, p // 2, p % 2, :, :, :, 2 * HID : MW] = grad_dn.reshape(2, 2, 64, HID).astype(BF16)
    step_m = reduce_send(r.w_mlp, "rm", 3, both)

    dm = dm_finish()
    resid = r.resid[...]
    inv_m = row_scale(resid)
    scaled = dm * mlp_gain
    inner = jnp.mean(scaled * resid, axis=-1, keepdims=True)
    r.gains[...] = jnp.zeros((8, WIDTH), F32)
    r.gains[1:2] = jnp.sum(dm * resid * inv_m, axis=0, keepdims=True)
    dresid = reorder(r.cot[...].astype(F32)) + inv_m * scaled - resid * (inv_m * inv_m * inv_m * inner)
    r.resid[...] = dresid
    r.d_full[b_own] = dresid.astype(BF16)
    d_forward = square_gather(r.d_full)

    down = down_finish()
    r.layer_out[...] = reorder(down).astype(BF16)
    d_rest = d_forward()
    reduce_add(r.w_mlp, "rm", 3, both, step_m)
    step_m = reduce_send(r.w_mlp, "rm", 2, both)
    wait_recv(d_rest)

    def do_block(blk, carry):
        rows = r.d_full[blk]
        for g in range(2):
            grad = dot_nn(rows, w_o(g))
            for h in range(2):
                part = grad[:, h * HEAD : (h + 1) * HEAD].astype(BF16)
                r.dos[g, blk, h * ROWS : (h + 1) * ROWS] = part
                prod = part.astype(F32) * r.os[g, blk, h * ROWS : (h + 1) * ROWS].astype(F32)
                inner = jnp.sum(prod.T, axis=0, keepdims=True)
                r.delta[g, blk, :, h * ROWS : (h + 1) * ROWS] = jnp.broadcast_to(inner, (8, ROWS))
            r.dk[g, blk] = jnp.zeros((ROWS, HEAD), F32)
            r.dv[g, blk] = jnp.zeros((ROWS, HEAD), F32)
        return carry

    lax.fori_loop(0, 4, do_block, 0)
    reduce_add(r.w_mlp, "rm", 2, both, step_m)
    step_m = reduce_send(r.w_mlp, "rm", 1, both)

    def back_step(i, j, carry, diagonal):
        out = []
        for g in range(2):
            probs = weights_t(g, i, j, diagonal) * r.linv[g, i, 0:1]
            grads = dot_nt(r.vs[g, j], r.dos[g, i])
            dz = (probs * (grads - r.delta[g, i, 0:1])).astype(BF16)
            r.dv[g, j] += dot_nn(probs.astype(BF16), r.dos[g, i])
            r.dk[g, j] += dot_nn(dz, r.qs[g, i])
            out.append(carry[g] + dot_nn(r.kt[g, j], dz))
        return tuple(out)

    def unnorm(pre, gain, grad):
        inv = row_scale(pre)
        hat = pre * inv
        scaled = grad * gain
        back = inv * (scaled - hat * jnp.mean(scaled * hat, axis=-1, keepdims=True))
        return back.astype(BF16), jnp.sum(grad * hat, axis=0, keepdims=True)

    def turn_back(grad, blk):
        return grad * r.cosf[blk] - pltpu.roll(grad, 64, 1) * r.sinf[blk]

    def back_block(i, gain_sum):
        zero = jnp.zeros((HEAD, 512), F32)
        state = lax.fori_loop(0, i, lambda j, s: back_step(i, j, s, False), (zero, zero))
        state = back_step(i, i, state, True)
        for g in range(2):
            for h in range(2):
                grad = turn_back(state[g][:, h * ROWS : (h + 1) * ROWS].T * SCORE_SCALE, i)
                low, part = unnorm(r.qkp[g, i, :, h * HEAD : (h + 1) * HEAD], query_gain, grad)
                r.dgu[g, i, :, h * HEAD : (h + 1) * HEAD] = low
                gain_sum = gain_sum + part
        return gain_sum

    q_gain_part = lax.fori_loop(0, 4, back_block, jnp.zeros((1, HEAD), F32))

    def key_block(j, gain_sum):
        for g in range(2):
            grad = turn_back(r.dk[g, j] * SCORE_SCALE, j)
            low, part = unnorm(r.qkp[g, j, :, 256:384], key_gain, grad)
            r.dgu[g, j, :, 256:384] = low
            r.dgu[g, j, :, 384:512] = r.dv[g, j].astype(BF16)
            gain_sum = gain_sum + part
        return gain_sum

    k_gain_part = lax.fori_loop(0, 4, key_block, jnp.zeros((1, HEAD), F32))
    r.gains[2:3, 0:HEAD] = q_gain_part
    r.gains[2:3, HEAD : 2 * HEAD] = k_gain_part
    reduce_add(r.w_mlp, "rm", 1, both, step_m)
    step_m = reduce_send(r.w_mlp, "rm", 0, both)

    def part_da(blk):
        acc = dot_nt(r.dgu[0, blk, :, 0:QKV], w_qkv(0)) + dot_nt(r.dgu[1, blk, :, 0:QKV], w_qkv(1))
        r.gains[0:1] += jnp.sum(acc * r.a_full[blk].astype(F32), axis=0, keepdims=True)
        return acc

    tail = {}

    def attn_grads():
        reduce_add(r.w_mlp, "rm", 0, both, step_m)

        @pl.when(lends)
        def _():
            mlp_back_x.start()

        for p in range(4):
            cols = pl.ds(256 * p, 256)
            rows_t = r.a_full[:, :, cols].reshape(SEQ, 256)
            grads_t = r.d_full[:, :, cols].reshape(SEQ, 256)
            for g in range(2):
                grad_qkv = dot_tn(rows_t, r.dgu[g, :, :, 0:QKV].reshape(SEQ, QKV))
                r.w_attn[g, p // 2, p % 2, :, :, :, 0:QKV] = grad_qkv.reshape(2, 2, 64, QKV).astype(BF16)
                heads = r.os[g]
                mixed = jnp.concatenate(
                    [heads[:, :ROWS].reshape(SEQ, HEAD), heads[:, ROWS:].reshape(SEQ, HEAD)], axis=1
                )
                grad_o = dot_tn(grads_t, mixed)
                r.w_attn[g, p // 2, p % 2, :, :, :, QKV:AW] = grad_o.reshape(2, 2, 64, 256).astype(BF16)
        other = pl.ds(flip(core), 1)
        whole = (both, both, both, both)
        to_core = send(r.w_attn.at[(*whole, other)], r.core_in, "c")
        to_core.wait_recv()
        index = (*whole, lane)
        r.w_attn[index] = (r.w_attn[index].astype(F32) + r.core_in[...].astype(F32)).astype(BF16)
        tail["step"] = reduce_send(r.w_attn, "ra", 3, lane)

    mlp_back_x = rcopy(mlp_pair, r.mlp_x, "x")
    mlp_back_c = rcopy(r.mlp_sum.at[flip(core)], r.mlp_c, "c")
    da = square_sum(part_da, r.rs_q_n, r.rs_q_d, attn_grads)

    rows_x = rows_x_again(r)
    inv_a = row_scale(rows_x)
    scaled = da * attn_gain
    inner = jnp.mean(scaled * rows_x, axis=-1, keepdims=True)
    r.input_grad[...] = reorder(r.resid[...] + inv_a * scaled - rows_x * (inv_a * inv_a * inv_a * inner))

    step_a = tail["step"]
    reduce_add(r.w_attn, "ra", 3, lane, step_a)
    step_a = reduce_send(r.w_attn, "ra", 2, lane)

    @pl.when(carries)
    def _():
        mlp_back_x.wait_recv()
        r.mlp_sum[...] = mlp_pair[...].astype(F32) + r.mlp_x[...].astype(F32)
        mlp_back_c.start()

    links = ["c", "x", "y", "xo", "yo", "za", "zb"]

    def gain_send(n):
        return send(r.gains, r.gain_in.at[n], links[n])

    def gain_add(n, copy):
        copy.wait()
        unsent[:] = [other for other in unsent if other is not copy]
        r.gains[...] += r.gain_in[n]

    g_step = gain_send(0)
    reduce_add(r.w_attn, "ra", 2, lane, step_a)
    step_a = reduce_send(r.w_attn, "ra", 1, lane)
    gain_add(0, g_step)
    g_step = gain_send(1)
    gain_add(1, g_step)
    g_step = gain_send(2)
    reduce_add(r.w_attn, "ra", 1, lane, step_a)
    step_a = reduce_send(r.w_attn, "ra", 0, lane)
    gain_add(2, g_step)
    g_step = gain_send(3)

    @pl.when(lends)
    def _():
        mlp_back_c.wait_recv()
        r.d_mlp[...] = r.mlp_c[...]

    @pl.when(carries)
    def _():
        r.d_mlp[...] = r.mlp_sum[core]

    gain_add(3, g_step)
    g_step = gain_send(4)
    for part in range(4):
        rows = pl.ds(16 * part, 16)
        step_a[part].wait_recv()
        total = r.w_attn[(*own_slot(lane), rows)].astype(F32) + getattr(r, f"ra_{part}_0")[...].astype(F32)
        r.attn_sum[16 * part : 16 * part + 16] = total.reshape(16, AW)
    attn_back = rcopy(r.attn_sum, r.attn_x, "x")

    @pl.when(x_hi == 1)
    def _():
        attn_back.start()

    gain_add(4, g_step)
    g_step = gain_send(5)

    @pl.when(x_hi == 0)
    def _():
        r.d_attn[...] = r.attn_sum[...]

    gain_add(5, g_step)
    g_step = gain_send(6)

    @pl.when(x_hi == 1)
    def _():
        attn_back.wait_recv()
        r.d_attn[...] = r.attn_x[...]

    gain_add(6, g_step)
    sums = r.gains[...]
    inv_gain = 1.0 / attn_gain
    r.d_gain[...] = reorder(sums)
    r.d_gain[0:1] = reorder(sums[0:1] * inv_gain)
    r.d_gain[2:3] = sums[2:3]
    flush()

    @pl.when(x_hi == 1)
    def _():
        swap.wait_send()
        attn_back.wait_send()

    @pl.when(lends)
    def _():
        mlp_to_core.wait_send()
        mlp_back_x.wait_send()

    @pl.when(carries)
    def _():
        mlp_back_c.wait_send()


def rows_x_again(r):
    return reorder(r.tok[...].astype(F32))


def rope_tables():
    position = np.arange(SEQ, dtype=np.float32)[:, None]
    channel = np.arange(HEAD // 2, dtype=np.float32)[None, :]
    rate = np.exp(channel * np.float32(-2.0 * math.log(ROPE_BASE) / HEAD)).astype(np.float32)
    angle = (position * rate).astype(np.float32).astype(np.float64)
    cos = np.cos(angle).astype(np.float32)
    sin = np.sin(angle).astype(np.float32)
    shape = (4, ROWS, HEAD)
    return (
        np.concatenate([cos, cos], axis=1).reshape(shape),
        np.concatenate([-sin, sin], axis=1).reshape(shape),
    )


def body(
    tokens,
    attn_gain,
    w_query,
    key_weight,
    value_weight,
    query_gain,
    key_gain,
    w_out,
    mlp_gain,
    w_gate,
    w_up,
    w_down,
    out_cotangent,
):
    pack_attn = jnp.concatenate([w_query, key_weight, value_weight, w_out.T], axis=1)
    pack_mlp = jnp.concatenate([w_gate, w_up, w_down.T], axis=1)
    cosf, sinf = rope_tables()
    vmem = pl.BlockSpec(memory_space=pltpu.VMEM)
    layer_out, input_grad, d_attn, d_mlp, d_gain = pl.pallas_call(
        kernel,
        out_shape=(
            jax.ShapeDtypeStruct((ROWS, WIDTH), BF16),
            jax.ShapeDtypeStruct((ROWS, WIDTH), F32),
            jax.ShapeDtypeStruct((64, AW), F32),
            jax.ShapeDtypeStruct((64, MW), F32),
            jax.ShapeDtypeStruct((8, WIDTH), F32),
        ),
        in_specs=[vmem] * len(INPUTS),
        out_specs=(vmem,) * len(OUTPUTS),
        scratch_shapes=[pltpu.VMEM(*SCRATCH[name]) for name in NAMES]
        + [pltpu.SemaphoreType.DMA((N_SEM,)), pltpu.SemaphoreType.DMA((N_SEM,))],
        compiler_params=pltpu.CompilerParams(
            collective_id=0, has_side_effects=True, vmem_limit_bytes=64 * 2**20 - 2**17
        ),
        name="layer",
    )(
        tokens,
        out_cotangent,
        pack_attn,
        pack_mlp,
        attn_gain.reshape(1, -1),
        mlp_gain.reshape(1, -1),
        query_gain.reshape(1, -1),
        key_gain.reshape(1, -1),
        jnp.asarray(cosf),
        jnp.asarray(sinf),
    )
    return (
        layer_out,
        input_grad,
        d_gain[0],
        d_attn[:, 0:256],
        d_attn[:, 256:384],
        d_attn[:, 384:512],
        d_gain[2, 0:HEAD],
        d_gain[2, HEAD : 2 * HEAD],
        d_attn[:, 512:768].T,
        d_gain[1],
        d_mlp[:, 0:HID],
        d_mlp[:, HID : 2 * HID],
        d_mlp[:, 2 * HID : MW].T,
    )


def solution(mesh):
    rows = P(("dp", "tensor"), None)
    first = P("dp", "tensor")
    second = P("tensor", "dp")
    whole = P()
    return jax.shard_map(
        body,
        mesh=mesh,
        in_specs=(
            rows,
            whole,
            first,
            first,
            first,
            whole,
            whole,
            second,
            whole,
            first,
            first,
            second,
            rows,
        ),
        out_specs=(
            rows,
            rows,
            whole,
            first,
            first,
            first,
            whole,
            whole,
            second,
            whole,
            first,
            first,
            second,
        ),
        check_vma=False,
    )
```

```python
import math

import jax
import jax.numpy as jnp
import numpy as np
from jax import lax
from jax.experimental import pallas as pl
from jax.experimental.pallas import tpu as pltpu
from jax.sharding import PartitionSpec as P

HEAD = 128
SEQ = 1024
WIDTH = 1024
ROWS = 256
QKV = 512
OW = 256
AW = QKV + OW
HID = 384
MW = 3 * HID
EPS = 1e-06
ROPE_BASE = 1000000.0
EXP_SCALE = math.log2(math.e) / math.sqrt(HEAD)
SCORE_SCALE = 1.0 / math.sqrt(HEAD)
MESH = pl.DeviceIdType.MESH
F32 = jnp.float32
BF16 = jnp.bfloat16


def dot_nn(a, b):
    return jnp.dot(a, b, preferred_element_type=F32)


def dot_nt(a, b):
    return lax.dot_general(a, b, (((1,), (1,)), ((), ())), preferred_element_type=F32)


def dot_tn(a, b):
    return lax.dot_general(a, b, (((0,), (0,)), ((), ())), preferred_element_type=F32)


def reorder(v):
    return jnp.concatenate([v[:, :512], v[:, 768:], v[:, 512:768]], axis=1)


def row_scale(v):
    return lax.rsqrt(jnp.mean(v * v, axis=-1, keepdims=True) + EPS)


def flip(bit):
    return 1 - bit


SCRATCH = {
    "w_q": ((2, 2, 2, 2, 2, 64, QKV), BF16),
    "w_o": ((2, 2, 2, 2, 2, 64, OW), BF16),
    "w_m": ((2, 2, 2, 2, 2, 64, MW), BF16),
    "pack_q": ((64, QKV), BF16),
    "pack_o": ((64, OW), BF16),
    "pack_m": ((64, MW), BF16),
    "a_full": ((4, ROWS, WIDTH), BF16),
    "m_full": ((4, ROWS, WIDTH), BF16),
    "c_full": ((4, ROWS, WIDTH), BF16),
    "d_full": ((4, ROWS, WIDTH), BF16),
    "qkp": ((2, 4, ROWS, 384), F32),
    "qs": ((2, 4, 512, HEAD), BF16),
    "ks": ((2, 4, ROWS, HEAD), BF16),
    "kt": ((2, 4, HEAD, ROWS), BF16),
    "vs": ((2, 4, ROWS, HEAD), BF16),
    "vt": ((2, 4, HEAD, ROWS), BF16),
    "os": ((2, 4, 512, HEAD), BF16),
    "linv": ((2, 4, 8, 512), F32),
    "dos": ((2, 512, HEAD), BF16),
    "dk": ((2, 4, ROWS, HEAD), F32),
    "dv": ((2, 4, ROWS, HEAD), F32),
    "hid": ((2, 4, ROWS, HID), BF16),
    "dgu": ((2, 4, ROWS, 2 * HID), BF16),
    "own": ((ROWS, WIDTH), F32),
    "own_down": ((ROWS, WIDTH), F32),
    "resid": ((ROWS, WIDTH), F32),
    "stage": ((3, ROWS, WIDTH), BF16),
    "stage_down": ((3, ROWS, WIDTH), BF16),
    "far": ((2, 128, WIDTH), BF16),
    "near": ((2, ROWS, WIDTH), BF16),
    "sum_m": ((3, ROWS, WIDTH), BF16),
    "sum_d": ((3, ROWS, WIDTH), BF16),
    "gains": ((8, WIDTH), F32),
    "gain_in": ((7, 8, WIDTH), F32),
    "core_q": ((2, 2, 2, 2, 1, 64, QKV), BF16),
    "core_o": ((2, 2, 2, 2, 1, 64, OW), BF16),
    "mlp_x": ((2, 64, MW), BF16),
    "mlp_c": ((64, MW), F32),
    "attn_x": ((64, AW), F32),
    "attn_sum": ((64, AW), F32),
    "mlp_sum": ((2, 64, MW), F32),
}
AXES = {"xo": 3, "yo": 0, "za": 2, "zb": 1}
ORDER = ["xo", "yo", "za", "zb"]


def part_axes(part):
    return [ORDER[(part + step) % 4] for step in range(4)]


def cube_shape(part, step, cores, width):
    shape = [1, 1, 1, 1]
    for axis in part_axes(part)[:step]:
        shape[AXES[axis]] = 2
    return (*shape, cores, 16, width)


for _part in range(4):
    for _step in range(4):
        SCRATCH[f"sum_q_{_part}_{_step}"] = (cube_shape(_part, _step, 1, QKV), BF16)
        SCRATCH[f"sum_o_{_part}_{_step}"] = (cube_shape(_part, _step, 1, OW), BF16)
        SCRATCH[f"sum_w_{_part}_{_step}"] = (cube_shape(_part, _step, 2, MW), BF16)

NAMES = list(SCRATCH)
N_SEM = 107
INPUTS = ["tok", "cot", "wq", "wk", "wv", "wo", "wg", "wu", "wd", "ag", "mg", "qg", "kg", "cosf", "sinf"]
OUTPUTS = ["layer_out", "input_grad", "d_attn", "d_mlp", "d_gain"]


class Refs:
    pass


class Copy:
    def __init__(self, copy, gives, takes):
        self.copy, self.gives, self.takes = copy, gives, takes
        self.started = self.received = self.sent = False

    def run(self, cond, act):
        if cond is None:
            act()
        else:
            pl.when(cond)(act)

    def start(self):
        self.started = True
        self.run(self.gives, self.copy.start)

    def wait_recv(self):
        self.received = True
        self.run(self.takes, self.copy.wait_recv)

    def wait_send(self):
        self.sent = True
        self.run(self.gives, self.copy.wait_send)


def kernel(*refs):
    r = Refs()
    names = INPUTS + OUTPUTS + NAMES
    for name, ref in zip(names, refs):
        setattr(r, name, ref)
    ssem, rsem = refs[len(names)], refs[len(names) + 1]

    dp = lax.axis_index("dp")
    tn = lax.axis_index("tensor")
    z = dp // 4
    x_hi = (dp // 2) % 2
    core = dp % 2
    y = tn // 2
    x_lo = tn % 2
    y_lo = y % 2
    y_hi = y // 2
    gz = jnp.where(z < 2, z, 5 - z)
    own_bit = {"xo": x_hi, "yo": y_hi, "za": gz % 2, "zb": gz // 2}
    nbr = {
        "c": (dp + 1 - 2 * core, tn),
        "x": (dp, tn + 1 - 2 * x_lo),
        "y": (dp, tn + 2 - 4 * y_lo),
        "xo": (dp + 2 - 4 * x_hi, tn + 1 - 2 * x_lo),
        "yo": (dp, (3 - y) * 2 + x_lo),
        "za": (dp + 4 - 8 * (z % 2), tn),
        "zb": (dp + 4 * (3 - 2 * z), tn),
    }
    pair = "y"

    def square(k):
        kx, ky = k % 2, k // 2
        return (y_lo + ky - 2 * y_lo * ky) * 2 + x_lo + kx - 2 * x_lo * kx

    def group(k):
        kc = k % 2
        return (k // 2) * 2 + core + kc - 2 * core * kc

    ids = {}
    copies = r.copies = []
    unsent = []

    def later(src, dst, to, key, gives=None, takes=None):
        i = ids.setdefault(key, len(ids))
        copy = pltpu.make_async_remote_copy(
            src_ref=src,
            dst_ref=dst,
            send_sem=ssem.at[i],
            recv_sem=rsem.at[i],
            device_id=nbr[to],
            device_id_type=MESH,
        )
        copies.append(Copy(copy, gives, takes))
        unsent.append(copies[-1])
        return copies[-1]

    def send(*args, **kinds):
        copy = later(*args, **kinds)
        copy.start()
        return copy

    def flush():
        for copy in unsent:
            if copy.started and not copy.sent:
                copy.wait_send()
        unsent[:] = [copy for copy in unsent if not copy.sent]

    def wait_recv(group):
        for copy in group:
            copy.wait_recv()

    def at(k, value, act):
        pl.when(k == value)(act)

    def slots(full, current, cores):
        index = [None] * 4
        for axis in ORDER:
            if axis in full:
                index[AXES[axis]] = pl.ds(0, 2)
            else:
                bit = own_bit[axis]
                index[AXES[axis]] = pl.ds(flip(bit) if current == axis else bit, 1)
        return (*index, cores)

    both = pl.ds(0, 2)
    lane = pl.ds(core, 1)
    lanes = {"q": lane, "o": lane, "w": both}
    weights = {"q": r.w_q, "o": r.w_o, "w": r.w_m}
    own_slot = (own_bit["yo"], own_bit["zb"], own_bit["za"], own_bit["xo"])
    own_view = tuple(pl.ds(bit, 1) for bit in own_slot)

    def step_key(kind, part, step, back):
        return (kind, part, step, back and kind == "w" and step == 3)

    def gather_step(kind, step):
        out = []
        for part in range(4):
            axes = part_axes(part)
            rows = pl.ds(16 * part, 16)
            view = weights[kind].at[(*slots(axes[:step], None, lanes[kind]), rows)]
            out.append(send(view, view, axes[step], step_key(kind, part, step, False)))
        return out

    def core_send(kind, late):
        out = []
        for part in range(4):
            axes = part_axes(part)
            rows = pl.ds(16 * part, 16)
            view = weights[kind].at[(*slots(axes[:3], axes[3] if late else None, lane), rows)]
            out.append(send(view, view, "c", ("core", kind, late, part)))
        return out

    def reduce_later(kind, step):
        out = []
        for part in range(4):
            axes = part_axes(part)
            rows = pl.ds(16 * part, 16)
            view = weights[kind].at[(*slots(axes[:step], axes[step], lanes[kind]), rows)]
            buf = getattr(r, f"sum_{kind}_{part}_{step}")
            out.append(later(view, buf, axes[step], step_key(kind, part, step, True)))
        return out

    def start(group):
        for copy in group:
            copy.start()

    def reduce_add(kind, step, group):
        for part in range(4):
            axes = part_axes(part)
            rows = pl.ds(16 * part, 16)
            index = (*slots(axes[:step], None, lanes[kind]), rows)
            group[part].wait_recv()
            total = weights[kind][index].astype(F32) + getattr(r, f"sum_{kind}_{part}_{step}")[...].astype(F32)
            weights[kind][index] = total.astype(BF16)

    barrier = pltpu.get_barrier_semaphore()
    for to in nbr:
        pl.semaphore_signal(barrier, inc=1, device_id=nbr[to], device_id_type=MESH)

    carries = core == x_lo
    lends = core != x_lo
    r.pack_q[:, 0:256] = r.wq[...]
    r.pack_q[:, 256:384] = r.wk[...]
    r.pack_q[:, 384:512] = r.wv[...]
    r.pack_o[...] = r.wo[...]
    r.pack_m[:, 0:HID] = r.wg[...]
    r.pack_m[:, HID : 2 * HID] = r.wu[...]
    r.pack_m[:, 2 * HID : MW] = r.wd[...]

    @pl.when(x_hi == 0)
    def _():
        r.w_q[(*own_view, lane)] = r.pack_q[...].reshape(1, 1, 1, 1, 1, 64, QKV)
        r.w_o[(*own_view, lane)] = r.pack_o[...].reshape(1, 1, 1, 1, 1, 64, OW)

    @pl.when(carries)
    def _():
        r.w_m[(*own_view, lane)] = r.pack_m[...].reshape(1, 1, 1, 1, 1, 64, MW)

    attn_gain = reorder(r.ag[...].astype(F32).reshape(1, WIDTH))
    mlp_gain = reorder(r.mg[...].astype(F32).reshape(1, WIDTH))
    query_gain = r.qg[...].astype(F32).reshape(1, HEAD)
    key_gain = r.kg[...].astype(F32).reshape(1, HEAD)

    def rows_in():
        return reorder(r.tok[...].astype(F32))

    rows_x = rows_in()
    r.a_full[square(0)] = (rows_x * row_scale(rows_x) * attn_gain).astype(BF16)
    r.c_full[group(0)] = reorder(r.cot[...])
    pl.semaphore_wait(barrier, len(nbr))

    swap_q = send(r.pack_q, r.w_q.at[(*own_slot, core)], "x", "swap_q", gives=x_hi == 1, takes=x_hi == 1)
    swap_o = send(r.pack_o, r.w_o.at[(*own_slot, core)], "x", "swap_o", gives=x_hi == 1, takes=x_hi == 1)
    mlp_pair = r.w_m.at[own_slot]
    mlp_to_core = send(r.pack_m, r.w_m.at[(*own_slot, core)], "c", "mlp_c", gives=lends, takes=carries)
    mlp_to_x = later(mlp_pair, mlp_pair, "x", "mlp_x", gives=carries, takes=lends)

    def square_gather(buf):
        def half(k, n):
            return buf.at[square(k), pl.ds(128 * n, 128)]

        x0 = send(half(0, 0), half(0, 0), "x", "sg_x0")
        y1 = send(half(0, 1), half(0, 1), "y", "sg_y1")
        x1 = send(half(0, 1), half(0, 1), "x", "sg_x1")
        y0 = send(half(0, 0), half(0, 0), "y", "sg_y0")
        fy = later(half(1, 0), half(1, 0), "y", "sg_fy")
        fx = later(half(2, 1), half(2, 1), "x", "sg_fx")

        def forward():
            x0.wait_recv()
            fy.start()
            y1.wait_recv()
            fx.start()

        return forward, x1, y0, [fx, fy]

    a_forward, a_x1, a_y0, a_far = square_gather(r.a_full)

    swap_q.wait_recv()
    step_q = gather_step("q", 0)
    wait_recv(step_q)
    step_q = gather_step("q", 1)
    swap_o.wait_recv()
    step_o = gather_step("o", 0)
    mlp_to_core.wait_recv()
    mlp_to_x.start()
    a_forward()
    wait_recv(step_q)
    step_q = gather_step("q", 2)
    wait_recv(step_o)
    step_o = gather_step("o", 1)
    wait_recv(step_q)
    step_q = gather_step("q", 3)
    early = core_send("q", False)
    wait_recv(step_o)
    step_o = gather_step("o", 2)
    mlp_to_x.wait_recv()
    step_w = gather_step("w", 0)
    wait_recv(step_q)
    late = core_send("q", True)
    wait_recv(step_o)
    step_o = gather_step("o", 3)
    early_o = core_send("o", False)
    wait_recv(early)
    wait_recv(late)

    def w_qkv(g):
        return r.w_q[g].reshape(WIDTH, QKV)

    def w_out(g):
        return r.w_o[g].reshape(WIDTH, OW)

    def w_gu(g):
        return r.w_m[g, :, :, :, :, :, 0 : 2 * HID].reshape(WIDTH, 2 * HID)

    def w_dn(g):
        return r.w_m[g, :, :, :, :, :, 2 * HID : MW].reshape(WIDTH, HID)

    c_pair = later(r.c_full.at[group(0)], r.c_full.at[core + 2], pair, "cot_p")
    c_core = later(r.c_full.at[group(0)], r.c_full.at[group(0)], "c", "cot_c")

    def qkv_block(k, carry):
        at(k, 1, a_x1.wait_recv)
        at(k, 2, a_y0.wait_recv)

        @pl.when(k == 3)
        def _():
            wait_recv(a_far)
            c_pair.start()
            c_core.start()

        blk = square(k)
        rows = r.a_full[blk]
        cos = r.cosf[blk]
        sin = r.sinf[blk]
        for g in range(2):
            acc = dot_nn(rows, w_qkv(g))
            r.qkp[g, blk] = acc[:, :384]
            for h in range(3):
                pre = acc[:, h * HEAD : (h + 1) * HEAD]
                normed = pre * row_scale(pre) * (key_gain if h == 2 else query_gain)
                turned = normed * cos + pltpu.roll(normed, 64, 1) * sin
                if h == 2:
                    r.ks[g, blk] = turned.astype(BF16)
                    r.kt[g, blk] = turned.T.astype(BF16)
                else:
                    r.qs[g, blk, h * ROWS : (h + 1) * ROWS] = turned.astype(BF16)
            value = acc[:, 384:]
            r.vs[g, blk] = value.astype(BF16)
            r.vt[g, blk] = value.T.astype(BF16)
        return carry

    lax.fori_loop(0, 4, qkv_block, 0)
    wait_recv(step_w)
    step_w = gather_step("w", 1)
    wait_recv(step_o)
    late_o = core_send("o", True)

    key_at = lax.broadcasted_iota(jnp.int32, (ROWS, 512), 0)
    query_at = lax.broadcasted_iota(jnp.int32, (ROWS, 512), 1) % ROWS
    visible = key_at <= query_at

    def weights_t(g, i, j, diagonal):
        scores = dot_nt(r.ks[g, j], r.qs[g, i])
        exps = jnp.exp2(scores * EXP_SCALE)
        if diagonal:
            exps = jnp.where(visible, exps, 0.0)
        return exps

    def attend_step(i, j, carry, diagonal):
        out = []
        for g in range(2):
            total, acc = carry[g]
            exps = weights_t(g, i, j, diagonal)
            total = total + jnp.sum(exps, axis=0, keepdims=True)
            acc = acc + dot_nn(r.vt[g, j], exps.astype(BF16))
            out.append((total, acc))
        return tuple(out)

    def attend_block(i):
        zero = (jnp.zeros((1, 512), F32), jnp.zeros((HEAD, 512), F32))
        state = lax.fori_loop(0, i, lambda j, s: attend_step(i, j, s, False), (zero, zero))
        state = attend_step(i, i, state, True)
        for g in range(2):
            total, acc = state[g]
            inv = 1.0 / total
            r.linv[g, i] = jnp.broadcast_to(inv, (8, 512))
            r.os[g, i] = (acc * inv).T.astype(BF16)

    def part_o(blk):
        acc = jnp.zeros((ROWS, WIDTH), F32)
        for g in range(2):
            heads = r.os[g, blk]
            acc = acc + dot_nt(jnp.concatenate([heads[:ROWS], heads[ROWS:]], axis=1), w_out(g))
        return acc

    def square_sum(part_of, steps):
        def out(n, rows, buf, to, key):
            return later(r.stage.at[n, pl.ds(*rows)], buf, to, key)

        low, high = (0, 128), (128, 128)
        d0 = out(2, low, r.far.at[0], "x", "ss_d0")
        d1 = out(2, high, r.far.at[1], "y", "ss_d1")
        x0 = out(0, low, r.near.at[0, pl.ds(*low)], "x", "ss_x0")
        x1 = out(0, high, r.near.at[0, pl.ds(*high)], "x", "ss_x1")
        y0 = out(1, low, r.near.at[1, pl.ds(*low)], "y", "ss_y0")
        y1 = out(1, high, r.near.at[1, pl.ds(*high)], "y", "ss_y1")

        def block(n, carry):
            k = jnp.where(n == 0, 3, n % 3)
            for value, act in steps.items():
                at(n, value, act)
            acc = part_of(square(k))

            @pl.when(n < 3)
            def _():
                r.stage[(n + 2) % 3] = acc.astype(BF16)

            @pl.when(n == 3)
            def _():
                r.own[...] = acc

            @pl.when(n == 0)
            def _():
                d0.start()
                d1.start()

            at(n, 1, x0.start)
            at(n, 2, y1.start)
            return carry

        lax.fori_loop(0, 4, block, 0)
        d1.wait_recv()
        r.stage[0, 128:256] = (r.stage[0, 128:256].astype(F32) + r.far[1].astype(F32)).astype(BF16)
        x1.start()
        d0.wait_recv()
        r.stage[1, 0:128] = (r.stage[1, 0:128].astype(F32) + r.far[0].astype(F32)).astype(BF16)
        y0.start()

        def finish():
            wait_recv([x0, y1, x1, y0])
            return r.own[...] + r.near[0].astype(F32) + r.near[1].astype(F32)

        return finish

    def attend_and_part(blk):
        attend_block(blk)
        return part_o(blk)

    wait_recv(early_o)
    wait_recv(late_o)
    wait_recv(step_w)
    step_w = gather_step("w", 2)
    o_finish = square_sum(attend_and_part, {})
    wait_recv(step_w)
    step_w = gather_step("w", 3)
    c_pair.wait_recv()
    c_forward = send(r.c_full.at[core + 2], r.c_full.at[core + 2], "c", "cot_f")
    resid = rows_in() + o_finish()
    r.resid[...] = resid

    r.m_full[group(0)] = (resid * row_scale(resid) * mlp_gain).astype(BF16)
    m_pair = []
    m_forward = []
    for n in range(2):
        rows = pl.ds(128 * n, 128)
        m_pair.append(send(r.m_full.at[group(0), rows], r.m_full.at[core + 2, rows], pair, ("m_p", n)))
        m_forward.append(later(r.m_full.at[core + 2, rows], r.m_full.at[core + 2, rows], "c", ("m_f", n)))
    m_core = send(r.m_full.at[group(0)], r.m_full.at[group(0)], "c", "m_c")
    wait_recv(step_w)
    wait_recv([c_core, c_forward])

    def mlp_block(k, carry):
        at(k, 1, m_core.wait_recv)

        @pl.when(k == 2)
        def _():
            for n in range(2):
                m_pair[n].wait_recv()
                m_forward[n].start()

        @pl.when(k == 3)
        def _():
            wait_recv(m_forward)

        i = group(k)
        rows = r.m_full[i]
        cots = r.c_full[i]
        for g in range(2):
            pre = dot_nn(rows, w_gu(g))
            grad = dot_nn(cots, w_dn(g))
            gate = pre[:, :HID]
            up = pre[:, HID:]
            sig = 1.0 / (1.0 + jnp.exp(-gate))
            act = gate * sig
            r.hid[g, i] = (act * up).astype(BF16)
            r.dgu[g, i, :, 0:HID] = (grad * up * sig * (1.0 + gate * (1.0 - sig))).astype(BF16)
            r.dgu[g, i, :, HID : 2 * HID] = (grad * act).astype(BF16)
        return carry

    lax.fori_loop(0, 4, mlp_block, 0)
    flush()

    def pair_sum(part_of, stage, recv, own, name, hold):
        s3 = later(stage.at[2], recv.at[0], "c", (name, 3))
        s1 = later(stage.at[0], recv.at[1], "c", (name, 1))
        s2 = later(stage.at[1], recv.at[2], pair, (name, 2))

        def block(n, carry):
            acc = part_of(group(3 - n))

            @pl.when(n == 0)
            def _():
                stage[2] = acc.astype(BF16)
                s3.start()

            @pl.when(n == 1)
            def _():
                s3.wait_recv()
                stage[1] = (acc + recv[0].astype(F32)).astype(BF16)
                if not hold:
                    s2.start()

            @pl.when(n == 2)
            def _():
                stage[0] = acc.astype(BF16)
                s1.start()

            @pl.when(n == 3)
            def _():
                own[...] = acc

            return carry

        lax.fori_loop(0, 4, block, 0)

        def finish():
            wait_recv([s1, s2])
            return own[...] + recv[1].astype(F32) + recv[2].astype(F32)

        return finish, s2

    def part_dm(i):
        return dot_nt(r.dgu[0, i], w_gu(0)) + dot_nt(r.dgu[1, i], w_gu(1))

    def part_down(i):
        return dot_nt(r.hid[0, i], w_dn(0)) + dot_nt(r.hid[1, i], w_dn(1))

    dm_finish, _ = pair_sum(part_dm, r.stage, r.sum_m, r.own, "dm", False)
    down_finish, down_pair = pair_sum(part_down, r.stage_down, r.sum_d, r.own_down, "down", True)
    r.own_down[...] += r.resid[...]

    def mlp_grads(p, carry):
        cols = pl.ds(pl.multiple_of(256 * p, 256), 256)
        rows_t = r.m_full[:, :, cols].reshape(SEQ, 256)
        cots_t = r.c_full[:, :, cols].reshape(SEQ, 256)
        for g in range(2):
            grad_gu = dot_tn(rows_t, r.dgu[g].reshape(SEQ, 2 * HID))
            grad_dn = dot_tn(cots_t, r.hid[g].reshape(SEQ, HID))
            r.w_m[g, p // 2, p % 2, :, :, :, 0 : 2 * HID] = grad_gu.reshape(2, 2, 64, 2 * HID).astype(BF16)
            r.w_m[g, p // 2, p % 2, :, :, :, 2 * HID : MW] = grad_dn.reshape(2, 2, 64, HID).astype(BF16)
        return carry

    lax.fori_loop(0, 4, mlp_grads, 0)
    back_w = {step: reduce_later("w", step) for step in range(4)}
    start(back_w[3])

    dm = dm_finish()
    resid = r.resid[...]
    inv_m = row_scale(resid)
    scaled = dm * mlp_gain
    inner = jnp.mean(scaled * resid, axis=-1, keepdims=True)
    r.gains[...] = jnp.zeros((8, WIDTH), F32)
    r.gains[1:2] = jnp.sum(dm * resid * inv_m, axis=0, keepdims=True)
    dresid = reorder(r.cot[...].astype(F32)) + inv_m * scaled - resid * (inv_m * inv_m * inv_m * inner)
    r.resid[...] = dresid
    r.d_full[square(0)] = dresid.astype(BF16)
    d_forward, d_x1, d_y0, d_far = square_gather(r.d_full)
    r.dk[...] = jnp.zeros((2, 4, ROWS, HEAD), F32)
    r.dv[...] = jnp.zeros((2, 4, ROWS, HEAD), F32)

    def back_step(i, j, carry, diagonal, delta):
        out = []
        for g in range(2):
            probs = weights_t(g, i, j, diagonal) * r.linv[g, i, 0:1]
            grads = dot_nt(r.vs[g, j], r.dos[g])
            dz = (probs * (grads - delta[g])).astype(BF16)
            r.dv[g, j] += dot_nn(probs.astype(BF16), r.dos[g])
            r.dk[g, j] += dot_nn(dz, r.qs[g, i])
            out.append(carry[g] + dot_nn(r.kt[g, j], dz))
        return tuple(out)

    def unnorm(pre, gain, grad):
        inv = row_scale(pre)
        hat = pre * inv
        scaled = grad * gain
        back = inv * (scaled - hat * jnp.mean(scaled * hat, axis=-1, keepdims=True))
        return back.astype(BF16), jnp.sum(grad * hat, axis=0, keepdims=True)

    def turn_back(grad, blk):
        return grad * r.cosf[blk] - pltpu.roll(grad, 64, 1) * r.sinf[blk]

    def back_block(k, gain_sum):
        @pl.when(k == 1)
        def _():
            d_forward()
            down_pair.start()
            d_x1.wait_recv()
            reduce_add("w", 3, back_w[3])
            start(back_w[2])

        at(k, 2, d_y0.wait_recv)

        @pl.when(k == 3)
        def _():
            wait_recv(d_far)
            reduce_add("w", 2, back_w[2])
            start(back_w[1])

        i = square(k)
        rows = r.d_full[i]
        delta = []
        for g in range(2):
            grad = dot_nn(rows, w_out(g))
            inner = []
            for h in range(2):
                part = grad[:, h * HEAD : (h + 1) * HEAD].astype(BF16)
                r.dos[g, h * ROWS : (h + 1) * ROWS] = part
                prod = part.astype(F32) * r.os[g, i, h * ROWS : (h + 1) * ROWS].astype(F32)
                inner.append(jnp.sum(prod.T, axis=0, keepdims=True))
            delta.append(jnp.concatenate(inner, axis=1))
        zero = jnp.zeros((HEAD, 512), F32)
        state = lax.fori_loop(0, i, lambda j, s: back_step(i, j, s, False, delta), (zero, zero))
        state = back_step(i, i, state, True, delta)
        for g in range(2):
            for h in range(2):
                grad = turn_back(state[g][:, h * ROWS : (h + 1) * ROWS].T * SCORE_SCALE, i)
                low, part = unnorm(r.qkp[g, i, :, h * HEAD : (h + 1) * HEAD], query_gain, grad)
                r.dgu[g, i, :, h * HEAD : (h + 1) * HEAD] = low
                gain_sum = gain_sum + part
        return gain_sum

    q_gain_part = lax.fori_loop(0, 4, back_block, jnp.zeros((1, HEAD), F32))

    other = pl.ds(flip(core), 1)
    whole = (both, both, both, both)

    def out_grads(p, carry):
        cols = pl.ds(pl.multiple_of(256 * p, 256), 256)
        grads_t = r.d_full[:, :, cols].reshape(SEQ, 256)
        for g in range(2):
            heads = r.os[g]
            mixed = jnp.concatenate(
                [heads[:, :ROWS].reshape(SEQ, HEAD), heads[:, ROWS:].reshape(SEQ, HEAD)], axis=1
            )
            r.w_o[g, p // 2, p % 2] = dot_tn(grads_t, mixed).reshape(2, 2, 64, OW).astype(BF16)
        return carry

    def core_sum(kind, buf, copy):
        copy.wait_recv()
        index = (*whole, lane)
        total = weights[kind][index].astype(F32) + buf[...].astype(F32)
        weights[kind][index] = total.astype(BF16)

    lax.fori_loop(0, 4, out_grads, 0)
    o_core = send(r.w_o.at[(*whole, other)], r.core_o, "c", "o_core")

    def key_block(j, gain_sum):
        for g in range(2):
            grad = turn_back(r.dk[g, j] * SCORE_SCALE, j)
            low, part = unnorm(r.qkp[g, j, :, 256:384], key_gain, grad)
            r.dgu[g, j, :, 256:384] = low
            r.dgu[g, j, :, 384:512] = r.dv[g, j].astype(BF16)
            gain_sum = gain_sum + part
        return gain_sum

    k_gain_part = lax.fori_loop(0, 4, key_block, jnp.zeros((1, HEAD), F32))
    r.gains[2:3, 0:HEAD] = q_gain_part
    r.gains[2:3, HEAD : 2 * HEAD] = k_gain_part
    flush()

    def part_da(blk):
        acc = dot_nt(r.dgu[0, blk, :, 0:QKV], w_qkv(0)) + dot_nt(r.dgu[1, blk, :, 0:QKV], w_qkv(1))
        r.gains[0:1] += jnp.sum(acc * r.a_full[blk].astype(F32), axis=0, keepdims=True)
        return acc

    back_o = {step: reduce_later("o", step) for step in range(4)}
    back_q = {step: reduce_later("q", step) for step in range(4)}

    def tail_o():
        core_sum("o", r.core_o, o_core)
        start(back_o[3])

    def tail_w():
        reduce_add("w", 1, back_w[1])
        start(back_w[0])

    a_finish = square_sum(part_da, {1: tail_o, 2: tail_w})

    def qkv_grads(p, carry):
        cols = pl.ds(pl.multiple_of(256 * p, 256), 256)
        rows_t = r.a_full[:, :, cols].reshape(SEQ, 256)
        for g in range(2):
            grad = dot_tn(rows_t, r.dgu[g, :, :, 0:QKV].reshape(SEQ, QKV))
            r.w_q[g, p // 2, p % 2] = grad.reshape(2, 2, 64, QKV).astype(BF16)
        return carry

    links = ["c", "za", "zb", "yo", "xo", "y", "x"]

    def gain_send(n):
        return send(r.gains, r.gain_in.at[n], links[n], ("gain", n))

    def gain_add(n, copy):
        copy.wait_send()
        copy.wait_recv()
        r.gains[...] += r.gain_in[n]

    g_step = gain_send(0)
    lax.fori_loop(0, 4, qkv_grads, 0)
    q_core = send(r.w_q.at[(*whole, other)], r.core_q, "c", "q_core")
    gain_add(0, g_step)
    g_step = gain_send(1)
    reduce_add("o", 3, back_o[3])
    start(back_o[2])
    core_sum("q", r.core_q, q_core)
    start(back_q[3])
    gain_add(1, g_step)
    g_step = gain_send(2)
    mlp_back_x = later(mlp_pair, r.mlp_x, "x", "mlp_x", gives=lends, takes=carries)
    mlp_back_c = later(r.mlp_sum.at[flip(core)], r.mlp_c, "c", "mlp_c", gives=carries, takes=lends)
    reduce_add("w", 0, back_w[0])
    mlp_back_x.start()
    reduce_add("o", 2, back_o[2])
    start(back_o[1])
    r.layer_out[...] = reorder(down_finish()).astype(BF16)
    gain_add(2, g_step)
    g_step = gain_send(3)
    reduce_add("q", 3, back_q[3])
    start(back_q[2])
    reduce_add("o", 1, back_o[1])
    start(back_o[0])
    gain_add(3, g_step)
    g_step = gain_send(4)
    reduce_add("q", 2, back_q[2])
    start(back_q[1])
    mlp_back_x.wait_recv()

    @pl.when(carries)
    def _():
        r.mlp_sum[...] = mlp_pair[...].astype(F32) + r.mlp_x[...].astype(F32)

    mlp_back_c.start()
    gain_add(4, g_step)

    rows_x = rows_in()
    inv_a = row_scale(rows_x)
    scaled = a_finish() * attn_gain
    g_step = gain_send(5)
    inner = jnp.mean(scaled * rows_x, axis=-1, keepdims=True)
    r.input_grad[...] = reorder(r.resid[...] + inv_a * scaled - rows_x * (inv_a * inv_a * inv_a * inner))
    reduce_add("q", 1, back_q[1])
    start(back_q[0])
    gain_add(5, g_step)
    g_step = gain_send(6)

    def last_step(kind, group, cols):
        for part in range(4):
            rows = pl.ds(16 * part, 16)
            group[part].wait_recv()
            total = weights[kind][(*own_view, lane, rows)].astype(F32) + getattr(r, f"sum_{kind}_{part}_0")[...].astype(F32)
            r.attn_sum[16 * part : 16 * part + 16, cols] = total.reshape(16, -1)

    last_step("o", back_o[0], slice(QKV, AW))
    mlp_back_c.wait_recv()

    @pl.when(lends)
    def _():
        r.d_mlp[...] = r.mlp_c[...]

    @pl.when(carries)
    def _():
        r.d_mlp[...] = r.mlp_sum[core]

    last_step("q", back_q[0], slice(0, QKV))
    attn_back = send(r.attn_sum, r.attn_x, "x", "swap_q", gives=x_hi == 1, takes=x_hi == 1)
    gain_add(6, g_step)
    sums = r.gains[...]
    r.d_gain[...] = reorder(sums)
    r.d_gain[0:1] = reorder(sums[0:1] / attn_gain)
    r.d_gain[2:3] = sums[2:3]

    @pl.when(x_hi == 0)
    def _():
        r.d_attn[...] = r.attn_sum[...]

    attn_back.wait_recv()

    @pl.when(x_hi == 1)
    def _():
        r.d_attn[...] = r.attn_x[...]

    flush()


def unpack(*refs):
    layer_in, input_in, d_attn, d_mlp, d_gain = refs[:5]
    (
        layer_out,
        input_grad,
        attn_gain,
        w_query,
        w_key,
        w_value,
        query_gain,
        key_gain,
        w_out,
        mlp_gain,
        w_gate,
        w_up,
        w_down,
    ) = refs[5:18]
    layer_out[...] = layer_in[...]
    input_grad[...] = input_in[...]
    attn_gain[...] = d_gain[0]
    mlp_gain[...] = d_gain[1]
    query_gain[...] = d_gain[2, 0:HEAD]
    key_gain[...] = d_gain[2, HEAD : 2 * HEAD]
    w_query[...] = d_attn[:, 0:256]
    w_key[...] = d_attn[:, 256:384]
    w_value[...] = d_attn[:, 384:512]
    w_out[...] = d_attn[:, 512:768]
    w_gate[...] = d_mlp[:, 0:HID]
    w_up[...] = d_mlp[:, HID : 2 * HID]
    w_down[...] = d_mlp[:, 2 * HID : MW]


def rope_tables():
    position = np.arange(SEQ, dtype=np.float32)[:, None]
    channel = np.arange(HEAD // 2, dtype=np.float32)[None, :]
    rate = np.exp(channel * np.float32(-2.0 * math.log(ROPE_BASE) / HEAD)).astype(np.float32)
    angle = (position * rate).astype(np.float32).astype(np.float64)
    cos = np.cos(angle).astype(np.float32)
    sin = np.sin(angle).astype(np.float32)
    shape = (4, ROWS, HEAD)
    return (
        np.concatenate([cos, cos], axis=1).reshape(shape),
        np.concatenate([-sin, sin], axis=1).reshape(shape),
    )


def body(
    tokens,
    attn_gain,
    w_query,
    key_weight,
    value_weight,
    query_gain,
    key_gain,
    w_out,
    mlp_gain,
    w_gate,
    w_up,
    w_down,
    out_cotangent,
):
    cosf, sinf = rope_tables()
    vmem = pl.BlockSpec(memory_space=pltpu.VMEM)

    def out(*shape):
        return jax.ShapeDtypeStruct(shape, F32)

    packed = pl.pallas_call(
        kernel,
        out_shape=(
            jax.ShapeDtypeStruct((ROWS, WIDTH), BF16),
            out(ROWS, WIDTH),
            out(64, AW),
            out(64, MW),
            out(8, WIDTH),
        ),
        in_specs=[vmem] * len(INPUTS),
        out_specs=(vmem,) * len(OUTPUTS),
        scratch_shapes=[pltpu.VMEM(*SCRATCH[name]) for name in NAMES]
        + [pltpu.SemaphoreType.DMA((N_SEM,)), pltpu.SemaphoreType.DMA((N_SEM,))],
        compiler_params=pltpu.CompilerParams(
            collective_id=0, has_side_effects=True, vmem_limit_bytes=64 * 2**20 - 2**17
        ),
        name="layer",
    )(
        tokens,
        out_cotangent,
        w_query,
        key_weight,
        value_weight,
        w_out.T,
        w_gate,
        w_up,
        w_down.T,
        attn_gain,
        mlp_gain,
        query_gain,
        key_gain,
        jnp.asarray(cosf),
        jnp.asarray(sinf),
    )
    parts = list(pl.pallas_call(
        unpack,
        out_shape=[
            jax.ShapeDtypeStruct((ROWS, WIDTH), BF16),
            out(ROWS, WIDTH),
            out(WIDTH),
            out(64, 256),
            out(64, HEAD),
            out(64, HEAD),
            out(HEAD),
            out(HEAD),
            out(64, 256),
            out(WIDTH),
            out(64, HID),
            out(64, HID),
            out(64, HID),
        ],
        in_specs=[vmem] * 5,
        out_specs=[vmem] * 13,
        name="unpack",
    )(*packed))
    parts[8] = parts[8].T
    parts[12] = parts[12].T
    return tuple(parts)


def solution(mesh):
    rows = P(("dp", "tensor"), None)
    first = P("dp", "tensor")
    second = P("tensor", "dp")
    whole = P()
    return jax.shard_map(
        body,
        mesh=mesh,
        in_specs=(
            rows,
            whole,
            first,
            first,
            first,
            whole,
            whole,
            second,
            whole,
            first,
            first,
            second,
            rows,
        ),
        out_specs=(
            rows,
            rows,
            whole,
            first,
            first,
            first,
            whole,
            whole,
            second,
            whole,
            first,
            first,
            second,
        ),
        check_vma=False,
    )
```

```python
import math

import jax
import jax.numpy as jnp
import numpy as np
from jax import lax
from jax.experimental import pallas as pl
from jax.experimental.pallas import tpu as pltpu
from jax.sharding import PartitionSpec as P

HEAD = 128
SEQ = 1024
WIDTH = 1024
ROWS = 256
QKV = 512
OW = 256
AW = QKV + OW
HID = 384
MW = 3 * HID
EPS = 1e-06
ROPE_BASE = 1000000.0
EXP_SCALE = math.log2(math.e) / math.sqrt(HEAD)
SCORE_SCALE = 1.0 / math.sqrt(HEAD)
MESH = pl.DeviceIdType.MESH
F32 = jnp.float32
BF16 = jnp.bfloat16


def dot_nn(a, b):
    return jnp.dot(a, b, preferred_element_type=F32)


def dot_nt(a, b):
    return lax.dot_general(a, b, (((1,), (1,)), ((), ())), preferred_element_type=F32)


def dot_tn(a, b):
    return lax.dot_general(a, b, (((0,), (0,)), ((), ())), preferred_element_type=F32)


def reorder(v):
    return jnp.concatenate([v[:, :512], v[:, 768:], v[:, 512:768]], axis=1)


def row_scale(v):
    return lax.rsqrt(jnp.mean(v * v, axis=-1, keepdims=True) + EPS)


def flip(bit):
    return 1 - bit


SCRATCH = {
    "w_q": ((2, 2, 2, 2, 2, 64, QKV), BF16),
    "w_o": ((2, 2, 2, 2, 2, 64, OW), BF16),
    "w_m": ((2, 2, 2, 2, 2, 64, MW), BF16),
    "pack_q": ((64, QKV), BF16),
    "pack_o": ((64, OW), BF16),
    "pack_m": ((64, MW), BF16),
    "a_full": ((4, ROWS, WIDTH), BF16),
    "m_full": ((2, 2, 2, 2, 2, 64, 512), BF16),
    "c_full": ((4, ROWS, WIDTH), BF16),
    "d_full": ((4, ROWS, WIDTH), BF16),
    "qkp": ((2, 4, ROWS, 384), F32),
    "qs": ((2, 4, 512, HEAD), BF16),
    "ks": ((2, 4, ROWS, HEAD), BF16),
    "kt": ((2, 4, HEAD, ROWS), BF16),
    "vs": ((2, 4, ROWS, HEAD), BF16),
    "vt": ((2, 4, HEAD, ROWS), BF16),
    "os": ((2, 4, 512, HEAD), BF16),
    "linv": ((2, 4, 8, 512), F32),
    "dos": ((2, 512, HEAD), BF16),
    "dk": ((2, 4, ROWS, HEAD), F32),
    "dv": ((2, 4, ROWS, HEAD), F32),
    "hid": ((2, 4, ROWS, HID), BF16),
    "dgu": ((2, 4, ROWS, 2 * HID), BF16),
    "own": ((ROWS, WIDTH), F32),
    "resid": ((ROWS, WIDTH), F32),
    "stage": ((3, ROWS, WIDTH), BF16),
    "stage_down": ((3, ROWS, WIDTH), BF16),
    "far": ((2, 128, WIDTH), BF16),
    "near": ((2, ROWS, WIDTH), BF16),
    "sum_m": ((3, ROWS, WIDTH), BF16),
    "sum_d": ((3, ROWS, WIDTH), BF16),
    "gains": ((8, WIDTH), F32),
    "gain_in": ((7, 8, WIDTH), F32),
    "core_q": ((2, 2, 2, 2, 1, 64, QKV), BF16),
    "core_o": ((2, 2, 2, 2, 1, 64, OW), BF16),
    "raw": ((2, 2, 64, MW), BF16),
    "mlp_x": ((2, 64, MW), BF16),
    "mlp_c": ((64, MW), F32),
    "attn_x": ((64, AW), BF16),
    "attn_low": ((64, AW), BF16),
    "attn_sum": ((64, AW), F32),
    "mlp_sum": ((2, 64, MW), F32),
}
AXES = {"xo": 3, "yo": 0, "za": 2, "zb": 1}
ORDER = ["xo", "yo", "za", "zb"]


def part_axes(part):
    return [ORDER[(part + step) % 4] for step in range(4)]


def cube_shape(part, step, cores, width):
    shape = [1, 1, 1, 1]
    for axis in part_axes(part)[:step]:
        shape[AXES[axis]] = 2
    return (*shape, cores, 16, width)


for _part in range(4):
    for _step in range(4):
        SCRATCH[f"sum_q_{_part}_{_step}"] = (cube_shape(_part, _step, 1, QKV), BF16)
        SCRATCH[f"sum_o_{_part}_{_step}"] = (cube_shape(_part, _step, 1, OW), BF16)
        SCRATCH[f"sum_w_{_part}_{_step}"] = (cube_shape(_part, _step, 2, MW), BF16)

NAMES = list(SCRATCH)
N_SEM = 109
INPUTS = ["tok", "cot", "wq", "wk", "wv", "wo", "wg", "wu", "wd", "ag", "mg", "qg", "kg", "rope"]
OUTPUTS = ["layer_out", "input_grad", "d_attn", "d_mlp", "d_gain"]


class Refs:
    pass


class Copy:
    def __init__(self, copy, gives, takes):
        self.copy, self.gives, self.takes = copy, gives, takes
        self.started = self.received = self.sent = False

    def run(self, cond, act):
        if cond is None:
            act()
        else:
            pl.when(cond)(act)

    def start(self):
        self.started = True
        self.run(self.gives, self.copy.start)

    def wait_recv(self):
        self.received = True
        self.run(self.takes, self.copy.wait_recv)

    def wait_send(self):
        self.sent = True
        self.run(self.gives, self.copy.wait_send)


def kernel(*refs):
    r = Refs()
    names = INPUTS + OUTPUTS + NAMES
    for name, ref in zip(names, refs):
        setattr(r, name, ref)
    ssem, rsem = refs[len(names)], refs[len(names) + 1]

    dp = lax.axis_index("dp")
    tn = lax.axis_index("tensor")
    z = dp // 4
    x_hi = (dp // 2) % 2
    core = dp % 2
    y = tn // 2
    x_lo = tn % 2
    y_lo = y % 2
    y_hi = y // 2
    gz = jnp.where(z < 2, z, 5 - z)
    own_bit = {"xo": x_hi, "yo": y_hi, "za": gz % 2, "zb": gz // 2}
    nbr = {
        "c": (dp + 1 - 2 * core, tn),
        "x": (dp, tn + 1 - 2 * x_lo),
        "y": (dp, tn + 2 - 4 * y_lo),
        "xo": (dp + 2 - 4 * x_hi, tn + 1 - 2 * x_lo),
        "yo": (dp, (3 - y) * 2 + x_lo),
        "za": (dp + 4 - 8 * (z % 2), tn),
        "zb": (dp + 4 * (3 - 2 * z), tn),
    }
    links = list(nbr)
    pair = "p"
    nbr["p"] = (dp, tn + jnp.where(core == 0, 2 - 4 * y_lo, 1 - 2 * x_lo))
    kx = (x_lo + x_hi) % 2
    lends = (core + x_lo) % 2
    role = 2 * lends + kx

    def square(k):
        kx, ky = k % 2, k // 2
        return (y_lo + ky - 2 * y_lo * ky) * 2 + x_lo + kx - 2 * x_lo * kx

    def group(k):
        kc = k % 2
        return (k // 2) * 2 + core + kc - 2 * core * kc

    ids = {}
    copies = r.copies = []
    unsent = []

    def later(src, dst, to, key, gives=None, takes=None):
        i = ids.setdefault(key, len(ids))
        copy = pltpu.make_async_remote_copy(
            src_ref=src,
            dst_ref=dst,
            send_sem=ssem.at[i],
            recv_sem=rsem.at[i],
            device_id=nbr[to],
            device_id_type=MESH,
        )
        copies.append(Copy(copy, gives, takes))
        unsent.append(copies[-1])
        return copies[-1]

    def send(*args, **kinds):
        copy = later(*args, **kinds)
        copy.start()
        return copy

    def flush():
        for copy in unsent:
            if copy.started and not copy.sent:
                copy.wait_send()
        unsent[:] = [copy for copy in unsent if not copy.sent]

    def wait_recv(group):
        for copy in group:
            copy.wait_recv()

    def at(k, value, act):
        pl.when(k == value)(act)

    def slots(full, current, cores):
        index = [None] * 4
        for axis in ORDER:
            if axis in full:
                index[AXES[axis]] = pl.ds(0, 2)
            else:
                bit = own_bit[axis]
                index[AXES[axis]] = pl.ds(flip(bit) if current == axis else bit, 1)
        return (*index, cores)

    both = pl.ds(0, 2)
    lane = pl.ds(core, 1)
    lanes = {"q": lane, "o": lane, "w": both}
    weights = {"q": r.w_q, "o": r.w_o, "w": r.w_m}
    grads = {"q": r.m_full, "o": r.w_o, "w": r.w_m}
    own_slot = (own_bit["yo"], own_bit["zb"], own_bit["za"], own_bit["xo"])
    own_view = tuple(pl.ds(bit, 1) for bit in own_slot)

    def step_key(kind, part, step, back):
        return (kind, part, step, back and kind == "w" and step == 3)

    def gather_later(kind, step):
        out = []
        for part in range(4):
            axes = part_axes(part)
            rows = pl.ds(16 * part, 16)
            view = weights[kind].at[(*slots(axes[:step], None, lanes[kind]), rows)]
            out.append(later(view, view, axes[step], step_key(kind, part, step, False)))
        return out

    def core_later(kind, late):
        out = []
        for part in range(4):
            axes = part_axes(part)
            rows = pl.ds(16 * part, 16)
            view = weights[kind].at[(*slots(axes[:3], axes[3] if late else None, lane), rows)]
            out.append(later(view, view, "c", ("core", kind, late, part)))
        return out

    def reduce_later(kind, step):
        out = []
        for part in range(4):
            axes = part_axes(part)
            rows = pl.ds(16 * part, 16)
            view = grads[kind].at[(*slots(axes[:step], axes[step], lanes[kind]), rows)]
            buf = getattr(r, f"sum_{kind}_{part}_{step}")
            out.append(later(view, buf, axes[step], step_key(kind, part, step, True)))
        return out

    def start(group):
        for copy in group:
            copy.start()

    def reduce_add(kind, step, group):
        for part in range(4):
            axes = part_axes(part)
            rows = pl.ds(16 * part, 16)
            index = (*slots(axes[:step], None, lanes[kind]), rows)
            group[part].wait_recv()
            total = grads[kind][index].astype(F32) + getattr(r, f"sum_{kind}_{part}_{step}")[...].astype(F32)
            grads[kind][index] = total.astype(BF16)

    barrier = pltpu.get_barrier_semaphore()
    for to in links:
        pl.semaphore_signal(barrier, inc=1, device_id=nbr[to], device_id_type=MESH)

    r.pack_q[:, 0:256] = r.wq[...]
    r.pack_q[:, 256:384] = r.wk[...]
    r.pack_q[:, 384:512] = r.wv[...]
    r.pack_o[...] = r.wo[...]
    r.pack_m[:, 0:HID] = r.wg[...]
    r.pack_m[:, HID : 2 * HID] = r.wu[...]
    r.pack_m[:, 2 * HID : MW] = r.wd[...]

    @pl.when(x_hi == 0)
    def _():
        r.w_q[(*own_view, lane)] = r.pack_q[...].reshape(1, 1, 1, 1, 1, 64, QKV)
        r.w_o[(*own_view, lane)] = r.pack_o[...].reshape(1, 1, 1, 1, 1, 64, OW)

    @pl.when(lends == 0)
    def _():
        r.raw[0, pl.ds(core, 1)] = r.pack_m[...].reshape(1, 64, MW)

    attn_gain = reorder(r.ag[...].astype(F32).reshape(1, WIDTH))
    mlp_gain = reorder(r.mg[...].astype(F32).reshape(1, WIDTH))
    query_gain = r.qg[...].astype(F32).reshape(1, HEAD)
    key_gain = r.kg[...].astype(F32).reshape(1, HEAD)

    def rows_in():
        return reorder(r.tok[...].astype(F32))

    rows_x = rows_in()
    r.a_full[square(0)] = (rows_x * row_scale(rows_x) * attn_gain).astype(BF16)
    r.c_full[group(0)] = reorder(r.cot[...])
    pl.semaphore_wait(barrier, len(links))

    odd = x_hi == 1
    swap_q = send(r.pack_q, r.w_q.at[(*own_slot, core)], "x", "swap_q", gives=odd, takes=odd)
    swap_o = send(r.pack_o, r.w_o.at[(*own_slot, core)], "x", "swap_o", gives=odd, takes=odd)
    mlp_pair = r.w_m.at[own_slot]
    raw_y = send(r.pack_m, r.raw.at[1, core], "y", "raw_y")
    raw_c0 = send(r.pack_m, r.raw.at[0, core], "c", "raw_c0", gives=lends == 1, takes=lends == 0)
    raw_c1 = later(r.raw.at[1, core], r.raw.at[1, core], "c", "raw_c1", gives=lends == 1, takes=lends == 0)
    mlp_to_x = later(r.raw.at[1 - kx], mlp_pair, "x", "mlp_x", gives=lends == 0, takes=lends == 1)

    def square_gather(buf):
        def half(k, n):
            return buf.at[square(k), pl.ds(128 * n, 128)]

        x0 = send(half(0, 0), half(0, 0), "x", "sg_x0")
        y1 = send(half(0, 1), half(0, 1), "y", "sg_y1")
        x1 = later(half(0, 1), half(0, 1), "x", "sg_x1")
        y0 = later(half(0, 0), half(0, 0), "y", "sg_y0")
        fy = later(half(1, 0), half(1, 0), "y", "sg_fy")
        fx = later(half(2, 1), half(2, 1), "x", "sg_fx")

        def second():
            x1.start()
            y0.start()

        def forward():
            x0.wait_recv()
            fy.start()
            y1.wait_recv()
            fx.start()

        return second, forward, x1, y0, [fx, fy]

    a_second, a_forward, a_x1, a_y0, a_far = square_gather(r.a_full)
    gather = {kind: [gather_later(kind, step) for step in range(4)] for kind in "qow"}
    to_core = {kind: [core_later(kind, late) for late in (False, True)] for kind in "qo"}

    def advance(kind, step):
        wait_recv(gather[kind][step - 1])
        start(gather[kind][step])

    swap_q.wait_recv()
    start(gather["q"][0])
    raw_y.wait_recv()
    raw_c1.start()
    swap_o.wait_recv()
    advance("q", 1)
    start(gather["o"][0])
    raw_c0.wait_recv()
    raw_c1.wait_recv()
    mlp_to_x.start()
    advance("q", 2)
    a_forward()

    @pl.when(lends == 0)
    def _():
        r.w_m[own_view] = r.raw[pl.ds(kx, 1)].reshape(1, 1, 1, 1, 2, 64, MW)

    advance("q", 3)
    start(to_core["q"][0])
    advance("o", 1)
    mlp_to_x.wait_recv()
    start(gather["w"][0])
    a_second()
    wait_recv(gather["q"][3])
    start(to_core["q"][1])
    advance("o", 2)
    advance("w", 1)
    wait_recv(to_core["q"][0])
    wait_recv(to_core["q"][1])

    def w_qkv(g):
        return r.w_q[g].reshape(WIDTH, QKV)

    def w_out(g):
        return r.w_o[g].reshape(WIDTH, OW)

    def w_gu(g):
        return r.w_m[g, :, :, :, :, :, 0 : 2 * HID].reshape(WIDTH, 2 * HID)

    def w_dn(g):
        return r.w_m[g, :, :, :, :, :, 2 * HID : MW].reshape(WIDTH, HID)

    c_pair = later(r.c_full.at[group(0)], r.c_full.at[core + 2], pair, "cot_p")
    c_core = later(r.c_full.at[group(0)], r.c_full.at[group(0)], "c", "cot_c")

    first_half = lax.broadcasted_iota(jnp.int32, (ROWS, HEAD), 1) < HEAD // 2

    def turns(blk):
        table = r.rope[blk]
        swapped = pltpu.roll(table, 64, 1)
        return jnp.where(first_half, table, swapped), jnp.where(first_half, -swapped, table)

    def qkv_block(k, carry):
        @pl.when(k == 1)
        def _():
            a_x1.wait_recv()
            c_pair.start()
            c_core.start()
            advance("o", 3)
            start(to_core["o"][0])

        @pl.when(k == 2)
        def _():
            a_y0.wait_recv()
            advance("w", 2)

        @pl.when(k == 3)
        def _():
            wait_recv(a_far)
            wait_recv(gather["o"][3])
            start(to_core["o"][1])

        blk = square(k)
        rows = r.a_full[blk]
        cos, sin = turns(blk)
        for g in range(2):
            acc = dot_nn(rows, w_qkv(g))
            r.qkp[g, blk] = acc[:, :384]
            for h in range(3):
                pre = acc[:, h * HEAD : (h + 1) * HEAD]
                normed = pre * row_scale(pre) * (key_gain if h == 2 else query_gain)
                turned = normed * cos + pltpu.roll(normed, 64, 1) * sin
                if h == 2:
                    r.ks[g, blk] = turned.astype(BF16)
                    r.kt[g, blk] = turned.T.astype(BF16)
                else:
                    r.qs[g, blk, h * ROWS : (h + 1) * ROWS] = turned.astype(BF16)
            value = acc[:, 384:]
            r.vs[g, blk] = value.astype(BF16)
            r.vt[g, blk] = value.T.astype(BF16)
        return carry

    lax.fori_loop(0, 4, qkv_block, 0)

    key_at = lax.broadcasted_iota(jnp.int32, (ROWS, 512), 0)
    query_at = lax.broadcasted_iota(jnp.int32, (ROWS, 512), 1) % ROWS
    visible = key_at <= query_at

    def weights_t(g, i, j, diagonal):
        scores = dot_nt(r.ks[g, j], r.qs[g, i])
        exps = jnp.exp2(scores * EXP_SCALE)
        if diagonal:
            exps = jnp.where(visible, exps, 0.0)
        return exps

    def attend_step(i, j, carry, diagonal):
        out = []
        for g in range(2):
            total, acc = carry[g]
            exps = weights_t(g, i, j, diagonal)
            total = total + jnp.sum(exps, axis=0, keepdims=True)
            acc = acc + dot_nn(r.vt[g, j], exps.astype(BF16))
            out.append((total, acc))
        return tuple(out)

    def attend_block(i):
        zero = (jnp.zeros((1, 512), F32), jnp.zeros((HEAD, 512), F32))
        state = lax.fori_loop(0, i, lambda j, s: attend_step(i, j, s, False), (zero, zero))
        state = attend_step(i, i, state, True)
        for g in range(2):
            total, acc = state[g]
            inv = 1.0 / total
            r.linv[g, i] = jnp.broadcast_to(inv, (8, 512))
            r.os[g, i] = (acc * inv).T.astype(BF16)

    def part_o(blk):
        acc = jnp.zeros((ROWS, WIDTH), F32)
        for g in range(2):
            heads = r.os[g, blk]
            acc = acc + dot_nt(jnp.concatenate([heads[:ROWS], heads[ROWS:]], axis=1), w_out(g))
        return acc

    def square_sum(part_of, steps):
        def out(n, rows, buf, to, key):
            return later(r.stage.at[n, pl.ds(*rows)], buf, to, key)

        low, high = (0, 128), (128, 128)
        d0 = out(2, low, r.far.at[0], "x", "ss_d0")
        d1 = out(2, high, r.far.at[1], "y", "ss_d1")
        x0 = out(0, low, r.near.at[0, pl.ds(*low)], "x", "ss_x0")
        x1 = out(0, high, r.near.at[0, pl.ds(*high)], "x", "ss_x1")
        y0 = out(1, low, r.near.at[1, pl.ds(*low)], "y", "ss_y0")
        y1 = out(1, high, r.near.at[1, pl.ds(*high)], "y", "ss_y1")

        def block(n, carry):
            k = jnp.where(n == 0, 3, n % 3)
            for value, act in steps.items():
                at(n, value, act)
            acc = part_of(square(k))

            @pl.when(n < 3)
            def _():
                r.stage[(n + 2) % 3] = acc.astype(BF16)

            @pl.when(n == 3)
            def _():
                r.own[...] = acc

            @pl.when(n == 0)
            def _():
                d0.start()
                d1.start()

            at(n, 2, x0.start)
            at(n, 3, y1.start)
            return carry

        lax.fori_loop(0, 4, block, 0)

        def relay():
            d1.wait_recv()
            r.stage[0, 128:256] = (r.stage[0, 128:256].astype(F32) + r.far[1].astype(F32)).astype(BF16)
            x1.start()
            d0.wait_recv()
            r.stage[1, 0:128] = (r.stage[1, 0:128].astype(F32) + r.far[0].astype(F32)).astype(BF16)
            y0.start()

        def finish():
            wait_recv([x0, y1, x1, y0])
            return r.own[...] + r.near[0].astype(F32) + r.near[1].astype(F32)

        return relay, finish

    def attend_and_part(blk):
        attend_block(blk)
        return part_o(blk)

    wait_recv(to_core["o"][0])
    wait_recv(to_core["o"][1])
    o_relay, o_finish = square_sum(attend_and_part, {3: lambda: advance("w", 3)})
    o_relay()
    c_pair.wait_recv()
    c_forward = send(r.c_full.at[core + 2], r.c_full.at[core + 2], "c", "cot_f")
    resid = rows_in() + o_finish()
    r.resid[...] = resid
    normed = (resid * row_scale(resid) * mlp_gain).astype(BF16)
    for half in range(2):
        r.m_full[0, pl.ds(core, 1), half] = normed[:, 512 * half : 512 * half + 512].reshape(1, 2, 2, 64, 512)
    m_pair = []
    m_forward = []
    for n in range(2):
        near_rows, far_rows = (r.m_full.at[place, core, :, n] for place in range(2))
        m_pair.append(send(near_rows, far_rows, pair, ("m_p", n)))
        m_forward.append(later(far_rows, far_rows, "c", ("m_f", n)))
    m_core = send(r.m_full.at[0, core], r.m_full.at[0, core], "c", "m_c")
    wait_recv(gather["w"][3])
    wait_recv([c_core, c_forward])

    def mlp_block(k, carry):
        at(k, 1, m_core.wait_recv)

        @pl.when(k == 2)
        def _():
            for n in range(2):
                m_pair[n].wait_recv()
                m_forward[n].start()

        @pl.when(k == 3)
        def _():
            wait_recv(m_forward)

        i = group(k)
        rows = jnp.concatenate([r.m_full[i // 2, i % 2, half].reshape(ROWS, 512) for half in range(2)], axis=1)
        cots = r.c_full[i]
        for g in range(2):
            pre = dot_nn(rows, w_gu(g))
            grad = dot_nn(cots, w_dn(g))
            gate = pre[:, :HID]
            up = pre[:, HID:]
            sig = 1.0 / (1.0 + jnp.exp(-gate))
            act = gate * sig
            r.hid[g, i] = (act * up).astype(BF16)
            r.dgu[g, i, :, 0:HID] = (grad * up * sig * (1.0 + gate * (1.0 - sig))).astype(BF16)
            r.dgu[g, i, :, HID : 2 * HID] = (grad * act).astype(BF16)
        return carry

    lax.fori_loop(0, 4, mlp_block, 0)
    flush()

    def pair_sum(part_of, stage, recv, own, name, hold):
        s3 = later(stage.at[2], recv.at[0], "c", (name, 3))
        s1 = later(stage.at[0], recv.at[1], "c", (name, 1))
        s2 = later(stage.at[1], recv.at[2], pair, (name, 2))

        def block(n, carry):
            acc = part_of(group(3 - n))

            @pl.when(n == 0)
            def _():
                stage[2] = acc.astype(BF16)
                s3.start()

            @pl.when(n == 1)
            def _():
                s3.wait_recv()
                stage[1] = (acc + recv[0].astype(F32)).astype(BF16)
                if not hold:
                    s2.start()

            @pl.when(n == 2)
            def _():
                stage[0] = acc.astype(BF16)
                s1.start()

            @pl.when(n == 3)
            def _():
                own[...] = own[...] + acc if hold else acc

            return carry

        lax.fori_loop(0, 4, block, 0)

        def finish():
            wait_recv([s1, s2])
            return own[...] + recv[1].astype(F32) + recv[2].astype(F32)

        return finish, s2

    def part_dm(i):
        return dot_nt(r.dgu[0, i], w_gu(0)) + dot_nt(r.dgu[1, i], w_gu(1))

    def part_down(i):
        return dot_nt(r.hid[0, i], w_dn(0)) + dot_nt(r.hid[1, i], w_dn(1))

    dm_finish, _ = pair_sum(part_dm, r.stage, r.sum_m, r.own, "dm", False)

    r.input_grad[...] = r.resid[...]
    down_finish, down_pair = pair_sum(part_down, r.stage_down, r.sum_d, r.input_grad, "down", True)
    def mlp_grads(p, carry):
        cols = pl.ds(pl.multiple_of(256 * p, 256), 256)
        half_cols = pl.ds(pl.multiple_of(256 * (p % 2), 256), 256)
        rows_t = r.m_full[:, :, p // 2, :, :, :, half_cols].reshape(SEQ, 256)
        cots_t = r.c_full[:, :, cols].reshape(SEQ, 256)
        for g in range(2):
            grad_gu = dot_tn(rows_t, r.dgu[g].reshape(SEQ, 2 * HID))
            grad_dn = dot_tn(cots_t, r.hid[g].reshape(SEQ, HID))
            r.w_m[g, p // 2, p % 2, :, :, :, 0 : 2 * HID] = grad_gu.reshape(2, 2, 64, 2 * HID).astype(BF16)
            r.w_m[g, p // 2, p % 2, :, :, :, 2 * HID : MW] = grad_dn.reshape(2, 2, 64, HID).astype(BF16)
        return carry

    lax.fori_loop(0, 2, mlp_grads, 0)
    back_w = {step: reduce_later("w", step) for step in range(4)}

    dm = dm_finish()
    resid = r.resid[...]
    inv_m = row_scale(resid)
    scaled = dm * mlp_gain
    inner = jnp.mean(scaled * resid, axis=-1, keepdims=True)
    r.gains[...] = jnp.zeros((8, WIDTH), F32)
    r.gains[1:2] = jnp.sum(dm * resid * inv_m, axis=0, keepdims=True)
    dresid = reorder(r.cot[...].astype(F32)) + inv_m * scaled - resid * (inv_m * inv_m * inv_m * inner)
    r.resid[...] = dresid
    r.d_full[square(0)] = dresid.astype(BF16)
    d_second, d_forward, d_x1, d_y0, d_far = square_gather(r.d_full)
    lax.fori_loop(2, 4, mlp_grads, 0)
    start(back_w[3])
    d_second()
    r.dk[...] = jnp.zeros((2, 4, ROWS, HEAD), F32)
    r.dv[...] = jnp.zeros((2, 4, ROWS, HEAD), F32)

    def back_step(i, j, carry, diagonal, delta):
        out = []
        for g in range(2):
            probs = weights_t(g, i, j, diagonal) * r.linv[g, i, 0:1]
            grads = dot_nt(r.vs[g, j], r.dos[g])
            dz = (probs * (grads - delta[g])).astype(BF16)
            r.dv[g, j] += dot_nn(probs.astype(BF16), r.dos[g])
            r.dk[g, j] += dot_nn(dz, r.qs[g, i])
            out.append(carry[g] + dot_nn(r.kt[g, j], dz))
        return tuple(out)

    def unnorm(pre, gain, grad):
        inv = row_scale(pre)
        hat = pre * inv
        scaled = grad * gain
        back = inv * (scaled - hat * jnp.mean(scaled * hat, axis=-1, keepdims=True))
        return back.astype(BF16), jnp.sum(grad * hat, axis=0, keepdims=True)

    def turn_back(grad, blk):
        cos, sin = turns(blk)
        return grad * cos - pltpu.roll(grad, 64, 1) * sin

    def back_block(k, gain_sum):
        @pl.when(k == 1)
        def _():
            d_forward()
            d_x1.wait_recv()

        @pl.when(k == 2)
        def _():
            d_y0.wait_recv()
            reduce_add("w", 3, back_w[3])
            start(back_w[2])

        @pl.when(k == 3)
        def _():
            wait_recv(d_far)
            down_pair.start()

        i = square(k)
        rows = r.d_full[i]
        delta = []
        for g in range(2):
            grad = dot_nn(rows, w_out(g))
            inner = []
            for h in range(2):
                part = grad[:, h * HEAD : (h + 1) * HEAD].astype(BF16)
                r.dos[g, h * ROWS : (h + 1) * ROWS] = part
                prod = part.astype(F32) * r.os[g, i, h * ROWS : (h + 1) * ROWS].astype(F32)
                inner.append(jnp.sum(prod.T, axis=0, keepdims=True))
            delta.append(jnp.concatenate(inner, axis=1))
        zero = jnp.zeros((HEAD, 512), F32)
        state = lax.fori_loop(0, i, lambda j, s: back_step(i, j, s, False, delta), (zero, zero))
        state = back_step(i, i, state, True, delta)
        for g in range(2):
            for h in range(2):
                grad = turn_back(state[g][:, h * ROWS : (h + 1) * ROWS].T * SCORE_SCALE, i)
                low, part = unnorm(r.qkp[g, i, :, h * HEAD : (h + 1) * HEAD], query_gain, grad)
                r.dgu[g, i, :, h * HEAD : (h + 1) * HEAD] = low
                gain_sum = gain_sum + part
        return gain_sum

    q_gain_part = lax.fori_loop(0, 4, back_block, jnp.zeros((1, HEAD), F32))

    other = pl.ds(flip(core), 1)
    whole = (both, both, both, both)

    def core_sum(kind, buf, copy):
        copy.wait_recv()
        index = (*whole, lane)
        total = grads[kind][index].astype(F32) + buf[...].astype(F32)
        grads[kind][index] = total.astype(BF16)

    def key_block(j, gain_sum):
        for g in range(2):
            grad = turn_back(r.dk[g, j] * SCORE_SCALE, j)
            low, part = unnorm(r.qkp[g, j, :, 256:384], key_gain, grad)
            r.dgu[g, j, :, 256:384] = low
            r.dgu[g, j, :, 384:512] = r.dv[g, j].astype(BF16)
            gain_sum = gain_sum + part
        return gain_sum

    k_gain_part = lax.fori_loop(0, 4, key_block, jnp.zeros((1, HEAD), F32))
    r.gains[2:3, 0:HEAD] = q_gain_part
    r.gains[2:3, HEAD : 2 * HEAD] = k_gain_part

    def qkv_grads(p, carry):
        cols = pl.ds(pl.multiple_of(256 * p, 256), 256)
        rows_t = r.a_full[:, :, cols].reshape(SEQ, 256)
        for g in range(2):
            grad = dot_tn(rows_t, r.dgu[g, :, :, 0:QKV].reshape(SEQ, QKV))
            r.m_full[g, p // 2, p % 2] = grad.reshape(2, 2, 64, QKV).astype(BF16)
        return carry

    def out_grads(p, carry):
        cols = pl.ds(pl.multiple_of(256 * p, 256), 256)
        grads_t = r.d_full[:, :, cols].reshape(SEQ, 256)
        for g in range(2):
            heads = r.os[g]
            mixed = jnp.concatenate(
                [heads[:, :ROWS].reshape(SEQ, HEAD), heads[:, ROWS:].reshape(SEQ, HEAD)], axis=1
            )
            r.w_o[g, p // 2, p % 2] = dot_tn(grads_t, mixed).reshape(2, 2, 64, OW).astype(BF16)
        return carry

    lax.fori_loop(0, 4, qkv_grads, 0)
    q_core = send(r.m_full.at[(*whole, other)], r.core_q, "c", "q_core")
    lax.fori_loop(0, 4, out_grads, 0)
    o_core = send(r.w_o.at[(*whole, other)], r.core_o, "c", "o_core")
    reduce_add("w", 2, back_w[2])
    start(back_w[1])
    flush()

    def part_da(blk):
        acc = dot_nt(r.dgu[0, blk, :, 0:QKV], w_qkv(0)) + dot_nt(r.dgu[1, blk, :, 0:QKV], w_qkv(1))
        r.gains[0:1] += jnp.sum(acc * r.a_full[blk].astype(F32), axis=0, keepdims=True)
        return acc

    back_o = {step: reduce_later("o", step) for step in range(4)}
    back_q = {step: reduce_later("q", step) for step in range(4)}

    def tail_q():
        core_sum("q", r.core_q, q_core)
        start(back_q[3])

    def tail_o():
        core_sum("o", r.core_o, o_core)
        start(back_o[3])

    a_relay, a_finish = square_sum(part_da, {1: tail_q, 3: tail_o})

    gain_links = ["c", "za", "zb", "yo", "xo", "y", "x"]

    def gain_send(n):
        return send(r.gains, r.gain_in.at[n], gain_links[n], ("gain", n))

    def gain_add(n, copy):
        copy.wait_send()
        copy.wait_recv()
        r.gains[...] += r.gain_in[n]

    sum_pair = r.w_m.at[own_slot]
    back_x = later(sum_pair, r.mlp_x, "x", "mlp_x", gives=lends == 1, takes=lends == 0)
    back_y0 = later(r.mlp_x, r.raw.at[0], "y", "raw_y", gives=role == 0, takes=role == 0)
    back_y1 = later(sum_pair, r.raw.at[0], "y", "raw_y", gives=role == 1, takes=role == 1)
    mlp_back_c = later(r.mlp_sum.at[flip(core)], r.mlp_c, "c", "raw_c0", gives=lends == 0, takes=lends == 1)

    def reduce_next(kind, step, back):
        reduce_add(kind, step, back[step])
        start(back[step - 1])

    g_step = gain_send(0)
    reduce_next("w", 1, back_w)
    gain_add(0, g_step)
    g_step = gain_send(1)
    reduce_next("q", 3, back_q)
    a_relay()
    reduce_next("o", 3, back_o)
    gain_add(1, g_step)
    g_step = gain_send(2)
    reduce_add("w", 0, back_w[0])
    back_x.start()
    back_y1.start()
    r.layer_out[...] = reorder(down_finish()).astype(BF16)
    reduce_next("q", 2, back_q)
    reduce_next("o", 2, back_o)
    gain_add(2, g_step)
    g_step = gain_send(3)
    back_x.wait_recv()
    back_y0.start()
    reduce_next("q", 1, back_q)
    reduce_next("o", 1, back_o)
    gain_add(3, g_step)
    g_step = gain_send(4)

    def last_step(kind, group, cols):
        for part in range(4):
            rows = pl.ds(16 * part, 16)
            group[part].wait_recv()
            total = grads[kind][(*own_view, lane, rows)].astype(F32) + getattr(r, f"sum_{kind}_{part}_0")[...].astype(F32)
            r.attn_sum[16 * part : 16 * part + 16, cols] = total.reshape(16, -1)
        r.attn_low[:, cols] = r.attn_sum[:, cols].astype(BF16)

    last_step("o", back_o[0], slice(QKV, AW))
    last_step("q", back_q[0], slice(0, QKV))
    attn_back = send(r.attn_low, r.attn_x, "x", "swap_q", gives=odd, takes=odd)
    gain_add(4, g_step)
    g_step = gain_send(5)

    rows_x = rows_in()
    inv_a = row_scale(rows_x)
    scaled = a_finish() * attn_gain
    inner = jnp.mean(scaled * rows_x, axis=-1, keepdims=True)
    r.input_grad[...] = reorder(r.resid[...] + inv_a * scaled - rows_x * (inv_a * inv_a * inv_a * inner))
    gain_add(5, g_step)
    g_step = gain_send(6)
    back_y0.wait_recv()
    back_y1.wait_recv()

    @pl.when(role == 0)
    def _():
        r.mlp_sum[...] = sum_pair[...].astype(F32) + r.raw[0].astype(F32)

    @pl.when(role == 1)
    def _():
        r.mlp_sum[...] = r.mlp_x[...].astype(F32) + r.raw[0].astype(F32)

    mlp_back_c.start()

    @pl.when(lends == 0)
    def _():
        r.d_mlp[...] = r.mlp_sum[core]

    @pl.when(x_hi == 0)
    def _():
        r.d_attn[...] = r.attn_sum[...]

    attn_back.wait_recv()

    @pl.when(odd)
    def _():
        r.d_attn[...] = r.attn_x[...].astype(F32)

    mlp_back_c.wait_recv()

    @pl.when(lends == 1)
    def _():
        r.d_mlp[...] = r.mlp_c[...]

    gain_add(6, g_step)
    sums = r.gains[...]
    r.d_gain[...] = reorder(sums)
    r.d_gain[0:1] = reorder(sums[0:1] / attn_gain)
    r.d_gain[2:3] = sums[2:3]
    flush()


def unpack(*refs):
    layer_in, input_in, d_attn, d_mlp, d_gain = refs[:5]
    (
        layer_out,
        input_grad,
        attn_gain,
        w_query,
        w_key,
        w_value,
        query_gain,
        key_gain,
        w_out,
        mlp_gain,
        w_gate,
        w_up,
        w_down,
    ) = refs[5:18]
    layer_out[...] = layer_in[...]
    input_grad[...] = input_in[...]
    attn_gain[...] = d_gain[0]
    mlp_gain[...] = d_gain[1]
    query_gain[...] = d_gain[2, 0:HEAD]
    key_gain[...] = d_gain[2, HEAD : 2 * HEAD]
    w_query[...] = d_attn[:, 0:256]
    w_key[...] = d_attn[:, 256:384]
    w_value[...] = d_attn[:, 384:512]
    w_out[...] = d_attn[:, 512:768]
    w_gate[...] = d_mlp[:, 0:HID]
    w_up[...] = d_mlp[:, HID : 2 * HID]
    w_down[...] = d_mlp[:, 2 * HID : MW]


def rope_table():
    position = np.arange(SEQ, dtype=np.float32)[:, None]
    channel = np.arange(HEAD // 2, dtype=np.float32)[None, :]
    rate = np.exp(channel * np.float32(-2.0 * math.log(ROPE_BASE) / HEAD)).astype(np.float32)
    angle = (position * rate).astype(np.float32).astype(np.float64)
    cos = np.cos(angle).astype(np.float32)
    sin = np.sin(angle).astype(np.float32)
    return np.concatenate([cos, sin], axis=1).reshape(4, ROWS, HEAD)


def body(
    tokens,
    attn_gain,
    w_query,
    key_weight,
    value_weight,
    query_gain,
    key_gain,
    w_out,
    mlp_gain,
    w_gate,
    w_up,
    w_down,
    out_cotangent,
):
    vmem = pl.BlockSpec(memory_space=pltpu.VMEM)

    def out(*shape):
        return jax.ShapeDtypeStruct(shape, F32)

    packed = pl.pallas_call(
        kernel,
        out_shape=(
            jax.ShapeDtypeStruct((ROWS, WIDTH), BF16),
            out(ROWS, WIDTH),
            out(64, AW),
            out(64, MW),
            out(8, WIDTH),
        ),
        in_specs=[vmem] * len(INPUTS),
        out_specs=(vmem,) * len(OUTPUTS),
        scratch_shapes=[pltpu.VMEM(*SCRATCH[name]) for name in NAMES]
        + [pltpu.SemaphoreType.DMA((N_SEM,)), pltpu.SemaphoreType.DMA((N_SEM,))],
        compiler_params=pltpu.CompilerParams(
            collective_id=0, has_side_effects=True, vmem_limit_bytes=64 * 2**20 - 2**17
        ),
        name="layer",
    )(
        tokens,
        out_cotangent,
        w_query,
        key_weight,
        value_weight,
        w_out.T,
        w_gate,
        w_up,
        w_down.T,
        attn_gain,
        mlp_gain,
        query_gain,
        key_gain,
        jnp.asarray(rope_table()),
    )
    parts = list(pl.pallas_call(
        unpack,
        out_shape=[
            jax.ShapeDtypeStruct((ROWS, WIDTH), BF16),
            out(ROWS, WIDTH),
            out(WIDTH),
            out(64, 256),
            out(64, HEAD),
            out(64, HEAD),
            out(HEAD),
            out(HEAD),
            out(64, 256),
            out(WIDTH),
            out(64, HID),
            out(64, HID),
            out(64, HID),
        ],
        in_specs=[vmem] * 5,
        out_specs=[vmem] * 13,
        name="unpack",
    )(*packed))
    parts[8] = parts[8].T
    parts[12] = parts[12].T
    return tuple(parts)


def solution(mesh):
    rows = P(("dp", "tensor"), None)
    first = P("dp", "tensor")
    second = P("tensor", "dp")
    whole = P()
    return jax.shard_map(
        body,
        mesh=mesh,
        in_specs=(
            rows,
            whole,
            first,
            first,
            first,
            whole,
            whole,
            second,
            whole,
            first,
            first,
            second,
            rows,
        ),
        out_specs=(
            rows,
            rows,
            whole,
            first,
            first,
            first,
            whole,
            whole,
            second,
            whole,
            first,
            first,
            second,
        ),
        check_vma=False,
    )
```

```python
import math

import jax
import jax.numpy as jnp
import numpy as np
from jax import lax
from jax.experimental import pallas as pl
from jax.experimental.pallas import tpu as pltpu
from jax.sharding import PartitionSpec as P

HEAD = 128
SEQ = 1024
WIDTH = 1024
ROWS = 256
QKV = 512
OW = 256
AW = QKV + OW
HID = 384
MW = 3 * HID
EPS = 1e-06
ROPE_BASE = 1000000.0
EXP_SCALE = math.log2(math.e) / math.sqrt(HEAD)
SCORE_SCALE = 1.0 / math.sqrt(HEAD)
MESH = pl.DeviceIdType.MESH
F32 = jnp.float32
BF16 = jnp.bfloat16


def dot_nn(a, b):
    return jnp.dot(a, b, preferred_element_type=F32)


def dot_nt(a, b):
    return lax.dot_general(a, b, (((1,), (1,)), ((), ())), preferred_element_type=F32)


def dot_tn(a, b):
    return lax.dot_general(a, b, (((0,), (0,)), ((), ())), preferred_element_type=F32)


def reorder(v):
    return jnp.concatenate([v[:, :512], v[:, 768:], v[:, 512:768]], axis=1)


def row_scale(v):
    return lax.rsqrt(jnp.mean(v * v, axis=-1, keepdims=True) + EPS)


def flip(bit):
    return 1 - bit


SCRATCH = {
    "w_q": ((2, 2, 2, 2, 2, 64, QKV), BF16),
    "w_o": ((2, 2, 2, 2, 2, 64, OW), BF16),
    "w_m": ((2, 2, 2, 2, 2, 64, MW), BF16),
    "pack_q": ((64, QKV), BF16),
    "pack_o": ((64, OW), BF16),
    "pack_m": ((64, MW), BF16),
    "a_full": ((4, ROWS, WIDTH), BF16),
    "m_full": ((2, 2, 2, 2, 2, 64, 512), BF16),
    "c_full": ((4, ROWS, WIDTH), BF16),
    "d_full": ((4, ROWS, WIDTH), BF16),
    "qkp": ((2, 4, ROWS, 384), F32),
    "qs": ((2, 4, 512, HEAD), BF16),
    "ks": ((2, 4, ROWS, HEAD), BF16),
    "kt": ((2, 4, HEAD, ROWS), BF16),
    "vs": ((2, 4, ROWS, HEAD), BF16),
    "vt": ((2, 4, HEAD, ROWS), BF16),
    "os": ((2, 4, 512, HEAD), BF16),
    "linv": ((2, 4, 8, 512), F32),
    "dos": ((2, 512, HEAD), BF16),
    "dk": ((2, 4, ROWS, HEAD), F32),
    "dv": ((2, 4, ROWS, HEAD), F32),
    "hid": ((2, 4, ROWS, HID), BF16),
    "dgu": ((2, 4, ROWS, 2 * HID), BF16),
    "own": ((ROWS, WIDTH), F32),
    "resid": ((ROWS, WIDTH), F32),
    "stage": ((3, ROWS, WIDTH), BF16),
    "w_dn": ((2, WIDTH, HID), BF16),
    "far": ((2, 128, WIDTH), BF16),
    "near": ((2, ROWS, WIDTH), BF16),
    "sum_m": ((3, ROWS, WIDTH), BF16),
    "sum_d": ((3, ROWS, WIDTH), BF16),
    "gains": ((8, WIDTH), F32),
    "gain_in": ((7, 8, WIDTH), F32),
    "core_q": ((2, 2, 2, 2, 1, 64, QKV), BF16),
    "core_o": ((2, 2, 2, 2, 1, 64, OW), BF16),
    "raw": ((2, 2, 64, MW), BF16),
    "mlp_x": ((2, 64, MW), BF16),
    "mlp_c": ((64, MW), F32),
    "attn_x": ((64, AW), BF16),
    "attn_low": ((64, AW), BF16),
    "attn_sum": ((64, AW), F32),
    "mlp_sum": ((2, 64, MW), F32),
}
AXES = {"xo": 3, "yo": 0, "za": 2, "zb": 1}
ORDER = ["xo", "yo", "za", "zb"]


def part_axes(part):
    return [ORDER[(part + step) % 4] for step in range(4)]


def cube_shape(part, step, cores, width):
    shape = [1, 1, 1, 1]
    for axis in part_axes(part)[:step]:
        shape[AXES[axis]] = 2
    return (*shape, cores, 16, width)


for _part in range(4):
    for _step in range(4):
        SCRATCH[f"sum_q_{_part}_{_step}"] = (cube_shape(_part, _step, 1, QKV), BF16)
        SCRATCH[f"sum_o_{_part}_{_step}"] = (cube_shape(_part, _step, 1, OW), BF16)
        SCRATCH[f"sum_w_{_part}_{_step}"] = (cube_shape(_part, _step, 2, MW), BF16)

NAMES = list(SCRATCH)
N_SEM = 109
INPUTS = ["tok", "cot", "wq", "wk", "wv", "wo", "wg", "wu", "wd", "ag", "mg", "qg", "kg", "rope"]
OUTPUTS = ["layer_out", "input_grad", "d_attn", "d_mlp", "d_gain"]


class Refs:
    pass


class Copy:
    def __init__(self, copy, gives, takes):
        self.copy, self.gives, self.takes = copy, gives, takes
        self.started = self.received = self.sent = False

    def run(self, cond, act):
        if cond is None:
            act()
        else:
            pl.when(cond)(act)

    def start(self):
        self.started = True
        self.run(self.gives, self.copy.start)

    def wait_recv(self):
        self.received = True
        self.run(self.takes, self.copy.wait_recv)

    def wait_send(self):
        self.sent = True
        self.run(self.gives, self.copy.wait_send)


def kernel(*refs):
    r = Refs()
    names = INPUTS + OUTPUTS + NAMES
    for name, ref in zip(names, refs):
        setattr(r, name, ref)
    ssem, rsem = refs[len(names)], refs[len(names) + 1]

    dp = lax.axis_index("dp")
    tn = lax.axis_index("tensor")
    z = dp // 4
    x_hi = (dp // 2) % 2
    core = dp % 2
    y = tn // 2
    x_lo = tn % 2
    y_lo = y % 2
    y_hi = y // 2
    gz = jnp.where(z < 2, z, 5 - z)
    own_bit = {"xo": x_hi, "yo": y_hi, "za": gz % 2, "zb": gz // 2}
    nbr = {
        "c": (dp + 1 - 2 * core, tn),
        "x": (dp, tn + 1 - 2 * x_lo),
        "y": (dp, tn + 2 - 4 * y_lo),
        "xo": (dp + 2 - 4 * x_hi, tn + 1 - 2 * x_lo),
        "yo": (dp, (3 - y) * 2 + x_lo),
        "za": (dp + 4 - 8 * (z % 2), tn),
        "zb": (dp + 4 * (3 - 2 * z), tn),
    }
    links = list(nbr)
    pair = "p"
    nbr["p"] = (dp, tn + jnp.where(core == 0, 2 - 4 * y_lo, 1 - 2 * x_lo))
    kx = (x_lo + x_hi) % 2
    lends = (core + x_lo) % 2
    role = 2 * lends + kx

    def square(k):
        kx, ky = k % 2, k // 2
        return (y_lo + ky - 2 * y_lo * ky) * 2 + x_lo + kx - 2 * x_lo * kx

    def group(k):
        kc = k % 2
        return (k // 2) * 2 + core + kc - 2 * core * kc

    ids = {}
    copies = r.copies = []
    unsent = []

    def later(src, dst, to, key, gives=None, takes=None):
        i = ids.setdefault(key, len(ids))
        copy = pltpu.make_async_remote_copy(
            src_ref=src,
            dst_ref=dst,
            send_sem=ssem.at[i],
            recv_sem=rsem.at[i],
            device_id=nbr[to],
            device_id_type=MESH,
        )
        copies.append(Copy(copy, gives, takes))
        unsent.append(copies[-1])
        return copies[-1]

    def send(*args, **kinds):
        copy = later(*args, **kinds)
        copy.start()
        return copy

    def flush():
        for copy in unsent:
            if copy.started and not copy.sent:
                copy.wait_send()
        unsent[:] = [copy for copy in unsent if not copy.sent]

    def wait_recv(group):
        for copy in group:
            copy.wait_recv()

    def at(k, value, act):
        pl.when(k == value)(act)

    def slots(full, current, cores):
        index = [None] * 4
        for axis in ORDER:
            if axis in full:
                index[AXES[axis]] = pl.ds(0, 2)
            else:
                bit = own_bit[axis]
                index[AXES[axis]] = pl.ds(flip(bit) if current == axis else bit, 1)
        return (*index, cores)

    both = pl.ds(0, 2)
    lane = pl.ds(core, 1)
    lanes = {"q": lane, "o": lane, "w": both}
    weights = {"q": r.w_q, "o": r.w_o, "w": r.w_m}
    grads = {"q": r.m_full, "o": r.w_o, "w": r.w_m}
    own_slot = (own_bit["yo"], own_bit["zb"], own_bit["za"], own_bit["xo"])
    own_view = tuple(pl.ds(bit, 1) for bit in own_slot)

    def step_key(kind, part, step, back):
        return (kind, part, step, back and kind == "w" and step == 3)

    def gather_later(kind, step):
        out = []
        for part in range(4):
            axes = part_axes(part)
            rows = pl.ds(16 * part, 16)
            view = weights[kind].at[(*slots(axes[:step], None, lanes[kind]), rows)]
            out.append(later(view, view, axes[step], step_key(kind, part, step, False)))
        return out

    def core_later(kind, late):
        out = []
        for part in range(4):
            axes = part_axes(part)
            rows = pl.ds(16 * part, 16)
            view = weights[kind].at[(*slots(axes[:3], axes[3] if late else None, lane), rows)]
            out.append(later(view, view, "c", ("core", kind, late, part)))
        return out

    def reduce_later(kind, step):
        out = []
        for part in range(4):
            axes = part_axes(part)
            rows = pl.ds(16 * part, 16)
            view = grads[kind].at[(*slots(axes[:step], axes[step], lanes[kind]), rows)]
            buf = getattr(r, f"sum_{kind}_{part}_{step}")
            out.append(later(view, buf, axes[step], step_key(kind, part, step, True)))
        return out

    def start(group):
        for copy in group:
            copy.start()

    def reduce_add(kind, step, group):
        for part in range(4):
            axes = part_axes(part)
            rows = pl.ds(16 * part, 16)
            index = (*slots(axes[:step], None, lanes[kind]), rows)
            group[part].wait_recv()
            total = grads[kind][index].astype(F32) + getattr(r, f"sum_{kind}_{part}_{step}")[...].astype(F32)
            grads[kind][index] = total.astype(BF16)

    barrier = pltpu.get_barrier_semaphore()
    for to in links:
        pl.semaphore_signal(barrier, inc=1, device_id=nbr[to], device_id_type=MESH)

    r.pack_q[:, 0:256] = r.wq[...]
    r.pack_q[:, 256:384] = r.wk[...]
    r.pack_q[:, 384:512] = r.wv[...]
    r.pack_o[...] = r.wo[...]
    r.pack_m[:, 0:HID] = r.wg[...]
    r.pack_m[:, HID : 2 * HID] = r.wu[...]
    r.pack_m[:, 2 * HID : MW] = r.wd[...]

    @pl.when(x_hi == 0)
    def _():
        r.w_q[(*own_view, lane)] = r.pack_q[...].reshape(1, 1, 1, 1, 1, 64, QKV)
        r.w_o[(*own_view, lane)] = r.pack_o[...].reshape(1, 1, 1, 1, 1, 64, OW)

    @pl.when(lends == 0)
    def _():
        r.raw[0, pl.ds(core, 1)] = r.pack_m[...].reshape(1, 64, MW)

    attn_gain = reorder(r.ag[...].astype(F32).reshape(1, WIDTH))
    mlp_gain = reorder(r.mg[...].astype(F32).reshape(1, WIDTH))
    query_gain = r.qg[...].astype(F32).reshape(1, HEAD)
    key_gain = r.kg[...].astype(F32).reshape(1, HEAD)

    def rows_in():
        return reorder(r.tok[...].astype(F32))

    rows_x = rows_in()
    r.a_full[square(0)] = (rows_x * row_scale(rows_x) * attn_gain).astype(BF16)
    r.c_full[group(0)] = reorder(r.cot[...])
    pl.semaphore_wait(barrier, len(links))

    odd = x_hi == 1
    swap_q = send(r.pack_q, r.w_q.at[(*own_slot, core)], "x", "swap_q", gives=odd, takes=odd)
    swap_o = send(r.pack_o, r.w_o.at[(*own_slot, core)], "x", "swap_o", gives=odd, takes=odd)
    mlp_pair = r.w_m.at[own_slot]
    raw_y = send(r.pack_m, r.raw.at[1, core], "y", "raw_y")
    raw_c0 = send(r.pack_m, r.raw.at[0, core], "c", "raw_c0", gives=lends == 1, takes=lends == 0)
    raw_c1 = later(r.raw.at[1, core], r.raw.at[1, core], "c", "raw_c1", gives=lends == 1, takes=lends == 0)
    mlp_to_x = later(r.raw.at[1 - kx], mlp_pair, "x", "mlp_x", gives=lends == 0, takes=lends == 1)

    def square_gather(buf):
        def half(k, n):
            return buf.at[square(k), pl.ds(128 * n, 128)]

        x0 = send(half(0, 0), half(0, 0), "x", "sg_x0")
        y1 = send(half(0, 1), half(0, 1), "y", "sg_y1")
        x1 = later(half(0, 1), half(0, 1), "x", "sg_x1")
        y0 = later(half(0, 0), half(0, 0), "y", "sg_y0")
        fy = later(half(1, 0), half(1, 0), "y", "sg_fy")
        fx = later(half(2, 1), half(2, 1), "x", "sg_fx")

        def second():
            x1.start()
            y0.start()

        def forward():
            x0.wait_recv()
            fy.start()
            y1.wait_recv()
            fx.start()

        return second, forward, x1, y0, [fx, fy]

    a_second, a_forward, a_x1, a_y0, a_far = square_gather(r.a_full)
    gather = {kind: [gather_later(kind, step) for step in range(4)] for kind in "qow"}
    to_core = {kind: [core_later(kind, late) for late in (False, True)] for kind in "qo"}

    def advance(kind, step):
        wait_recv(gather[kind][step - 1])
        start(gather[kind][step])

    swap_q.wait_recv()
    start(gather["q"][0])
    raw_y.wait_recv()
    raw_c1.start()
    swap_o.wait_recv()
    advance("q", 1)
    start(gather["o"][0])
    raw_c0.wait_recv()
    raw_c1.wait_recv()
    mlp_to_x.start()
    advance("q", 2)
    advance("o", 1)
    a_forward()

    @pl.when(lends == 0)
    def _():
        r.w_m[own_view] = r.raw[pl.ds(kx, 1)].reshape(1, 1, 1, 1, 2, 64, MW)

    advance("q", 3)
    start(to_core["q"][0])
    advance("o", 2)
    mlp_to_x.wait_recv()
    start(gather["w"][0])
    a_second()
    wait_recv(gather["q"][3])
    start(to_core["q"][1])
    advance("o", 3)
    start(to_core["o"][0])
    advance("w", 1)
    wait_recv(to_core["q"][0])
    wait_recv(to_core["q"][1])

    def w_qkv(g):
        return r.w_q[g].reshape(WIDTH, QKV)

    def w_out(g):
        return r.w_o[g].reshape(WIDTH, OW)

    def w_gu(g):
        return r.w_m[g, :, :, :, :, :, 0 : 2 * HID].reshape(WIDTH, 2 * HID)

    def w_dn(g):
        return r.w_dn[g]

    c_pair = later(r.c_full.at[group(0)], r.c_full.at[core + 2], pair, "cot_p")
    c_core = later(r.c_full.at[group(0)], r.c_full.at[group(0)], "c", "cot_c")

    first_half = lax.broadcasted_iota(jnp.int32, (ROWS, HEAD), 1) < HEAD // 2

    def turns(blk):
        table = r.rope[blk]
        swapped = pltpu.roll(table, 64, 1)
        return jnp.where(first_half, table, swapped), jnp.where(first_half, -swapped, table)

    def qkv_block(k, carry):
        @pl.when(k == 1)
        def _():
            a_x1.wait_recv()
            c_pair.start()
            c_core.start()

        @pl.when(k == 2)
        def _():
            a_y0.wait_recv()
            wait_recv(gather["o"][3])
            start(to_core["o"][1])
            advance("w", 2)

        @pl.when(k == 3)
        def _():
            wait_recv(a_far)

        blk = square(k)
        rows = r.a_full[blk]
        cos, sin = turns(blk)
        for g in range(2):
            acc = dot_nn(rows, w_qkv(g))
            r.qkp[g, blk] = acc[:, :384]
            for h in range(3):
                pre = acc[:, h * HEAD : (h + 1) * HEAD]
                normed = pre * row_scale(pre) * (key_gain if h == 2 else query_gain)
                turned = normed * cos + pltpu.roll(normed, 64, 1) * sin
                if h == 2:
                    r.ks[g, blk] = turned.astype(BF16)
                    r.kt[g, blk] = turned.T.astype(BF16)
                else:
                    r.qs[g, blk, h * ROWS : (h + 1) * ROWS] = turned.astype(BF16)
            value = acc[:, 384:]
            r.vs[g, blk] = value.astype(BF16)
            r.vt[g, blk] = value.T.astype(BF16)
        return carry

    lax.fori_loop(0, 4, qkv_block, 0)

    key_at = lax.broadcasted_iota(jnp.int32, (ROWS, 512), 0)
    query_at = lax.broadcasted_iota(jnp.int32, (ROWS, 512), 1) % ROWS
    visible = key_at <= query_at

    def weights_t(g, i, j, diagonal):
        scores = dot_nt(r.ks[g, j], r.qs[g, i])
        exps = jnp.exp2(scores * EXP_SCALE)
        if diagonal:
            exps = jnp.where(visible, exps, 0.0)
        return exps

    def attend_step(i, j, carry, diagonal):
        out = []
        for g in range(2):
            total, acc = carry[g]
            exps = weights_t(g, i, j, diagonal)
            total = total + jnp.sum(exps, axis=0, keepdims=True)
            acc = acc + dot_nn(r.vt[g, j], exps.astype(BF16))
            out.append((total, acc))
        return tuple(out)

    def attend_block(i):
        zero = (jnp.zeros((1, 512), F32), jnp.zeros((HEAD, 512), F32))
        state = lax.fori_loop(0, i, lambda j, s: attend_step(i, j, s, False), (zero, zero))
        state = attend_step(i, i, state, True)
        for g in range(2):
            total, acc = state[g]
            inv = 1.0 / total
            r.linv[g, i] = jnp.broadcast_to(inv, (8, 512))
            r.os[g, i] = (acc * inv).T.astype(BF16)

    def part_o(blk):
        acc = jnp.zeros((ROWS, WIDTH), F32)
        for g in range(2):
            heads = r.os[g, blk]
            acc = acc + dot_nt(jnp.concatenate([heads[:ROWS], heads[ROWS:]], axis=1), w_out(g))
        return acc

    def square_sum(part_of, steps):
        def out(n, rows, buf, to, key):
            return later(r.stage.at[n, pl.ds(*rows)], buf, to, key)

        low, high = (0, 128), (128, 128)
        d0 = out(2, low, r.far.at[0], "x", "ss_d0")
        d1 = out(2, high, r.far.at[1], "y", "ss_d1")
        x0 = out(0, low, r.near.at[0, pl.ds(*low)], "x", "ss_x0")
        x1 = out(0, high, r.near.at[0, pl.ds(*high)], "x", "ss_x1")
        y0 = out(1, low, r.near.at[1, pl.ds(*low)], "y", "ss_y0")
        y1 = out(1, high, r.near.at[1, pl.ds(*high)], "y", "ss_y1")

        def block(n, carry):
            k = jnp.where(n == 0, 3, n % 3)
            for value, act in steps.items():
                at(n, value, act)
            acc = part_of(square(k))

            @pl.when(n < 3)
            def _():
                r.stage[(n + 2) % 3] = acc.astype(BF16)

            @pl.when(n == 3)
            def _():
                r.own[...] = acc

            @pl.when(n == 0)
            def _():
                d0.start()
                d1.start()

            at(n, 2, x0.start)
            at(n, 3, y1.start)
            return carry

        lax.fori_loop(0, 4, block, 0)

        def relay():
            d1.wait_recv()
            r.stage[0, 128:256] = (r.stage[0, 128:256].astype(F32) + r.far[1].astype(F32)).astype(BF16)
            x1.start()
            d0.wait_recv()
            r.stage[1, 0:128] = (r.stage[1, 0:128].astype(F32) + r.far[0].astype(F32)).astype(BF16)
            y0.start()

        def finish():
            wait_recv([x0, y1, x1, y0])
            return r.own[...] + r.near[0].astype(F32) + r.near[1].astype(F32)

        return relay, finish

    def attend_and_part(blk):
        attend_block(blk)

        @pl.when(blk == square(3))
        def _():
            wait_recv(to_core["o"][0])
            wait_recv(to_core["o"][1])

        return part_o(blk)

    o_relay, o_finish = square_sum(attend_and_part, {3: lambda: advance("w", 3)})
    o_relay()
    c_pair.wait_recv()
    c_forward = send(r.c_full.at[core + 2], r.c_full.at[core + 2], "c", "cot_f")
    resid = rows_in() + o_finish()
    r.resid[...] = resid
    normed = (resid * row_scale(resid) * mlp_gain).astype(BF16)
    for half in range(2):
        r.m_full[0, pl.ds(core, 1), half] = normed[:, 512 * half : 512 * half + 512].reshape(1, 2, 2, 64, 512)
    m_pair = []
    m_forward = []
    for n in range(2):
        near_rows, far_rows = (r.m_full.at[place, core, :, n] for place in range(2))
        m_pair.append(send(near_rows, far_rows, pair, ("m_p", n)))
        m_forward.append(later(far_rows, far_rows, "c", ("m_f", n)))
    m_core = send(r.m_full.at[0, core], r.m_full.at[0, core], "c", "m_c")
    wait_recv(gather["w"][3])
    r.w_dn[...] = r.w_m[:, :, :, :, :, :, 2 * HID : MW].reshape(2, WIDTH, HID)
    wait_recv([c_core, c_forward])

    def mlp_block(k, carry):
        at(k, 1, m_core.wait_recv)

        @pl.when(k == 2)
        def _():
            for n in range(2):
                m_pair[n].wait_recv()
                m_forward[n].start()

        @pl.when(k == 3)
        def _():
            wait_recv(m_forward)

        i = group(k)
        rows = jnp.concatenate([r.m_full[i // 2, i % 2, half].reshape(ROWS, 512) for half in range(2)], axis=1)
        cots = r.c_full[i]
        for g in range(2):
            pre = dot_nn(rows, w_gu(g))
            grad = dot_nn(cots, w_dn(g))
            gate = pre[:, :HID]
            up = pre[:, HID:]
            sig = 1.0 / (1.0 + jnp.exp(-gate))
            act = gate * sig
            r.hid[g, i] = (act * up).astype(BF16)
            r.dgu[g, i, :, 0:HID] = (grad * up * sig * (1.0 + gate * (1.0 - sig))).astype(BF16)
            r.dgu[g, i, :, HID : 2 * HID] = (grad * act).astype(BF16)
        return carry

    def pair_sum(part_of, recv, own, name, hold):
        stage = r.stage
        s3 = later(stage.at[2], recv.at[0], "c", (name, 3))
        s1 = later(stage.at[0], recv.at[1], "c", (name, 1))
        s2 = later(stage.at[1], recv.at[2], pair, (name, 2))

        def block(n, carry):
            acc = part_of(group(n + (n // 2) * (5 - 2 * n)))

            @pl.when(n == 0)
            def _():
                own[...] = own[...] + acc if hold else acc

            @pl.when(n == 1)
            def _():
                stage[0] = acc.astype(BF16)
                s1.start()

            @pl.when(n == 2)
            def _():
                stage[2] = acc.astype(BF16)
                s3.start()

            @pl.when(n == 3)
            def _():
                s3.wait_recv()
                stage[1] = (acc + recv[0].astype(F32)).astype(BF16)
                if not hold:
                    s2.start()

            return carry

        def finish():
            wait_recv([s1, s2])
            return own[...] + recv[1].astype(F32) + recv[2].astype(F32)

        return block, finish, s2

    def part_dm(i):
        return dot_nt(r.dgu[0, i], w_gu(0)) + dot_nt(r.dgu[1, i], w_gu(1))

    def part_down(i):
        return dot_nt(r.hid[0, i], w_dn(0)) + dot_nt(r.hid[1, i], w_dn(1))

    dm_block, dm_finish, _ = pair_sum(part_dm, r.sum_m, r.own, "dm", False)
    flush()
    lax.fori_loop(0, 2, mlp_block, 0)
    lax.fori_loop(0, 2, dm_block, 0)
    lax.fori_loop(2, 4, mlp_block, 0)
    lax.fori_loop(2, 4, dm_block, 0)

    def mlp_grads(p, carry):
        cols = pl.ds(pl.multiple_of(256 * p, 256), 256)
        half_cols = pl.ds(pl.multiple_of(256 * (p % 2), 256), 256)
        rows_t = r.m_full[:, :, p // 2, :, :, :, half_cols].reshape(SEQ, 256)
        cots_t = r.c_full[:, :, cols].reshape(SEQ, 256)
        for g in range(2):
            grad_gu = dot_tn(rows_t, r.dgu[g].reshape(SEQ, 2 * HID))
            grad_dn = dot_tn(cots_t, r.hid[g].reshape(SEQ, HID))
            r.w_m[g, p // 2, p % 2, :, :, :, 0 : 2 * HID] = grad_gu.reshape(2, 2, 64, 2 * HID).astype(BF16)
            r.w_m[g, p // 2, p % 2, :, :, :, 2 * HID : MW] = grad_dn.reshape(2, 2, 64, HID).astype(BF16)
        return carry

    lax.fori_loop(0, 4, mlp_grads, 0)
    back_w = {step: reduce_later("w", step) for step in range(4)}
    flush()
    start(back_w[3])

    dm = dm_finish()
    resid = r.resid[...]
    inv_m = row_scale(resid)
    scaled = dm * mlp_gain
    inner = jnp.mean(scaled * resid, axis=-1, keepdims=True)
    r.gains[...] = jnp.zeros((8, WIDTH), F32)
    r.gains[1:2] = jnp.sum(dm * resid * inv_m, axis=0, keepdims=True)
    dresid = reorder(r.cot[...].astype(F32)) + inv_m * scaled - resid * (inv_m * inv_m * inv_m * inner)
    r.input_grad[...] = resid
    r.resid[...] = dresid
    r.d_full[square(0)] = dresid.astype(BF16)
    d_second, d_forward, d_x1, d_y0, d_far = square_gather(r.d_full)
    down_block, down_finish, down_pair = pair_sum(part_down, r.sum_d, r.input_grad, "down", True)
    lax.fori_loop(0, 4, down_block, 0)
    d_second()
    r.dk[...] = jnp.zeros((2, 4, ROWS, HEAD), F32)
    r.dv[...] = jnp.zeros((2, 4, ROWS, HEAD), F32)

    def back_step(i, j, carry, diagonal, delta):
        out = []
        for g in range(2):
            probs = weights_t(g, i, j, diagonal) * r.linv[g, i, 0:1]
            grads = dot_nt(r.vs[g, j], r.dos[g])
            dz = (probs * (grads - delta[g])).astype(BF16)
            r.dv[g, j] += dot_nn(probs.astype(BF16), r.dos[g])
            r.dk[g, j] += dot_nn(dz, r.qs[g, i])
            out.append(carry[g] + dot_nn(r.kt[g, j], dz))
        return tuple(out)

    def unnorm(pre, gain, grad):
        inv = row_scale(pre)
        hat = pre * inv
        scaled = grad * gain
        back = inv * (scaled - hat * jnp.mean(scaled * hat, axis=-1, keepdims=True))
        return back.astype(BF16), jnp.sum(grad * hat, axis=0, keepdims=True)

    def turn_back(grad, blk):
        cos, sin = turns(blk)
        return grad * cos - pltpu.roll(grad, 64, 1) * sin

    def back_block(k, gain_sum):
        @pl.when(k == 1)
        def _():
            d_forward()
            d_x1.wait_recv()

        @pl.when(k == 2)
        def _():
            d_y0.wait_recv()
            reduce_add("w", 3, back_w[3])
            start(back_w[2])

        @pl.when(k == 3)
        def _():
            wait_recv(d_far)
            down_pair.start()

        i = square(k)
        rows = r.d_full[i]
        delta = []
        for g in range(2):
            grad = dot_nn(rows, w_out(g))
            inner = []
            for h in range(2):
                part = grad[:, h * HEAD : (h + 1) * HEAD].astype(BF16)
                r.dos[g, h * ROWS : (h + 1) * ROWS] = part
                prod = part.astype(F32) * r.os[g, i, h * ROWS : (h + 1) * ROWS].astype(F32)
                inner.append(jnp.sum(prod.T, axis=0, keepdims=True))
            delta.append(jnp.concatenate(inner, axis=1))
        zero = jnp.zeros((HEAD, 512), F32)
        state = lax.fori_loop(0, i, lambda j, s: back_step(i, j, s, False, delta), (zero, zero))
        state = back_step(i, i, state, True, delta)
        for g in range(2):
            for h in range(2):
                grad = turn_back(state[g][:, h * ROWS : (h + 1) * ROWS].T * SCORE_SCALE, i)
                low, part = unnorm(r.qkp[g, i, :, h * HEAD : (h + 1) * HEAD], query_gain, grad)
                r.dgu[g, i, :, h * HEAD : (h + 1) * HEAD] = low
                gain_sum = gain_sum + part
        return gain_sum

    q_gain_part = lax.fori_loop(0, 4, back_block, jnp.zeros((1, HEAD), F32))

    other = pl.ds(flip(core), 1)
    whole = (both, both, both, both)

    def core_sum(kind, buf, copy):
        copy.wait_recv()
        index = (*whole, lane)
        total = grads[kind][index].astype(F32) + buf[...].astype(F32)
        grads[kind][index] = total.astype(BF16)

    def out_grads(p, carry):
        cols = pl.ds(pl.multiple_of(256 * p, 256), 256)
        grads_t = r.d_full[:, :, cols].reshape(SEQ, 256)
        for g in range(2):
            heads = r.os[g]
            mixed = jnp.concatenate(
                [heads[:, :ROWS].reshape(SEQ, HEAD), heads[:, ROWS:].reshape(SEQ, HEAD)], axis=1
            )
            r.w_o[g, p // 2, p % 2] = dot_tn(grads_t, mixed).reshape(2, 2, 64, OW).astype(BF16)
        return carry

    reduce_add("w", 2, back_w[2])
    start(back_w[1])
    lax.fori_loop(0, 4, out_grads, 0)
    o_core = send(r.w_o.at[(*whole, other)], r.core_o, "c", "o_core")
    def key_block(j, gain_sum):
        for g in range(2):
            grad = turn_back(r.dk[g, j] * SCORE_SCALE, j)
            low, part = unnorm(r.qkp[g, j, :, 256:384], key_gain, grad)
            r.dgu[g, j, :, 256:384] = low
            r.dgu[g, j, :, 384:512] = r.dv[g, j].astype(BF16)
            gain_sum = gain_sum + part
        return gain_sum

    k_gain_part = lax.fori_loop(0, 4, key_block, jnp.zeros((1, HEAD), F32))
    r.gains[2:3, 0:HEAD] = q_gain_part
    r.gains[2:3, HEAD : 2 * HEAD] = k_gain_part

    def qkv_grads(p, carry):
        cols = pl.ds(pl.multiple_of(256 * p, 256), 256)
        rows_t = r.a_full[:, :, cols].reshape(SEQ, 256)
        for g in range(2):
            grad = dot_tn(rows_t, r.dgu[g, :, :, 0:QKV].reshape(SEQ, QKV))
            r.m_full[g, p // 2, p % 2] = grad.reshape(2, 2, 64, QKV).astype(BF16)
        return carry

    sum_pair = r.w_m.at[own_slot]
    back_x = later(sum_pair, r.mlp_x, "x", "mlp_x", gives=lends == 1, takes=lends == 0)
    back_y0 = later(r.mlp_x, r.raw.at[0], "y", "raw_y", gives=role == 0, takes=role == 0)
    back_y1 = later(sum_pair, r.raw.at[0], "y", "raw_y", gives=role == 1, takes=role == 1)
    mlp_back_c = later(r.mlp_sum.at[flip(core)], r.mlp_c, "c", "raw_c0", gives=lends == 0, takes=lends == 1)

    lax.fori_loop(0, 4, qkv_grads, 0)
    flush()
    q_core = send(r.m_full.at[(*whole, other)], r.core_q, "c", "q_core")

    def part_da(blk):
        acc = dot_nt(r.dgu[0, blk, :, 0:QKV], w_qkv(0)) + dot_nt(r.dgu[1, blk, :, 0:QKV], w_qkv(1))
        r.gains[0:1] += jnp.sum(acc * r.a_full[blk].astype(F32), axis=0, keepdims=True)
        return acc

    back_o = {step: reduce_later("o", step) for step in range(4)}
    back_q = {step: reduce_later("q", step) for step in range(4)}

    def tail_q():
        core_sum("q", r.core_q, q_core)
        start(back_q[3])

    def tail_o():
        core_sum("o", r.core_o, o_core)
        start(back_o[3])

    a_relay, a_finish = square_sum(part_da, {0: tail_o, 1: tail_q})

    gain_links = ["c", "za", "zb", "yo", "xo", "y", "x"]

    def gain_send(n):
        return send(r.gains, r.gain_in.at[n], gain_links[n], ("gain", n))

    def gain_add(n, copy):
        copy.wait_send()
        copy.wait_recv()
        r.gains[...] += r.gain_in[n]

    def reduce_next(kind, step, back):
        reduce_add(kind, step, back[step])
        start(back[step - 1])

    g_step = gain_send(0)
    reduce_next("w", 1, back_w)
    gain_add(0, g_step)
    g_step = gain_send(1)
    reduce_next("o", 3, back_o)
    a_relay()
    reduce_next("q", 3, back_q)
    gain_add(1, g_step)
    g_step = gain_send(2)
    reduce_add("w", 0, back_w[0])
    back_x.start()
    back_y1.start()
    reduce_next("o", 2, back_o)
    r.layer_out[...] = reorder(down_finish()).astype(BF16)
    gain_add(2, g_step)
    g_step = gain_send(3)
    reduce_next("q", 2, back_q)
    reduce_next("o", 1, back_o)
    gain_add(3, g_step)
    g_step = gain_send(4)
    reduce_next("q", 1, back_q)

    def last_step(kind, group, cols):
        for part in range(4):
            rows = pl.ds(16 * part, 16)
            group[part].wait_recv()
            total = grads[kind][(*own_view, lane, rows)].astype(F32) + getattr(r, f"sum_{kind}_{part}_0")[...].astype(F32)
            r.attn_sum[16 * part : 16 * part + 16, cols] = total.reshape(16, -1)
        r.attn_low[:, cols] = r.attn_sum[:, cols].astype(BF16)

    last_step("o", back_o[0], slice(QKV, AW))
    rows_x = rows_in()
    inv_a = row_scale(rows_x)
    scaled = a_finish() * attn_gain
    inner = jnp.mean(scaled * rows_x, axis=-1, keepdims=True)
    r.input_grad[...] = reorder(r.resid[...] + inv_a * scaled - rows_x * (inv_a * inv_a * inv_a * inner))
    gain_add(4, g_step)
    g_step = gain_send(5)
    last_step("q", back_q[0], slice(0, QKV))
    attn_back = send(r.attn_low, r.attn_x, "x", "swap_q", gives=odd, takes=odd)
    back_x.wait_recv()
    back_y0.start()
    gain_add(5, g_step)
    g_step = gain_send(6)
    back_y0.wait_recv()
    back_y1.wait_recv()

    @pl.when(role == 0)
    def _():
        r.mlp_sum[...] = sum_pair[...].astype(F32) + r.raw[0].astype(F32)

    @pl.when(role == 1)
    def _():
        r.mlp_sum[...] = r.mlp_x[...].astype(F32) + r.raw[0].astype(F32)

    mlp_back_c.start()

    @pl.when(lends == 0)
    def _():
        r.d_mlp[...] = r.mlp_sum[core]

    @pl.when(x_hi == 0)
    def _():
        r.d_attn[...] = r.attn_sum[...]

    attn_back.wait_recv()

    @pl.when(odd)
    def _():
        r.d_attn[...] = r.attn_x[...].astype(F32)

    mlp_back_c.wait_recv()

    @pl.when(lends == 1)
    def _():
        r.d_mlp[...] = r.mlp_c[...]

    gain_add(6, g_step)
    sums = r.gains[...]
    r.d_gain[...] = reorder(sums)
    r.d_gain[0:1] = reorder(sums[0:1] / attn_gain)
    r.d_gain[2:3] = sums[2:3]
    flush()


def unpack(*refs):
    layer_in, input_in, d_attn, d_mlp, d_gain = refs[:5]
    (
        layer_out,
        input_grad,
        attn_gain,
        w_query,
        w_key,
        w_value,
        query_gain,
        key_gain,
        w_out,
        mlp_gain,
        w_gate,
        w_up,
        w_down,
    ) = refs[5:18]
    layer_out[...] = layer_in[...]
    input_grad[...] = input_in[...]
    attn_gain[...] = d_gain[0]
    mlp_gain[...] = d_gain[1]
    query_gain[...] = d_gain[2, 0:HEAD]
    key_gain[...] = d_gain[2, HEAD : 2 * HEAD]
    w_query[...] = d_attn[:, 0:256]
    w_key[...] = d_attn[:, 256:384]
    w_value[...] = d_attn[:, 384:512]
    w_out[...] = d_attn[:, 512:768]
    w_gate[...] = d_mlp[:, 0:HID]
    w_up[...] = d_mlp[:, HID : 2 * HID]
    w_down[...] = d_mlp[:, 2 * HID : MW]


def rope_table():
    position = np.arange(SEQ, dtype=np.float32)[:, None]
    channel = np.arange(HEAD // 2, dtype=np.float32)[None, :]
    rate = np.exp(channel * np.float32(-2.0 * math.log(ROPE_BASE) / HEAD)).astype(np.float32)
    angle = (position * rate).astype(np.float32).astype(np.float64)
    cos = np.cos(angle).astype(np.float32)
    sin = np.sin(angle).astype(np.float32)
    return np.concatenate([cos, sin], axis=1).reshape(4, ROWS, HEAD)


def body(
    tokens,
    attn_gain,
    w_query,
    key_weight,
    value_weight,
    query_gain,
    key_gain,
    w_out,
    mlp_gain,
    w_gate,
    w_up,
    w_down,
    out_cotangent,
):
    vmem = pl.BlockSpec(memory_space=pltpu.VMEM)

    def out(*shape):
        return jax.ShapeDtypeStruct(shape, F32)

    packed = pl.pallas_call(
        kernel,
        out_shape=(
            jax.ShapeDtypeStruct((ROWS, WIDTH), BF16),
            out(ROWS, WIDTH),
            out(64, AW),
            out(64, MW),
            out(8, WIDTH),
        ),
        in_specs=[vmem] * len(INPUTS),
        out_specs=(vmem,) * len(OUTPUTS),
        scratch_shapes=[pltpu.VMEM(*SCRATCH[name]) for name in NAMES]
        + [pltpu.SemaphoreType.DMA((N_SEM,)), pltpu.SemaphoreType.DMA((N_SEM,))],
        compiler_params=pltpu.CompilerParams(
            collective_id=0, has_side_effects=True, vmem_limit_bytes=64 * 2**20 - 2**17
        ),
        name="layer",
    )(
        tokens,
        out_cotangent,
        w_query,
        key_weight,
        value_weight,
        w_out.T,
        w_gate,
        w_up,
        w_down.T,
        attn_gain,
        mlp_gain,
        query_gain,
        key_gain,
        jnp.asarray(rope_table()),
    )
    parts = list(pl.pallas_call(
        unpack,
        out_shape=[
            jax.ShapeDtypeStruct((ROWS, WIDTH), BF16),
            out(ROWS, WIDTH),
            out(WIDTH),
            out(64, 256),
            out(64, HEAD),
            out(64, HEAD),
            out(HEAD),
            out(HEAD),
            out(64, 256),
            out(WIDTH),
            out(64, HID),
            out(64, HID),
            out(64, HID),
        ],
        in_specs=[vmem] * 5,
        out_specs=[vmem] * 13,
        name="unpack",
    )(*packed))
    parts[8] = parts[8].T
    parts[12] = parts[12].T
    return tuple(parts)


def solution(mesh):
    rows = P(("dp", "tensor"), None)
    first = P("dp", "tensor")
    second = P("tensor", "dp")
    whole = P()
    return jax.shard_map(
        body,
        mesh=mesh,
        in_specs=(
            rows,
            whole,
            first,
            first,
            first,
            whole,
            whole,
            second,
            whole,
            first,
            first,
            second,
            rows,
        ),
        out_specs=(
            rows,
            rows,
            whole,
            first,
            first,
            first,
            whole,
            whole,
            second,
            whole,
            first,
            first,
            second,
        ),
        check_vma=False,
    )
```

```python
import math

import jax
import jax.numpy as jnp
import numpy as np
from jax import lax
from jax.experimental import pallas as pl
from jax.experimental.pallas import tpu as pltpu
from jax.sharding import PartitionSpec as P

HEAD = 128
SEQ = 1024
WIDTH = 1024
ROWS = 256
QKV = 512
OW = 256
AW = QKV + OW
HID = 384
MW = 3 * HID
EPS = 1e-06
ROPE_BASE = 1000000.0
EXP_SCALE = math.log2(math.e) / math.sqrt(HEAD)
SCORE_SCALE = 1.0 / math.sqrt(HEAD)
MESH = pl.DeviceIdType.MESH
F32 = jnp.float32
BF16 = jnp.bfloat16


def dot_nn(a, b):
    return jnp.dot(a, b, preferred_element_type=F32)


def dot_nt(a, b):
    return lax.dot_general(a, b, (((1,), (1,)), ((), ())), preferred_element_type=F32)


def dot_tn(a, b):
    return lax.dot_general(a, b, (((0,), (0,)), ((), ())), preferred_element_type=F32)


def reorder(v):
    return jnp.concatenate([v[:, :512], v[:, 768:], v[:, 512:768]], axis=1)


def row_scale(v):
    return lax.rsqrt(jnp.mean(v * v, axis=-1, keepdims=True) + EPS)


def flip(bit):
    return 1 - bit


SCRATCH = {
    "w_q": ((2, 2, 2, 2, 2, 64, QKV), BF16),
    "w_o": ((2, 2, 2, 2, 2, 64, OW), BF16),
    "w_m": ((2, 2, 2, 2, 2, 64, MW), BF16),
    "pack_q": ((64, QKV), BF16),
    "pack_o": ((64, OW), BF16),
    "pack_m": ((64, MW), BF16),
    "a_full": ((4, ROWS, WIDTH), BF16),
    "m_full": ((2, 2, 2, 2, 2, 64, 512), BF16),
    "c_full": ((4, ROWS, WIDTH), BF16),
    "d_full": ((4, ROWS, WIDTH), BF16),
    "qkp": ((2, 4, ROWS, 384), F32),
    "qs": ((2, 4, 512, HEAD), BF16),
    "ks": ((2, 4, ROWS, HEAD), BF16),
    "kt": ((2, 4, HEAD, ROWS), BF16),
    "vs": ((2, 4, ROWS, HEAD), BF16),
    "vt": ((2, 4, HEAD, ROWS), BF16),
    "os": ((2, 4, 512, HEAD), BF16),
    "linv": ((2, 4, 8, 512), F32),
    "dos": ((2, 512, HEAD), BF16),
    "dk": ((2, 4, ROWS, HEAD), F32),
    "dv": ((2, 4, ROWS, HEAD), F32),
    "hid": ((2, 4, ROWS, HID), BF16),
    "dgu": ((2, 4, ROWS, 2 * HID), BF16),
    "own": ((ROWS, WIDTH), F32),
    "resid": ((ROWS, WIDTH), F32),
    "stage": ((3, ROWS, WIDTH), BF16),
    "w_dn": ((2, WIDTH, HID), BF16),
    "far": ((2, 128, WIDTH), BF16),
    "near": ((2, ROWS, WIDTH), BF16),
    "sum_m": ((3, ROWS, WIDTH), BF16),
    "sum_d": ((3, ROWS, WIDTH), BF16),
    "gains": ((8, WIDTH), F32),
    "gain_in": ((7, 8, WIDTH), F32),
    "core_q": ((2, 2, 2, 2, 1, 64, QKV), BF16),
    "core_o": ((2, 2, 2, 2, 1, 64, OW), BF16),
    "raw": ((2, 2, 64, MW), BF16),
    "mlp_x": ((2, 64, MW), BF16),
    "mlp_c": ((64, MW), F32),
    "attn_x": ((64, AW), BF16),
    "attn_low": ((64, AW), BF16),
    "attn_sum": ((64, AW), F32),
    "mlp_sum": ((2, 64, MW), F32),
}
AXES = {"xo": 3, "yo": 0, "za": 2, "zb": 1}
ORDER = ["xo", "yo", "za", "zb"]


def part_axes(part):
    return [ORDER[(part + step) % 4] for step in range(4)]


def cube_shape(part, step, cores, width):
    shape = [1, 1, 1, 1]
    for axis in part_axes(part)[:step]:
        shape[AXES[axis]] = 2
    return (*shape, cores, 16, width)


for _part in range(4):
    for _step in range(4):
        SCRATCH[f"sum_q_{_part}_{_step}"] = (cube_shape(_part, _step, 1, QKV), BF16)
        SCRATCH[f"sum_o_{_part}_{_step}"] = (cube_shape(_part, _step, 1, OW), BF16)
        SCRATCH[f"sum_w_{_part}_{_step}"] = (cube_shape(_part, _step, 2, MW), BF16)

NAMES = list(SCRATCH)
N_SEM = 109
INPUTS = ["tok", "cot", "wq", "wk", "wv", "wo", "wg", "wu", "wd", "ag", "mg", "qg", "kg", "rope"]
OUTPUTS = ["layer_out", "input_grad", "d_attn", "d_mlp", "d_gain"]


class Refs:
    pass


class Copy:
    def __init__(self, copy, gives, takes):
        self.copy, self.gives, self.takes = copy, gives, takes
        self.started = self.received = self.sent = False

    def run(self, cond, act):
        if cond is None:
            act()
        else:
            pl.when(cond)(act)

    def start(self):
        self.started = True
        self.run(self.gives, self.copy.start)

    def wait_recv(self):
        self.received = True
        self.run(self.takes, self.copy.wait_recv)

    def wait_send(self):
        self.sent = True
        self.run(self.gives, self.copy.wait_send)


def kernel(*refs):
    r = Refs()
    names = INPUTS + OUTPUTS + NAMES
    for name, ref in zip(names, refs):
        setattr(r, name, ref)
    ssem, rsem = refs[len(names)], refs[len(names) + 1]

    dp = lax.axis_index("dp")
    tn = lax.axis_index("tensor")
    z = dp // 4
    x_hi = (dp // 2) % 2
    core = dp % 2
    y = tn // 2
    x_lo = tn % 2
    y_lo = y % 2
    y_hi = y // 2
    gz = jnp.where(z < 2, z, 5 - z)
    own_bit = {"xo": x_hi, "yo": y_hi, "za": gz % 2, "zb": gz // 2}
    nbr = {
        "c": (dp + 1 - 2 * core, tn),
        "x": (dp, tn + 1 - 2 * x_lo),
        "y": (dp, tn + 2 - 4 * y_lo),
        "xo": (dp + 2 - 4 * x_hi, tn + 1 - 2 * x_lo),
        "yo": (dp, (3 - y) * 2 + x_lo),
        "za": (dp + 4 - 8 * (z % 2), tn),
        "zb": (dp + 4 * (3 - 2 * z), tn),
    }
    links = list(nbr)
    pair = "p"
    nbr["p"] = (dp, tn + jnp.where(core == 0, 2 - 4 * y_lo, 1 - 2 * x_lo))
    kx = (x_lo + x_hi) % 2
    lends = (core + x_lo) % 2
    role = 2 * lends + kx

    def square(k):
        kx, ky = k % 2, k // 2
        return (y_lo + ky - 2 * y_lo * ky) * 2 + x_lo + kx - 2 * x_lo * kx

    def group(k):
        kc = k % 2
        return (k // 2) * 2 + core + kc - 2 * core * kc

    ids = {}
    copies = r.copies = []
    unsent = []

    def later(src, dst, to, key, gives=None, takes=None):
        i = ids.setdefault(key, len(ids))
        copy = pltpu.make_async_remote_copy(
            src_ref=src,
            dst_ref=dst,
            send_sem=ssem.at[i],
            recv_sem=rsem.at[i],
            device_id=nbr[to],
            device_id_type=MESH,
        )
        copies.append(Copy(copy, gives, takes))
        unsent.append(copies[-1])
        return copies[-1]

    def send(*args, **kinds):
        copy = later(*args, **kinds)
        copy.start()
        return copy

    def flush():
        for copy in unsent:
            if copy.started and not copy.sent:
                copy.wait_send()
        unsent[:] = [copy for copy in unsent if not copy.sent]

    def wait_recv(group):
        for copy in group:
            copy.wait_recv()

    def at(k, value, act):
        pl.when(k == value)(act)

    def slots(full, current, cores):
        index = [None] * 4
        for axis in ORDER:
            if axis in full:
                index[AXES[axis]] = pl.ds(0, 2)
            else:
                bit = own_bit[axis]
                index[AXES[axis]] = pl.ds(flip(bit) if current == axis else bit, 1)
        return (*index, cores)

    both = pl.ds(0, 2)
    lane = pl.ds(core, 1)
    lanes = {"q": lane, "o": lane, "w": both}
    weights = {"q": r.w_q, "o": r.w_o, "w": r.w_m}
    grads = {"q": r.m_full, "o": r.w_o, "w": r.w_m}
    own_slot = (own_bit["yo"], own_bit["zb"], own_bit["za"], own_bit["xo"])
    own_view = tuple(pl.ds(bit, 1) for bit in own_slot)

    def step_key(kind, part, step, back):
        return (kind, part, step, back and kind == "w" and step == 3)

    def gather_later(kind, step):
        out = []
        for part in range(4):
            axes = part_axes(part)
            rows = pl.ds(16 * part, 16)
            view = weights[kind].at[(*slots(axes[:step], None, lanes[kind]), rows)]
            out.append(later(view, view, axes[step], step_key(kind, part, step, False)))
        return out

    def core_later(kind, late):
        out = []
        for part in range(4):
            axes = part_axes(part)
            rows = pl.ds(16 * part, 16)
            view = weights[kind].at[(*slots(axes[:3], axes[3] if late else None, lane), rows)]
            out.append(later(view, view, "c", ("core", kind, late, part)))
        return out

    def reduce_later(kind, step):
        out = []
        for part in range(4):
            axes = part_axes(part)
            rows = pl.ds(16 * part, 16)
            view = grads[kind].at[(*slots(axes[:step], axes[step], lanes[kind]), rows)]
            buf = getattr(r, f"sum_{kind}_{part}_{step}")
            out.append(later(view, buf, axes[step], step_key(kind, part, step, True)))
        return out

    def start(group):
        for copy in group:
            copy.start()

    def reduce_add(kind, step, group):
        for part in range(4):
            axes = part_axes(part)
            rows = pl.ds(16 * part, 16)
            index = (*slots(axes[:step], None, lanes[kind]), rows)
            group[part].wait_recv()
            total = grads[kind][index].astype(F32) + getattr(r, f"sum_{kind}_{part}_{step}")[...].astype(F32)
            grads[kind][index] = total.astype(BF16)

    barrier = pltpu.get_barrier_semaphore()
    for to in links:
        pl.semaphore_signal(barrier, inc=1, device_id=nbr[to], device_id_type=MESH)

    r.pack_q[:, 0:256] = r.wq[...]
    r.pack_q[:, 256:384] = r.wk[...]
    r.pack_q[:, 384:512] = r.wv[...]
    r.pack_o[...] = r.wo[...]
    r.pack_m[:, 0:HID] = r.wg[...]
    r.pack_m[:, HID : 2 * HID] = r.wu[...]
    r.pack_m[:, 2 * HID : MW] = r.wd[...]

    @pl.when(x_hi == 0)
    def _():
        r.w_q[(*own_view, lane)] = r.pack_q[...].reshape(1, 1, 1, 1, 1, 64, QKV)
        r.w_o[(*own_view, lane)] = r.pack_o[...].reshape(1, 1, 1, 1, 1, 64, OW)

    @pl.when(lends == 0)
    def _():
        r.raw[0, pl.ds(core, 1)] = r.pack_m[...].reshape(1, 64, MW)

    attn_gain = reorder(r.ag[...].astype(F32).reshape(1, WIDTH))
    mlp_gain = reorder(r.mg[...].astype(F32).reshape(1, WIDTH))
    query_gain = r.qg[...].astype(F32).reshape(1, HEAD)
    key_gain = r.kg[...].astype(F32).reshape(1, HEAD)

    def rows_in():
        return reorder(r.tok[...].astype(F32))

    rows_x = rows_in()
    r.a_full[square(0)] = (rows_x * row_scale(rows_x) * attn_gain).astype(BF16)
    r.c_full[group(0)] = reorder(r.cot[...])
    pl.semaphore_wait(barrier, len(links))

    odd = x_hi == 1
    swap_q = send(r.pack_q, r.w_q.at[(*own_slot, core)], "x", "swap_q", gives=odd, takes=odd)
    swap_o = send(r.pack_o, r.w_o.at[(*own_slot, core)], "x", "swap_o", gives=odd, takes=odd)
    mlp_pair = r.w_m.at[own_slot]
    raw_y = send(r.pack_m, r.raw.at[1, core], "y", "raw_y")
    raw_c0 = send(r.pack_m, r.raw.at[0, core], "c", "raw_c0", gives=lends == 1, takes=lends == 0)
    raw_c1 = later(r.raw.at[1, core], r.raw.at[1, core], "c", "raw_c1", gives=lends == 1, takes=lends == 0)
    mlp_to_x = later(r.raw.at[1 - kx], mlp_pair, "x", "mlp_x", gives=lends == 0, takes=lends == 1)

    def square_gather(buf):
        def half(k, n):
            return buf.at[square(k), pl.ds(128 * n, 128)]

        x0 = send(half(0, 0), half(0, 0), "x", "sg_x0")
        y1 = send(half(0, 1), half(0, 1), "y", "sg_y1")
        x1 = later(half(0, 1), half(0, 1), "x", "sg_x1")
        y0 = later(half(0, 0), half(0, 0), "y", "sg_y0")
        fy = later(half(1, 0), half(1, 0), "y", "sg_fy")
        fx = later(half(2, 1), half(2, 1), "x", "sg_fx")

        def second():
            x1.start()
            y0.start()

        def forward():
            x0.wait_recv()
            fy.start()
            y1.wait_recv()
            fx.start()

        return second, forward, x1, y0, [fx, fy]

    a_second, a_forward, a_x1, a_y0, a_far = square_gather(r.a_full)
    gather = {kind: [gather_later(kind, step) for step in range(4)] for kind in "qow"}
    to_core = {kind: [core_later(kind, late) for late in (False, True)] for kind in "qo"}

    def advance(kind, step):
        wait_recv(gather[kind][step - 1])
        start(gather[kind][step])

    swap_q.wait_recv()
    start(gather["q"][0])
    raw_y.wait_recv()
    raw_c1.start()
    swap_o.wait_recv()
    advance("q", 1)
    start(gather["o"][0])
    raw_c0.wait_recv()
    raw_c1.wait_recv()
    mlp_to_x.start()
    advance("q", 2)
    advance("o", 1)
    a_forward()

    @pl.when(lends == 0)
    def _():
        r.w_m[own_view] = r.raw[pl.ds(kx, 1)].reshape(1, 1, 1, 1, 2, 64, MW)

    advance("q", 3)
    start(to_core["q"][0])
    advance("o", 2)
    mlp_to_x.wait_recv()
    start(gather["w"][0])
    a_second()
    wait_recv(gather["q"][3])
    start(to_core["q"][1])
    advance("o", 3)
    start(to_core["o"][0])
    advance("w", 1)
    wait_recv(to_core["q"][0])
    wait_recv(to_core["q"][1])

    def w_qkv(g):
        return r.w_q[g].reshape(WIDTH, QKV)

    def w_out(g):
        return r.w_o[g].reshape(WIDTH, OW)

    def w_gu(g):
        return r.w_m[g, :, :, :, :, :, 0 : 2 * HID].reshape(WIDTH, 2 * HID)

    def w_dn(g):
        return r.w_dn[g]

    c_pair = later(r.c_full.at[group(0)], r.c_full.at[core + 2], pair, "cot_p")
    c_core = later(r.c_full.at[group(0)], r.c_full.at[group(0)], "c", "cot_c")

    first_half = lax.broadcasted_iota(jnp.int32, (ROWS, HEAD), 1) < HEAD // 2

    def turns(blk):
        table = r.rope[blk]
        swapped = pltpu.roll(table, 64, 1)
        return jnp.where(first_half, table, swapped), jnp.where(first_half, -swapped, table)

    def qkv_block(k, carry):
        @pl.when(k == 1)
        def _():
            a_x1.wait_recv()
            c_pair.start()
            c_core.start()

        @pl.when(k == 2)
        def _():
            a_y0.wait_recv()
            wait_recv(gather["o"][3])
            start(to_core["o"][1])
            advance("w", 2)

        @pl.when(k == 3)
        def _():
            wait_recv(a_far)

        blk = square(k)
        rows = r.a_full[blk]
        cos, sin = turns(blk)
        for g in range(2):
            acc = dot_nn(rows, w_qkv(g))
            r.qkp[g, blk] = acc[:, :384]
            for h in range(3):
                pre = acc[:, h * HEAD : (h + 1) * HEAD]
                normed = pre * row_scale(pre) * (key_gain if h == 2 else query_gain)
                turned = normed * cos + pltpu.roll(normed, 64, 1) * sin
                if h == 2:
                    r.ks[g, blk] = turned.astype(BF16)
                    r.kt[g, blk] = turned.T.astype(BF16)
                else:
                    r.qs[g, blk, h * ROWS : (h + 1) * ROWS] = turned.astype(BF16)
            value = acc[:, 384:]
            r.vs[g, blk] = value.astype(BF16)
            r.vt[g, blk] = value.T.astype(BF16)
        return carry

    lax.fori_loop(0, 4, qkv_block, 0)

    key_at = lax.broadcasted_iota(jnp.int32, (ROWS, 512), 0)
    query_at = lax.broadcasted_iota(jnp.int32, (ROWS, 512), 1) % ROWS
    visible = key_at <= query_at

    def weights_t(g, i, j, diagonal):
        scores = dot_nt(r.ks[g, j], r.qs[g, i])
        exps = jnp.exp2(scores * EXP_SCALE)
        if diagonal:
            exps = jnp.where(visible, exps, 0.0)
        return exps

    def attend_step(i, j, carry, diagonal):
        out = []
        for g in range(2):
            total, acc = carry[g]
            exps = weights_t(g, i, j, diagonal)
            total = total + jnp.sum(exps, axis=0, keepdims=True)
            acc = acc + dot_nn(r.vt[g, j], exps.astype(BF16))
            out.append((total, acc))
        return tuple(out)

    def attend_block(i):
        zero = (jnp.zeros((1, 512), F32), jnp.zeros((HEAD, 512), F32))
        state = lax.fori_loop(0, i, lambda j, s: attend_step(i, j, s, False), (zero, zero))
        state = attend_step(i, i, state, True)
        for g in range(2):
            total, acc = state[g]
            inv = 1.0 / total
            r.linv[g, i] = jnp.broadcast_to(inv, (8, 512))
            r.os[g, i] = (acc * inv).T.astype(BF16)

    def part_o(blk):
        acc = jnp.zeros((ROWS, WIDTH), F32)
        for g in range(2):
            heads = r.os[g, blk]
            acc = acc + dot_nt(jnp.concatenate([heads[:ROWS], heads[ROWS:]], axis=1), w_out(g))
        return acc

    def square_sum(part_of, steps):
        def out(n, rows, buf, to, key):
            return later(r.stage.at[n, pl.ds(*rows)], buf, to, key)

        low, high = (0, 128), (128, 128)
        d0 = out(2, low, r.far.at[0], "x", "ss_d0")
        d1 = out(2, high, r.far.at[1], "y", "ss_d1")
        x0 = out(0, low, r.near.at[0, pl.ds(*low)], "x", "ss_x0")
        x1 = out(0, high, r.near.at[0, pl.ds(*high)], "x", "ss_x1")
        y0 = out(1, low, r.near.at[1, pl.ds(*low)], "y", "ss_y0")
        y1 = out(1, high, r.near.at[1, pl.ds(*high)], "y", "ss_y1")

        def block(n, carry):
            k = jnp.where(n == 0, 3, n % 3)
            for value, act in steps.items():
                at(n, value, act)
            acc = part_of(square(k))

            @pl.when(n < 3)
            def _():
                r.stage[(n + 2) % 3] = acc.astype(BF16)

            @pl.when(n == 3)
            def _():
                r.own[...] = acc

            @pl.when(n == 0)
            def _():
                d0.start()
                d1.start()

            at(n, 2, x0.start)
            at(n, 3, y1.start)
            return carry

        lax.fori_loop(0, 4, block, 0)

        def relay():
            d1.wait_recv()
            r.stage[0, 128:256] = (r.stage[0, 128:256].astype(F32) + r.far[1].astype(F32)).astype(BF16)
            x1.start()
            d0.wait_recv()
            r.stage[1, 0:128] = (r.stage[1, 0:128].astype(F32) + r.far[0].astype(F32)).astype(BF16)
            y0.start()

        def finish():
            wait_recv([x0, y1, x1, y0])
            return r.own[...] + r.near[0].astype(F32) + r.near[1].astype(F32)

        return relay, finish

    def attend_and_part(blk):
        attend_block(blk)

        @pl.when(blk == square(3))
        def _():
            wait_recv(to_core["o"][0])
            wait_recv(to_core["o"][1])

        return part_o(blk)

    o_relay, o_finish = square_sum(attend_and_part, {3: lambda: advance("w", 3)})
    o_relay()
    r.dk[...] = jnp.zeros((2, 4, ROWS, HEAD), F32)
    r.dv[...] = jnp.zeros((2, 4, ROWS, HEAD), F32)
    c_pair.wait_recv()
    c_forward = send(r.c_full.at[core + 2], r.c_full.at[core + 2], "c", "cot_f")
    resid = rows_in() + o_finish()
    r.resid[...] = resid
    normed = (resid * row_scale(resid) * mlp_gain).astype(BF16)
    for half in range(2):
        r.m_full[0, pl.ds(core, 1), half] = normed[:, 512 * half : 512 * half + 512].reshape(1, 2, 2, 64, 512)
    m_pair = []
    m_forward = []
    for n in range(2):
        near_rows, far_rows = (r.m_full.at[place, core, :, n] for place in range(2))
        m_pair.append(send(near_rows, far_rows, pair, ("m_p", n)))
        m_forward.append(later(far_rows, far_rows, "c", ("m_f", n)))
    m_core = send(r.m_full.at[0, core], r.m_full.at[0, core], "c", "m_c")
    wait_recv(gather["w"][3])
    r.w_dn[...] = r.w_m[:, :, :, :, :, :, 2 * HID : MW].reshape(2, WIDTH, HID)
    wait_recv([c_core, c_forward])

    def mlp_block(k, carry):
        at(k, 1, m_core.wait_recv)

        @pl.when(k == 2)
        def _():
            for n in range(2):
                m_pair[n].wait_recv()
                m_forward[n].start()

        @pl.when(k == 3)
        def _():
            wait_recv(m_forward)

        i = group(k)
        rows = jnp.concatenate([r.m_full[i // 2, i % 2, half].reshape(ROWS, 512) for half in range(2)], axis=1)
        cots = r.c_full[i]
        for g in range(2):
            pre = dot_nn(rows, w_gu(g))
            grad = dot_nn(cots, w_dn(g))
            gate = pre[:, :HID]
            up = pre[:, HID:]
            sig = 1.0 / (1.0 + jnp.exp(-gate))
            act = gate * sig
            r.hid[g, i] = (act * up).astype(BF16)
            r.dgu[g, i, :, 0:HID] = (grad * up * sig * (1.0 + gate * (1.0 - sig))).astype(BF16)
            r.dgu[g, i, :, HID : 2 * HID] = (grad * act).astype(BF16)
        return carry

    def pair_sum(part_of, recv, own, name, hold):
        stage = r.stage
        s3 = later(stage.at[2], recv.at[0], "c", (name, 3))
        s1 = later(stage.at[0], recv.at[1], "c", (name, 1))
        s2 = later(stage.at[1], recv.at[2], pair, (name, 2))

        def block(n, carry):
            acc = part_of(group(n + (n // 2) * (5 - 2 * n)))

            @pl.when(n == 0)
            def _():
                own[...] = own[...] + acc if hold else acc

            @pl.when(n == 1)
            def _():
                stage[0] = acc.astype(BF16)
                s1.start()

            @pl.when(n == 2)
            def _():
                stage[2] = acc.astype(BF16)
                s3.start()

            @pl.when(n == 3)
            def _():
                s3.wait_recv()
                stage[1] = (acc + recv[0].astype(F32)).astype(BF16)
                if not hold:
                    s2.start()

            return carry

        def finish():
            wait_recv([s1, s2])
            return own[...] + recv[1].astype(F32) + recv[2].astype(F32)

        return block, finish, s2

    def part_dm(i):
        return dot_nt(r.dgu[0, i], w_gu(0)) + dot_nt(r.dgu[1, i], w_gu(1))

    def part_down(i):
        return dot_nt(r.hid[0, i], w_dn(0)) + dot_nt(r.hid[1, i], w_dn(1))

    dm_block, dm_finish, _ = pair_sum(part_dm, r.sum_m, r.own, "dm", False)
    flush()
    lax.fori_loop(0, 2, mlp_block, 0)
    lax.fori_loop(0, 2, dm_block, 0)
    lax.fori_loop(2, 4, mlp_block, 0)
    lax.fori_loop(2, 4, dm_block, 0)

    def mlp_grads(p, carry):
        cols = pl.ds(pl.multiple_of(256 * p, 256), 256)
        half_cols = pl.ds(pl.multiple_of(256 * (p % 2), 256), 256)
        rows_t = r.m_full[:, :, p // 2, :, :, :, half_cols].reshape(SEQ, 256)
        cots_t = r.c_full[:, :, cols].reshape(SEQ, 256)
        for g in range(2):
            grad_gu = dot_tn(rows_t, r.dgu[g].reshape(SEQ, 2 * HID))
            grad_dn = dot_tn(cots_t, r.hid[g].reshape(SEQ, HID))
            r.w_m[g, p // 2, p % 2, :, :, :, 0 : 2 * HID] = grad_gu.reshape(2, 2, 64, 2 * HID).astype(BF16)
            r.w_m[g, p // 2, p % 2, :, :, :, 2 * HID : MW] = grad_dn.reshape(2, 2, 64, HID).astype(BF16)
        return carry

    lax.fori_loop(0, 4, mlp_grads, 0)
    back_w = {step: reduce_later("w", step) for step in range(4)}
    flush()
    start(back_w[3])

    dm = dm_finish()
    resid = r.resid[...]
    inv_m = row_scale(resid)
    scaled = dm * mlp_gain
    inner = jnp.mean(scaled * resid, axis=-1, keepdims=True)
    r.gains[...] = jnp.zeros((8, WIDTH), F32)
    r.gains[1:2] = jnp.sum(dm * resid * inv_m, axis=0, keepdims=True)
    dresid = reorder(r.cot[...].astype(F32)) + inv_m * scaled - resid * (inv_m * inv_m * inv_m * inner)
    r.input_grad[...] = resid
    r.resid[...] = dresid
    r.d_full[square(0)] = dresid.astype(BF16)
    d_second, d_forward, d_x1, d_y0, d_far = square_gather(r.d_full)
    def down_order(n):
        return jnp.where(n == 0, 2, jnp.where(n == 3, 3, n - 1))

    down_block, down_finish, down_pair = pair_sum(part_down, r.sum_d, r.input_grad, "down", True)
    lax.fori_loop(0, 4, lambda n, carry: down_block(down_order(n), carry), 0)
    d_second()

    def back_step(i, j, carry, diagonal, delta):
        out = []
        for g in range(2):
            probs = weights_t(g, i, j, diagonal) * r.linv[g, i, 0:1]
            grads = dot_nt(r.vs[g, j], r.dos[g])
            dz = (probs * (grads - delta[g])).astype(BF16)
            r.dv[g, j] += dot_nn(probs.astype(BF16), r.dos[g])
            r.dk[g, j] += dot_nn(dz, r.qs[g, i])
            out.append(carry[g] + dot_nn(r.kt[g, j], dz))
        return tuple(out)

    def unnorm(pre, gain, grad):
        inv = row_scale(pre)
        hat = pre * inv
        scaled = grad * gain
        back = inv * (scaled - hat * jnp.mean(scaled * hat, axis=-1, keepdims=True))
        return back.astype(BF16), jnp.sum(grad * hat, axis=0, keepdims=True)

    def turn_back(grad, blk):
        cos, sin = turns(blk)
        return grad * cos - pltpu.roll(grad, 64, 1) * sin

    def back_block(k, gain_sum):
        @pl.when(k == 1)
        def _():
            d_forward()
            d_x1.wait_recv()

        @pl.when(k == 2)
        def _():
            d_y0.wait_recv()
            reduce_add("w", 3, back_w[3])
            start(back_w[2])

        @pl.when(k == 3)
        def _():
            wait_recv(d_far)
            down_pair.start()

        i = square(k)
        rows = r.d_full[i]
        delta = []
        for g in range(2):
            grad = dot_nn(rows, w_out(g))
            inner = []
            for h in range(2):
                part = grad[:, h * HEAD : (h + 1) * HEAD].astype(BF16)
                r.dos[g, h * ROWS : (h + 1) * ROWS] = part
                prod = part.astype(F32) * r.os[g, i, h * ROWS : (h + 1) * ROWS].astype(F32)
                inner.append(jnp.sum(prod.T, axis=0, keepdims=True))
            delta.append(jnp.concatenate(inner, axis=1))
        zero = jnp.zeros((HEAD, 512), F32)
        state = lax.fori_loop(0, i, lambda j, s: back_step(i, j, s, False, delta), (zero, zero))
        state = back_step(i, i, state, True, delta)
        for g in range(2):
            for h in range(2):
                grad = turn_back(state[g][:, h * ROWS : (h + 1) * ROWS].T * SCORE_SCALE, i)
                low, part = unnorm(r.qkp[g, i, :, h * HEAD : (h + 1) * HEAD], query_gain, grad)
                r.dgu[g, i, :, h * HEAD : (h + 1) * HEAD] = low
                gain_sum = gain_sum + part
        return gain_sum

    q_gain_part = lax.fori_loop(0, 4, back_block, jnp.zeros((1, HEAD), F32))

    other = pl.ds(flip(core), 1)
    whole = (both, both, both, both)

    def core_sum(kind, buf, copy):
        copy.wait_recv()
        index = (*whole, lane)
        total = grads[kind][index].astype(F32) + buf[...].astype(F32)
        grads[kind][index] = total.astype(BF16)

    def out_grads(p, carry):
        cols = pl.ds(pl.multiple_of(256 * p, 256), 256)
        grads_t = r.d_full[:, :, cols].reshape(SEQ, 256)
        for g in range(2):
            heads = r.os[g]
            mixed = jnp.concatenate(
                [heads[:, :ROWS].reshape(SEQ, HEAD), heads[:, ROWS:].reshape(SEQ, HEAD)], axis=1
            )
            r.w_o[g, p // 2, p % 2] = dot_tn(grads_t, mixed).reshape(2, 2, 64, OW).astype(BF16)
        return carry

    reduce_add("w", 2, back_w[2])
    start(back_w[1])

    def key_block(j, gain_sum):
        for g in range(2):
            grad = turn_back(r.dk[g, j] * SCORE_SCALE, j)
            low, part = unnorm(r.qkp[g, j, :, 256:384], key_gain, grad)
            r.dgu[g, j, :, 256:384] = low
            r.dgu[g, j, :, 384:512] = r.dv[g, j].astype(BF16)
            gain_sum = gain_sum + part
        return gain_sum

    k_gain_part = lax.fori_loop(0, 4, key_block, jnp.zeros((1, HEAD), F32))
    r.gains[2:3, 0:HEAD] = q_gain_part
    r.gains[2:3, HEAD : 2 * HEAD] = k_gain_part

    def qkv_grads(p, carry):
        cols = pl.ds(pl.multiple_of(256 * p, 256), 256)
        rows_t = r.a_full[:, :, cols].reshape(SEQ, 256)
        for g in range(2):
            grad = dot_tn(rows_t, r.dgu[g, :, :, 0:QKV].reshape(SEQ, QKV))
            r.m_full[g, p // 2, p % 2] = grad.reshape(2, 2, 64, QKV).astype(BF16)
        return carry

    sum_pair = r.w_m.at[own_slot]
    back_x = later(sum_pair, r.mlp_x, "x", "mlp_x", gives=lends == 1, takes=lends == 0)
    back_y0 = later(r.mlp_x, r.raw.at[0], "y", "raw_y", gives=role == 0, takes=role == 0)
    back_y1 = later(sum_pair, r.raw.at[0], "y", "raw_y", gives=role == 1, takes=role == 1)
    mlp_back_c = later(r.mlp_sum.at[flip(core)], r.mlp_c, "c", "raw_c0", gives=lends == 0, takes=lends == 1)

    lax.fori_loop(0, 4, qkv_grads, 0)
    flush()
    q_core = send(r.m_full.at[(*whole, other)], r.core_q, "c", "q_core")
    lax.fori_loop(0, 4, out_grads, 0)
    o_core = send(r.w_o.at[(*whole, other)], r.core_o, "c", "o_core")

    def part_da(blk):
        acc = dot_nt(r.dgu[0, blk, :, 0:QKV], w_qkv(0)) + dot_nt(r.dgu[1, blk, :, 0:QKV], w_qkv(1))
        r.gains[0:1] += jnp.sum(acc * r.a_full[blk].astype(F32), axis=0, keepdims=True)
        return acc

    back_o = {step: reduce_later("o", step) for step in range(4)}
    back_q = {step: reduce_later("q", step) for step in range(4)}

    def tail_q():
        core_sum("q", r.core_q, q_core)
        start(back_q[3])

    def tail_o():
        core_sum("o", r.core_o, o_core)
        start(back_o[3])

    a_relay, a_finish = square_sum(part_da, {1: tail_q, 3: tail_o})

    gain_links = ["c", "za", "zb", "yo", "xo", "y", "x"]

    def gain_send(n):
        return send(r.gains, r.gain_in.at[n], gain_links[n], ("gain", n))

    def gain_add(n, copy):
        copy.wait_send()
        copy.wait_recv()
        r.gains[...] += r.gain_in[n]

    def reduce_next(kind, step, back):
        reduce_add(kind, step, back[step])
        start(back[step - 1])

    g_step = gain_send(0)
    reduce_next("w", 1, back_w)
    gain_add(0, g_step)
    g_step = gain_send(1)
    a_relay()
    reduce_next("q", 3, back_q)
    reduce_next("o", 3, back_o)
    gain_add(1, g_step)
    g_step = gain_send(2)
    reduce_add("w", 0, back_w[0])
    back_x.start()
    back_y1.start()
    r.layer_out[...] = reorder(down_finish()).astype(BF16)
    gain_add(2, g_step)
    g_step = gain_send(3)
    reduce_next("q", 2, back_q)
    reduce_next("o", 2, back_o)
    gain_add(3, g_step)
    g_step = gain_send(4)
    reduce_next("q", 1, back_q)
    reduce_next("o", 1, back_o)

    def last_step(kind, group, cols):
        for part in range(4):
            rows = pl.ds(16 * part, 16)
            group[part].wait_recv()
            total = grads[kind][(*own_view, lane, rows)].astype(F32) + getattr(r, f"sum_{kind}_{part}_0")[...].astype(F32)
            r.attn_sum[16 * part : 16 * part + 16, cols] = total.reshape(16, -1)
        r.attn_low[:, cols] = r.attn_sum[:, cols].astype(BF16)

    back_x.wait_recv()
    back_y0.start()
    gain_add(4, g_step)
    g_step = gain_send(5)
    last_step("q", back_q[0], slice(0, QKV))
    last_step("o", back_o[0], slice(QKV, AW))
    attn_back = send(r.attn_low, r.attn_x, "x", "swap_q", gives=odd, takes=odd)
    rows_x = rows_in()
    inv_a = row_scale(rows_x)
    scaled = a_finish() * attn_gain
    inner = jnp.mean(scaled * rows_x, axis=-1, keepdims=True)
    r.input_grad[...] = reorder(r.resid[...] + inv_a * scaled - rows_x * (inv_a * inv_a * inv_a * inner))
    gain_add(5, g_step)
    g_step = gain_send(6)
    back_y0.wait_recv()
    back_y1.wait_recv()

    @pl.when(role == 0)
    def _():
        r.mlp_sum[...] = sum_pair[...].astype(F32) + r.raw[0].astype(F32)

    @pl.when(role == 1)
    def _():
        r.mlp_sum[...] = r.mlp_x[...].astype(F32) + r.raw[0].astype(F32)

    mlp_back_c.start()

    @pl.when(lends == 0)
    def _():
        r.d_mlp[...] = r.mlp_sum[core]

    @pl.when(x_hi == 0)
    def _():
        r.d_attn[...] = r.attn_sum[...]

    attn_back.wait_recv()

    @pl.when(odd)
    def _():
        r.d_attn[...] = r.attn_x[...].astype(F32)

    mlp_back_c.wait_recv()

    @pl.when(lends == 1)
    def _():
        r.d_mlp[...] = r.mlp_c[...]

    gain_add(6, g_step)
    sums = r.gains[...]
    r.d_gain[...] = reorder(sums)
    r.d_gain[0:1] = reorder(sums[0:1] / attn_gain)
    r.d_gain[2:3] = sums[2:3]
    flush()


def unpack(*refs):
    layer_in, input_in, d_attn, d_mlp, d_gain = refs[:5]
    (
        layer_out,
        input_grad,
        attn_gain,
        w_query,
        w_key,
        w_value,
        query_gain,
        key_gain,
        w_out,
        mlp_gain,
        w_gate,
        w_up,
        w_down,
    ) = refs[5:18]
    layer_out[...] = layer_in[...]
    input_grad[...] = input_in[...]
    attn_gain[...] = d_gain[0]
    mlp_gain[...] = d_gain[1]
    query_gain[...] = d_gain[2, 0:HEAD]
    key_gain[...] = d_gain[2, HEAD : 2 * HEAD]
    w_query[...] = d_attn[:, 0:256]
    w_key[...] = d_attn[:, 256:384]
    w_value[...] = d_attn[:, 384:512]
    w_out[...] = d_attn[:, 512:768]
    w_gate[...] = d_mlp[:, 0:HID]
    w_up[...] = d_mlp[:, HID : 2 * HID]
    w_down[...] = d_mlp[:, 2 * HID : MW]


def rope_table():
    position = np.arange(SEQ, dtype=np.float32)[:, None]
    channel = np.arange(HEAD // 2, dtype=np.float32)[None, :]
    rate = np.exp(channel * np.float32(-2.0 * math.log(ROPE_BASE) / HEAD)).astype(np.float32)
    angle = (position * rate).astype(np.float32).astype(np.float64)
    cos = np.cos(angle).astype(np.float32)
    sin = np.sin(angle).astype(np.float32)
    return np.concatenate([cos, sin], axis=1).reshape(4, ROWS, HEAD)


def body(
    tokens,
    attn_gain,
    w_query,
    key_weight,
    value_weight,
    query_gain,
    key_gain,
    w_out,
    mlp_gain,
    w_gate,
    w_up,
    w_down,
    out_cotangent,
):
    vmem = pl.BlockSpec(memory_space=pltpu.VMEM)

    def out(*shape):
        return jax.ShapeDtypeStruct(shape, F32)

    packed = pl.pallas_call(
        kernel,
        out_shape=(
            jax.ShapeDtypeStruct((ROWS, WIDTH), BF16),
            out(ROWS, WIDTH),
            out(64, AW),
            out(64, MW),
            out(8, WIDTH),
        ),
        in_specs=[vmem] * len(INPUTS),
        out_specs=(vmem,) * len(OUTPUTS),
        scratch_shapes=[pltpu.VMEM(*SCRATCH[name]) for name in NAMES]
        + [pltpu.SemaphoreType.DMA((N_SEM,)), pltpu.SemaphoreType.DMA((N_SEM,))],
        compiler_params=pltpu.CompilerParams(
            collective_id=0, has_side_effects=True, vmem_limit_bytes=64 * 2**20 - 2**17
        ),
        name="layer",
    )(
        tokens,
        out_cotangent,
        w_query,
        key_weight,
        value_weight,
        w_out.T,
        w_gate,
        w_up,
        w_down.T,
        attn_gain,
        mlp_gain,
        query_gain,
        key_gain,
        jnp.asarray(rope_table()),
    )
    parts = list(pl.pallas_call(
        unpack,
        out_shape=[
            jax.ShapeDtypeStruct((ROWS, WIDTH), BF16),
            out(ROWS, WIDTH),
            out(WIDTH),
            out(64, 256),
            out(64, HEAD),
            out(64, HEAD),
            out(HEAD),
            out(HEAD),
            out(64, 256),
            out(WIDTH),
            out(64, HID),
            out(64, HID),
            out(64, HID),
        ],
        in_specs=[vmem] * 5,
        out_specs=[vmem] * 13,
        name="unpack",
    )(*packed))
    parts[8] = parts[8].T
    parts[12] = parts[12].T
    return tuple(parts)


def solution(mesh):
    rows = P(("dp", "tensor"), None)
    first = P("dp", "tensor")
    second = P("tensor", "dp")
    whole = P()
    return jax.shard_map(
        body,
        mesh=mesh,
        in_specs=(
            rows,
            whole,
            first,
            first,
            first,
            whole,
            whole,
            second,
            whole,
            first,
            first,
            second,
            rows,
        ),
        out_specs=(
            rows,
            rows,
            whole,
            first,
            first,
            first,
            whole,
            whole,
            second,
            whole,
            first,
            first,
            second,
        ),
        check_vma=False,
    )
```

```python
import math

import jax
import jax.numpy as jnp
import numpy as np
from jax import lax
from jax.experimental import pallas as pl
from jax.experimental.pallas import tpu as pltpu
from jax.sharding import PartitionSpec as P

HEAD = 128
SEQ = 1024
WIDTH = 1024
ROWS = 256
QKV = 512
OW = 256
AW = QKV + OW
HID = 384
MW = 3 * HID
EPS = 1e-06
ROPE_BASE = 1000000.0
EXP_SCALE = math.log2(math.e) / math.sqrt(HEAD)
SCORE_SCALE = 1.0 / math.sqrt(HEAD)
MESH = pl.DeviceIdType.MESH
F32 = jnp.float32
BF16 = jnp.bfloat16


def dot_nn(a, b):
    return jnp.dot(a, b, preferred_element_type=F32)


def dot_nt(a, b):
    return lax.dot_general(a, b, (((1,), (1,)), ((), ())), preferred_element_type=F32)


def dot_tn(a, b):
    return lax.dot_general(a, b, (((0,), (0,)), ((), ())), preferred_element_type=F32)


def reorder(v):
    return jnp.concatenate([v[:, :512], v[:, 768:], v[:, 512:768]], axis=1)


def row_scale(v):
    return lax.rsqrt(jnp.mean(v * v, axis=-1, keepdims=True) + EPS)


def flip(bit):
    return 1 - bit


SCRATCH = {
    "w_q": ((2, 2, 2, 2, 2, 64, QKV), BF16),
    "w_o": ((2, 2, 2, 2, 2, 64, OW), BF16),
    "w_m": ((2, 2, 2, 2, 2, 64, MW), BF16),
    "pack_q": ((64, QKV), BF16),
    "pack_o": ((64, OW), BF16),
    "pack_m": ((64, MW), BF16),
    "a_full": ((4, ROWS, WIDTH), BF16),
    "m_full": ((2, 2, 2, 2, 2, 64, 512), BF16),
    "c_full": ((4, ROWS, WIDTH), BF16),
    "d_full": ((4, ROWS, WIDTH), BF16),
    "qkp": ((2, 4, ROWS, 384), F32),
    "qs": ((2, 4, 512, HEAD), BF16),
    "ks": ((2, 4, ROWS, HEAD), BF16),
    "kt": ((2, 4, HEAD, ROWS), BF16),
    "vs": ((2, 4, ROWS, HEAD), BF16),
    "vt": ((2, 4, HEAD, ROWS), BF16),
    "os": ((2, 4, 512, HEAD), BF16),
    "linv": ((2, 4, 8, 512), F32),
    "dos": ((2, 512, HEAD), BF16),
    "dk": ((2, 4, ROWS, HEAD), F32),
    "dv": ((2, 4, ROWS, HEAD), F32),
    "hid": ((2, 4, ROWS, HID), BF16),
    "dgu": ((2, 4, ROWS, 2 * HID), BF16),
    "own": ((ROWS, WIDTH), F32),
    "resid": ((ROWS, WIDTH), F32),
    "stage": ((3, ROWS, WIDTH), BF16),
    "w_dn": ((2, WIDTH, HID), BF16),
    "far": ((2, 128, WIDTH), BF16),
    "near": ((2, ROWS, WIDTH), BF16),
    "sum_m": ((3, ROWS, WIDTH), BF16),
    "sum_d": ((3, ROWS, WIDTH), BF16),
    "gains": ((8, WIDTH), F32),
    "gain_in": ((7, 8, WIDTH), F32),
    "core_q": ((2, 2, 2, 2, 1, 64, QKV), BF16),
    "core_o": ((2, 2, 2, 2, 1, 64, OW), BF16),
    "raw": ((2, 2, 64, MW), BF16),
    "mlp_x": ((2, 64, MW), BF16),
    "mlp_c": ((64, MW), F32),
    "attn_x": ((64, AW), BF16),
    "attn_low": ((64, AW), BF16),
    "attn_sum": ((64, AW), F32),
    "mlp_sum": ((2, 64, MW), F32),
}
AXES = {"xo": 3, "yo": 0, "za": 2, "zb": 1}
ORDER = ["xo", "yo", "za", "zb"]


def part_axes(part):
    return [ORDER[(part + step) % 4] for step in range(4)]


def cube_shape(part, step, cores, width):
    shape = [1, 1, 1, 1]
    for axis in part_axes(part)[:step]:
        shape[AXES[axis]] = 2
    return (*shape, cores, 16, width)


for _part in range(4):
    for _step in range(4):
        SCRATCH[f"sum_q_{_part}_{_step}"] = (cube_shape(_part, _step, 1, QKV), BF16)
        SCRATCH[f"sum_o_{_part}_{_step}"] = (cube_shape(_part, _step, 1, OW), BF16)
        SCRATCH[f"sum_w_{_part}_{_step}"] = (cube_shape(_part, _step, 2, MW), BF16)

NAMES = list(SCRATCH)
N_SEM = 109
INPUTS = ["tok", "cot", "wq", "wk", "wv", "wo", "wg", "wu", "wd", "ag", "mg", "qg", "kg", "rope"]
OUTPUTS = ["layer_out", "input_grad", "d_attn", "d_mlp", "d_gain"]


class Refs:
    pass


class Copy:
    def __init__(self, copy, gives, takes):
        self.copy, self.gives, self.takes = copy, gives, takes
        self.started = self.received = self.sent = False

    def run(self, cond, act):
        if cond is None:
            act()
        else:
            pl.when(cond)(act)

    def start(self):
        self.started = True
        self.run(self.gives, self.copy.start)

    def wait_recv(self):
        self.received = True
        self.run(self.takes, self.copy.wait_recv)

    def wait_send(self):
        self.sent = True
        self.run(self.gives, self.copy.wait_send)


def kernel(*refs):
    r = Refs()
    names = INPUTS + OUTPUTS + NAMES
    for name, ref in zip(names, refs):
        setattr(r, name, ref)
    ssem, rsem = refs[len(names)], refs[len(names) + 1]

    dp = lax.axis_index("dp")
    tn = lax.axis_index("tensor")
    z = dp // 4
    x_hi = (dp // 2) % 2
    core = dp % 2
    y = tn // 2
    x_lo = tn % 2
    y_lo = y % 2
    y_hi = y // 2
    gz = jnp.where(z < 2, z, 5 - z)
    own_bit = {"xo": x_hi, "yo": y_hi, "za": gz % 2, "zb": gz // 2}
    nbr = {
        "c": (dp + 1 - 2 * core, tn),
        "x": (dp, tn + 1 - 2 * x_lo),
        "y": (dp, tn + 2 - 4 * y_lo),
        "xo": (dp + 2 - 4 * x_hi, tn + 1 - 2 * x_lo),
        "yo": (dp, (3 - y) * 2 + x_lo),
        "za": (dp + 4 - 8 * (z % 2), tn),
        "zb": (dp + 4 * (3 - 2 * z), tn),
    }
    links = list(nbr)
    pair = "p"
    nbr["p"] = (dp, tn + jnp.where(core == 0, 2 - 4 * y_lo, 1 - 2 * x_lo))
    kx = (x_lo + x_hi) % 2
    lends = (core + x_lo) % 2
    role = 2 * lends + kx

    def square(k):
        kx, ky = k % 2, k // 2
        return (y_lo + ky - 2 * y_lo * ky) * 2 + x_lo + kx - 2 * x_lo * kx

    def group(k):
        kc = k % 2
        return (k // 2) * 2 + core + kc - 2 * core * kc

    ids = {}
    copies = r.copies = []
    unsent = []

    def later(src, dst, to, key, gives=None, takes=None):
        i = ids.setdefault(key, len(ids))
        copy = pltpu.make_async_remote_copy(
            src_ref=src,
            dst_ref=dst,
            send_sem=ssem.at[i],
            recv_sem=rsem.at[i],
            device_id=nbr[to],
            device_id_type=MESH,
        )
        copies.append(Copy(copy, gives, takes))
        unsent.append(copies[-1])
        return copies[-1]

    def send(*args, **kinds):
        copy = later(*args, **kinds)
        copy.start()
        return copy

    def flush():
        for copy in unsent:
            if copy.started and not copy.sent:
                copy.wait_send()
        unsent[:] = [copy for copy in unsent if not copy.sent]

    def wait_recv(group):
        for copy in group:
            copy.wait_recv()

    def at(k, value, act):
        pl.when(k == value)(act)

    def slots(full, current, cores):
        index = [None] * 4
        for axis in ORDER:
            if axis in full:
                index[AXES[axis]] = pl.ds(0, 2)
            else:
                bit = own_bit[axis]
                index[AXES[axis]] = pl.ds(flip(bit) if current == axis else bit, 1)
        return (*index, cores)

    both = pl.ds(0, 2)
    lane = pl.ds(core, 1)
    lanes = {"q": lane, "o": lane, "w": both}
    weights = {"q": r.w_q, "o": r.w_o, "w": r.w_m}
    grads = {"q": r.m_full, "o": r.w_o, "w": r.w_m}
    own_slot = (own_bit["yo"], own_bit["zb"], own_bit["za"], own_bit["xo"])
    own_view = tuple(pl.ds(bit, 1) for bit in own_slot)

    def step_key(kind, part, step, back):
        return (kind, part, step, back and kind == "w" and step == 3)

    def gather_later(kind, step):
        out = []
        for part in range(4):
            axes = part_axes(part)
            rows = pl.ds(16 * part, 16)
            view = weights[kind].at[(*slots(axes[:step], None, lanes[kind]), rows)]
            out.append(later(view, view, axes[step], step_key(kind, part, step, False)))
        return out

    def core_later(kind, late):
        out = []
        for part in range(4):
            axes = part_axes(part)
            rows = pl.ds(16 * part, 16)
            view = weights[kind].at[(*slots(axes[:3], axes[3] if late else None, lane), rows)]
            out.append(later(view, view, "c", ("core", kind, late, part)))
        return out

    def reduce_later(kind, step):
        out = []
        for part in range(4):
            axes = part_axes(part)
            rows = pl.ds(16 * part, 16)
            view = grads[kind].at[(*slots(axes[:step], axes[step], lanes[kind]), rows)]
            buf = getattr(r, f"sum_{kind}_{part}_{step}")
            out.append(later(view, buf, axes[step], step_key(kind, part, step, True)))
        return out

    def start(group):
        for copy in group:
            copy.start()

    def reduce_add(kind, step, group):
        for part in range(4):
            axes = part_axes(part)
            rows = pl.ds(16 * part, 16)
            index = (*slots(axes[:step], None, lanes[kind]), rows)
            group[part].wait_recv()
            total = grads[kind][index].astype(F32) + getattr(r, f"sum_{kind}_{part}_{step}")[...].astype(F32)
            grads[kind][index] = total.astype(BF16)

    barrier = pltpu.get_barrier_semaphore()
    for to in links:
        pl.semaphore_signal(barrier, inc=1, device_id=nbr[to], device_id_type=MESH)

    r.pack_q[:, 0:256] = r.wq[...]
    r.pack_q[:, 256:384] = r.wk[...]
    r.pack_q[:, 384:512] = r.wv[...]
    r.pack_o[...] = r.wo[...]
    r.pack_m[:, 0:HID] = r.wg[...]
    r.pack_m[:, HID : 2 * HID] = r.wu[...]
    r.pack_m[:, 2 * HID : MW] = r.wd[...]

    @pl.when(x_hi == 0)
    def _():
        r.w_q[(*own_view, lane)] = r.pack_q[...].reshape(1, 1, 1, 1, 1, 64, QKV)
        r.w_o[(*own_view, lane)] = r.pack_o[...].reshape(1, 1, 1, 1, 1, 64, OW)

    @pl.when(lends == 0)
    def _():
        r.raw[0, pl.ds(core, 1)] = r.pack_m[...].reshape(1, 64, MW)

    attn_gain = reorder(r.ag[...].astype(F32).reshape(1, WIDTH))
    mlp_gain = reorder(r.mg[...].astype(F32).reshape(1, WIDTH))
    query_gain = r.qg[...].astype(F32).reshape(1, HEAD)
    key_gain = r.kg[...].astype(F32).reshape(1, HEAD)

    def rows_in():
        return reorder(r.tok[...].astype(F32))

    rows_x = rows_in()
    r.a_full[square(0)] = (rows_x * row_scale(rows_x) * attn_gain).astype(BF16)
    r.c_full[group(0)] = reorder(r.cot[...])
    pl.semaphore_wait(barrier, len(links))

    odd = x_hi == 1
    swap_q = send(r.pack_q, r.w_q.at[(*own_slot, core)], "x", "swap_q", gives=odd, takes=odd)
    swap_o = send(r.pack_o, r.w_o.at[(*own_slot, core)], "x", "swap_o", gives=odd, takes=odd)
    mlp_pair = r.w_m.at[own_slot]
    raw_y = send(r.pack_m, r.raw.at[1, core], "y", "raw_y")
    raw_c0 = send(r.pack_m, r.raw.at[0, core], "c", "raw_c0", gives=lends == 1, takes=lends == 0)
    raw_c1 = later(r.raw.at[1, core], r.raw.at[1, core], "c", "raw_c1", gives=lends == 1, takes=lends == 0)
    mlp_to_x = later(r.raw.at[1 - kx], mlp_pair, "x", "mlp_x", gives=lends == 0, takes=lends == 1)

    def square_gather(buf):
        def half(k, n):
            return buf.at[square(k), pl.ds(128 * n, 128)]

        x0 = send(half(0, 0), half(0, 0), "x", "sg_x0")
        y1 = send(half(0, 1), half(0, 1), "y", "sg_y1")
        x1 = later(half(0, 1), half(0, 1), "x", "sg_x1")
        y0 = later(half(0, 0), half(0, 0), "y", "sg_y0")
        fy = later(half(1, 0), half(1, 0), "y", "sg_fy")
        fx = later(half(2, 1), half(2, 1), "x", "sg_fx")

        def second():
            x1.start()
            y0.start()

        def forward():
            x0.wait_recv()
            fy.start()
            y1.wait_recv()
            fx.start()

        return second, forward, x1, y0, [fx, fy]

    a_second, a_forward, a_x1, a_y0, a_far = square_gather(r.a_full)
    gather = {kind: [gather_later(kind, step) for step in range(4)] for kind in "qow"}
    to_core = {kind: [core_later(kind, late) for late in (False, True)] for kind in "qo"}

    def advance(kind, step):
        wait_recv(gather[kind][step - 1])
        start(gather[kind][step])

    swap_q.wait_recv()
    start(gather["q"][0])
    raw_y.wait_recv()
    raw_c1.start()
    swap_o.wait_recv()
    advance("q", 1)
    start(gather["o"][0])
    raw_c0.wait_recv()
    raw_c1.wait_recv()
    mlp_to_x.start()
    advance("q", 2)
    advance("o", 1)
    a_forward()

    @pl.when(lends == 0)
    def _():
        r.w_m[own_view] = r.raw[pl.ds(kx, 1)].reshape(1, 1, 1, 1, 2, 64, MW)

    advance("q", 3)
    start(to_core["q"][0])
    advance("o", 2)
    mlp_to_x.wait_recv()
    start(gather["w"][0])
    a_second()
    wait_recv(gather["q"][3])
    start(to_core["q"][1])
    advance("o", 3)
    start(to_core["o"][0])
    advance("w", 1)
    wait_recv(to_core["q"][0])
    wait_recv(to_core["q"][1])

    def w_qkv(g):
        return r.w_q[g].reshape(WIDTH, QKV)

    def w_out(g):
        return r.w_o[g].reshape(WIDTH, OW)

    def w_gu(g):
        return r.w_m[g, :, :, :, :, :, 0 : 2 * HID].reshape(WIDTH, 2 * HID)

    def w_dn(g):
        return r.w_dn[g]

    c_pair = later(r.c_full.at[group(0)], r.c_full.at[core + 2], pair, "cot_p")
    c_core = later(r.c_full.at[group(0)], r.c_full.at[group(0)], "c", "cot_c")

    first_half = lax.broadcasted_iota(jnp.int32, (ROWS, HEAD), 1) < HEAD // 2

    def turns(blk):
        table = r.rope[blk]
        swapped = pltpu.roll(table, 64, 1)
        return jnp.where(first_half, table, swapped), jnp.where(first_half, -swapped, table)

    def qkv_block(k, carry):
        @pl.when(k == 1)
        def _():
            a_x1.wait_recv()
            c_pair.start()
            c_core.start()

        @pl.when(k == 2)
        def _():
            a_y0.wait_recv()
            wait_recv(gather["o"][3])
            start(to_core["o"][1])
            advance("w", 2)

        @pl.when(k == 3)
        def _():
            wait_recv(a_far)

        blk = square(k)
        rows = r.a_full[blk]
        cos, sin = turns(blk)
        for g in range(2):
            acc = dot_nn(rows, w_qkv(g))
            r.qkp[g, blk] = acc[:, :384]
            for h in range(3):
                pre = acc[:, h * HEAD : (h + 1) * HEAD]
                normed = pre * row_scale(pre) * (key_gain if h == 2 else query_gain)
                turned = normed * cos + pltpu.roll(normed, 64, 1) * sin
                if h == 2:
                    r.ks[g, blk] = turned.astype(BF16)
                    r.kt[g, blk] = turned.T.astype(BF16)
                else:
                    r.qs[g, blk, h * ROWS : (h + 1) * ROWS] = turned.astype(BF16)
            value = acc[:, 384:]
            r.vs[g, blk] = value.astype(BF16)
            r.vt[g, blk] = value.T.astype(BF16)
        return carry

    lax.fori_loop(0, 4, qkv_block, 0)

    key_at = lax.broadcasted_iota(jnp.int32, (ROWS, 512), 0)
    query_at = lax.broadcasted_iota(jnp.int32, (ROWS, 512), 1) % ROWS
    visible = key_at <= query_at

    def weights_t(g, i, j, diagonal):
        scores = dot_nt(r.ks[g, j], r.qs[g, i])
        exps = jnp.exp2(scores * EXP_SCALE)
        if diagonal:
            exps = jnp.where(visible, exps, 0.0)
        return exps

    def attend_step(i, j, carry, diagonal):
        out = []
        for g in range(2):
            total, acc = carry[g]
            exps = weights_t(g, i, j, diagonal)
            total = total + jnp.sum(exps, axis=0, keepdims=True)
            acc = acc + dot_nn(r.vt[g, j], exps.astype(BF16))
            out.append((total, acc))
        return tuple(out)

    def attend_block(i):
        zero = (jnp.zeros((1, 512), F32), jnp.zeros((HEAD, 512), F32))
        state = lax.fori_loop(0, i, lambda j, s: attend_step(i, j, s, False), (zero, zero))
        state = attend_step(i, i, state, True)
        for g in range(2):
            total, acc = state[g]
            inv = 1.0 / total
            r.linv[g, i] = jnp.broadcast_to(inv, (8, 512))
            r.os[g, i] = (acc * inv).T.astype(BF16)

    def part_o(blk):
        acc = jnp.zeros((ROWS, WIDTH), F32)
        for g in range(2):
            heads = r.os[g, blk]
            acc = acc + dot_nt(jnp.concatenate([heads[:ROWS], heads[ROWS:]], axis=1), w_out(g))
        return acc

    def square_sum(part_of, steps):
        def out(n, rows, buf, to, key):
            return later(r.stage.at[n, pl.ds(*rows)], buf, to, key)

        low, high = (0, 128), (128, 128)
        d0 = out(2, low, r.far.at[0], "x", "ss_d0")
        d1 = out(2, high, r.far.at[1], "y", "ss_d1")
        x0 = out(0, low, r.near.at[0, pl.ds(*low)], "x", "ss_x0")
        x1 = out(0, high, r.near.at[0, pl.ds(*high)], "x", "ss_x1")
        y0 = out(1, low, r.near.at[1, pl.ds(*low)], "y", "ss_y0")
        y1 = out(1, high, r.near.at[1, pl.ds(*high)], "y", "ss_y1")

        def block(n, carry):
            k = jnp.where(n == 0, 3, n % 3)
            for value, act in steps.items():
                at(n, value, act)
            acc = part_of(square(k))

            @pl.when(n < 3)
            def _():
                r.stage[(n + 2) % 3] = acc.astype(BF16)

            @pl.when(n == 3)
            def _():
                r.own[...] = acc

            @pl.when(n == 0)
            def _():
                d0.start()
                d1.start()

            at(n, 2, x0.start)
            at(n, 3, y1.start)
            return carry

        lax.fori_loop(0, 4, block, 0)

        def relay():
            d1.wait_recv()
            r.stage[0, 128:256] = (r.stage[0, 128:256].astype(F32) + r.far[1].astype(F32)).astype(BF16)
            x1.start()
            d0.wait_recv()
            r.stage[1, 0:128] = (r.stage[1, 0:128].astype(F32) + r.far[0].astype(F32)).astype(BF16)
            y0.start()

        def finish():
            wait_recv([x0, y1, x1, y0])
            return r.own[...] + r.near[0].astype(F32) + r.near[1].astype(F32)

        return relay, finish

    def attend_and_part(blk):
        attend_block(blk)

        @pl.when(blk == square(3))
        def _():
            wait_recv(to_core["o"][0])
            wait_recv(to_core["o"][1])

        return part_o(blk)

    o_relay, o_finish = square_sum(attend_and_part, {3: lambda: advance("w", 3)})
    o_relay()
    r.dk[...] = jnp.zeros((2, 4, ROWS, HEAD), F32)
    r.dv[...] = jnp.zeros((2, 4, ROWS, HEAD), F32)
    c_pair.wait_recv()
    c_forward = send(r.c_full.at[core + 2], r.c_full.at[core + 2], "c", "cot_f")
    resid = rows_in() + o_finish()
    r.resid[...] = resid
    normed = (resid * row_scale(resid) * mlp_gain).astype(BF16)
    for half in range(2):
        r.m_full[0, pl.ds(core, 1), half] = normed[:, 512 * half : 512 * half + 512].reshape(1, 2, 2, 64, 512)
    m_pair = []
    m_forward = []
    for n in range(2):
        near_rows, far_rows = (r.m_full.at[place, core, :, n] for place in range(2))
        m_pair.append(send(near_rows, far_rows, pair, ("m_p", n)))
        m_forward.append(later(far_rows, far_rows, "c", ("m_f", n)))
    m_core = send(r.m_full.at[0, core], r.m_full.at[0, core], "c", "m_c")
    wait_recv(gather["w"][3])
    r.w_dn[...] = r.w_m[:, :, :, :, :, :, 2 * HID : MW].reshape(2, WIDTH, HID)
    wait_recv([c_core, c_forward])

    def mlp_block(k, carry):
        at(k, 1, m_core.wait_recv)

        @pl.when(k == 2)
        def _():
            for n in range(2):
                m_pair[n].wait_recv()
                m_forward[n].start()

        @pl.when(k == 3)
        def _():
            wait_recv(m_forward)

        i = group(k)
        rows = jnp.concatenate([r.m_full[i // 2, i % 2, half].reshape(ROWS, 512) for half in range(2)], axis=1)
        cots = r.c_full[i]
        for g in range(2):
            pre = dot_nn(rows, w_gu(g))
            grad = dot_nn(cots, w_dn(g))
            gate = pre[:, :HID]
            up = pre[:, HID:]
            sig = 1.0 / (1.0 + jnp.exp(-gate))
            act = gate * sig
            r.hid[g, i] = (act * up).astype(BF16)
            r.dgu[g, i, :, 0:HID] = (grad * up * sig * (1.0 + gate * (1.0 - sig))).astype(BF16)
            r.dgu[g, i, :, HID : 2 * HID] = (grad * act).astype(BF16)
        return carry

    def pair_sum(part_of, recv, own, name, hold):
        stage = r.stage
        s3 = later(stage.at[2], recv.at[0], "c", (name, 3))
        s1 = later(stage.at[0], recv.at[1], "c", (name, 1))
        s2 = later(stage.at[1], recv.at[2], pair, (name, 2))

        def block(n, carry):
            acc = part_of(group(n + (n // 2) * (5 - 2 * n)))

            @pl.when(n == 0)
            def _():
                own[...] = own[...] + acc if hold else acc

            @pl.when(n == 1)
            def _():
                stage[0] = acc.astype(BF16)
                s1.start()

            @pl.when(n == 2)
            def _():
                stage[2] = acc.astype(BF16)
                s3.start()

            @pl.when(n == 3)
            def _():
                s3.wait_recv()
                stage[1] = (acc + recv[0].astype(F32)).astype(BF16)
                if not hold:
                    s2.start()

            return carry

        def finish():
            wait_recv([s1, s2])
            return own[...] + recv[1].astype(F32) + recv[2].astype(F32)

        return block, finish, s2

    def part_dm(i):
        return dot_nt(r.dgu[0, i], w_gu(0)) + dot_nt(r.dgu[1, i], w_gu(1))

    def part_down(i):
        return dot_nt(r.hid[0, i], w_dn(0)) + dot_nt(r.hid[1, i], w_dn(1))

    dm_block, dm_finish, _ = pair_sum(part_dm, r.sum_m, r.own, "dm", False)
    flush()
    lax.fori_loop(0, 2, mlp_block, 0)
    lax.fori_loop(0, 2, dm_block, 0)
    lax.fori_loop(2, 4, mlp_block, 0)
    lax.fori_loop(2, 4, dm_block, 0)

    def mlp_grads(p, carry):
        cols = pl.ds(pl.multiple_of(256 * p, 256), 256)
        half_cols = pl.ds(pl.multiple_of(256 * (p % 2), 256), 256)
        rows_t = r.m_full[:, :, p // 2, :, :, :, half_cols].reshape(SEQ, 256)
        cots_t = r.c_full[:, :, cols].reshape(SEQ, 256)
        for g in range(2):
            grad_gu = dot_tn(rows_t, r.dgu[g].reshape(SEQ, 2 * HID))
            grad_dn = dot_tn(cots_t, r.hid[g].reshape(SEQ, HID))
            r.w_m[g, p // 2, p % 2, :, :, :, 0 : 2 * HID] = grad_gu.reshape(2, 2, 64, 2 * HID).astype(BF16)
            r.w_m[g, p // 2, p % 2, :, :, :, 2 * HID : MW] = grad_dn.reshape(2, 2, 64, HID).astype(BF16)
        return carry

    lax.fori_loop(0, 4, mlp_grads, 0)
    back_w = {step: reduce_later("w", step) for step in range(4)}
    flush()
    start(back_w[3])

    dm = dm_finish()
    resid = r.resid[...]
    inv_m = row_scale(resid)
    scaled = dm * mlp_gain
    inner = jnp.mean(scaled * resid, axis=-1, keepdims=True)
    r.gains[...] = jnp.zeros((8, WIDTH), F32)
    r.gains[1:2] = jnp.sum(dm * resid * inv_m, axis=0, keepdims=True)
    dresid = reorder(r.cot[...].astype(F32)) + inv_m * scaled - resid * (inv_m * inv_m * inv_m * inner)
    r.input_grad[...] = resid
    r.resid[...] = dresid
    r.d_full[square(0)] = dresid.astype(BF16)
    d_second, d_forward, d_x1, d_y0, d_far = square_gather(r.d_full)
    def down_order(n):
        return jnp.where(n == 0, 2, jnp.where(n == 3, 3, n - 1))

    down_block, down_finish, down_pair = pair_sum(part_down, r.sum_d, r.input_grad, "down", True)
    lax.fori_loop(0, 4, lambda n, carry: down_block(down_order(n), carry), 0)
    d_second()

    def back_step(i, j, carry, diagonal, delta):
        out = []
        for g in range(2):
            probs = weights_t(g, i, j, diagonal) * r.linv[g, i, 0:1]
            grads = dot_nt(r.vs[g, j], r.dos[g])
            dz = (probs * (grads - delta[g])).astype(BF16)
            r.dv[g, j] += dot_nn(probs.astype(BF16), r.dos[g])
            r.dk[g, j] += dot_nn(dz, r.qs[g, i])
            out.append(carry[g] + dot_nn(r.kt[g, j], dz))
        return tuple(out)

    def unnorm(pre, gain, grad):
        inv = row_scale(pre)
        hat = pre * inv
        scaled = grad * gain
        back = inv * (scaled - hat * jnp.mean(scaled * hat, axis=-1, keepdims=True))
        return back.astype(BF16), jnp.sum(grad * hat, axis=0, keepdims=True)

    def turn_back(grad, blk):
        cos, sin = turns(blk)
        return grad * cos - pltpu.roll(grad, 64, 1) * sin

    def back_block(k, gain_sum):
        @pl.when(k == 1)
        def _():
            d_forward()
            d_x1.wait_recv()

        @pl.when(k == 2)
        def _():
            d_y0.wait_recv()
            reduce_add("w", 3, back_w[3])
            start(back_w[2])

        @pl.when(k == 3)
        def _():
            wait_recv(d_far)
            down_pair.start()

        i = square(k)
        rows = r.d_full[i]
        delta = []
        for g in range(2):
            grad = dot_nn(rows, w_out(g))
            inner = []
            for h in range(2):
                part = grad[:, h * HEAD : (h + 1) * HEAD].astype(BF16)
                r.dos[g, h * ROWS : (h + 1) * ROWS] = part
                prod = part.astype(F32) * r.os[g, i, h * ROWS : (h + 1) * ROWS].astype(F32)
                inner.append(jnp.sum(prod.T, axis=0, keepdims=True))
            delta.append(jnp.concatenate(inner, axis=1))
        zero = jnp.zeros((HEAD, 512), F32)
        state = lax.fori_loop(0, i, lambda j, s: back_step(i, j, s, False, delta), (zero, zero))
        state = back_step(i, i, state, True, delta)
        for g in range(2):
            for h in range(2):
                grad = turn_back(state[g][:, h * ROWS : (h + 1) * ROWS].T * SCORE_SCALE, i)
                low, part = unnorm(r.qkp[g, i, :, h * HEAD : (h + 1) * HEAD], query_gain, grad)
                r.dgu[g, i, :, h * HEAD : (h + 1) * HEAD] = low
                gain_sum = gain_sum + part
        return gain_sum

    q_gain_part = lax.fori_loop(0, 4, back_block, jnp.zeros((1, HEAD), F32))

    other = pl.ds(flip(core), 1)
    whole = (both, both, both, both)

    def core_sum(kind, buf, copy):
        copy.wait_recv()
        index = (*whole, lane)
        total = grads[kind][index].astype(F32) + buf[...].astype(F32)
        grads[kind][index] = total.astype(BF16)

    def out_grads(p, carry):
        cols = pl.ds(pl.multiple_of(256 * p, 256), 256)
        grads_t = r.d_full[:, :, cols].reshape(SEQ, 256)
        for g in range(2):
            heads = r.os[g]
            mixed = jnp.concatenate(
                [heads[:, :ROWS].reshape(SEQ, HEAD), heads[:, ROWS:].reshape(SEQ, HEAD)], axis=1
            )
            r.w_o[g, p // 2, p % 2] = dot_tn(grads_t, mixed).reshape(2, 2, 64, OW).astype(BF16)
        return carry

    reduce_add("w", 2, back_w[2])
    start(back_w[1])

    def key_block(j, gain_sum):
        for g in range(2):
            grad = turn_back(r.dk[g, j] * SCORE_SCALE, j)
            low, part = unnorm(r.qkp[g, j, :, 256:384], key_gain, grad)
            r.dgu[g, j, :, 256:384] = low
            r.dgu[g, j, :, 384:512] = r.dv[g, j].astype(BF16)
            gain_sum = gain_sum + part
        return gain_sum

    k_gain_part = lax.fori_loop(0, 4, key_block, jnp.zeros((1, HEAD), F32))
    r.gains[2:3, 0:HEAD] = q_gain_part
    r.gains[2:3, HEAD : 2 * HEAD] = k_gain_part

    def qkv_grads(p, carry):
        cols = pl.ds(pl.multiple_of(256 * p, 256), 256)
        rows_t = r.a_full[:, :, cols].reshape(SEQ, 256)
        for g in range(2):
            grad = dot_tn(rows_t, r.dgu[g, :, :, 0:QKV].reshape(SEQ, QKV))
            r.m_full[g, p // 2, p % 2] = grad.reshape(2, 2, 64, QKV).astype(BF16)
        return carry

    sum_pair = r.w_m.at[own_slot]
    back_x = later(sum_pair, r.mlp_x, "x", "mlp_x", gives=lends == 1, takes=lends == 0)
    back_y0 = later(r.mlp_x, r.raw.at[0], "y", "raw_y", gives=role == 0, takes=role == 0)
    back_y1 = later(sum_pair, r.raw.at[0], "y", "raw_y", gives=role == 1, takes=role == 1)
    mlp_back_c = later(r.mlp_sum.at[flip(core)], r.mlp_c, "c", "raw_c0", gives=lends == 0, takes=lends == 1)

    lax.fori_loop(0, 4, qkv_grads, 0)
    flush()
    q_core = send(r.m_full.at[(*whole, other)], r.core_q, "c", "q_core")

    def part_da(blk):
        acc = dot_nt(r.dgu[0, blk, :, 0:QKV], w_qkv(0)) + dot_nt(r.dgu[1, blk, :, 0:QKV], w_qkv(1))
        r.gains[0:1] += jnp.sum(acc * r.a_full[blk].astype(F32), axis=0, keepdims=True)
        return acc

    back_o = {step: reduce_later("o", step) for step in range(4)}
    back_q = {step: reduce_later("q", step) for step in range(4)}

    def tail_q():
        core_sum("q", r.core_q, q_core)
        start(back_q[3])

    a_relay, a_finish = square_sum(part_da, {3: tail_q})
    lax.fori_loop(0, 4, out_grads, 0)
    o_core = send(r.w_o.at[(*whole, other)], r.core_o, "c", "o_core")

    gain_links = ["c", "za", "zb", "yo", "xo", "y", "x"]

    def gain_send(n):
        return send(r.gains, r.gain_in.at[n], gain_links[n], ("gain", n))

    def gain_add(n, copy):
        copy.wait_send()
        copy.wait_recv()
        r.gains[...] += r.gain_in[n]

    def reduce_next(kind, step, back):
        reduce_add(kind, step, back[step])
        start(back[step - 1])

    g_step = gain_send(0)
    reduce_next("w", 1, back_w)
    gain_add(0, g_step)
    g_step = gain_send(1)
    core_sum("o", r.core_o, o_core)
    start(back_o[3])
    a_relay()
    reduce_next("q", 3, back_q)
    reduce_next("o", 3, back_o)
    gain_add(1, g_step)
    g_step = gain_send(2)
    reduce_add("w", 0, back_w[0])
    back_x.start()
    back_y1.start()
    r.layer_out[...] = reorder(down_finish()).astype(BF16)
    gain_add(2, g_step)
    g_step = gain_send(3)
    reduce_next("q", 2, back_q)
    reduce_next("o", 2, back_o)
    gain_add(3, g_step)
    g_step = gain_send(4)
    reduce_next("q", 1, back_q)
    reduce_next("o", 1, back_o)

    def last_step(kind, group, cols):
        for part in range(4):
            rows = pl.ds(16 * part, 16)
            group[part].wait_recv()
            total = grads[kind][(*own_view, lane, rows)].astype(F32) + getattr(r, f"sum_{kind}_{part}_0")[...].astype(F32)
            r.attn_sum[16 * part : 16 * part + 16, cols] = total.reshape(16, -1)
        r.attn_low[:, cols] = r.attn_sum[:, cols].astype(BF16)

    back_x.wait_recv()
    back_y0.start()
    gain_add(4, g_step)
    g_step = gain_send(5)
    last_step("q", back_q[0], slice(0, QKV))
    last_step("o", back_o[0], slice(QKV, AW))
    attn_back = send(r.attn_low, r.attn_x, "x", "swap_q", gives=odd, takes=odd)
    rows_x = rows_in()
    inv_a = row_scale(rows_x)
    scaled = a_finish() * attn_gain
    inner = jnp.mean(scaled * rows_x, axis=-1, keepdims=True)
    r.input_grad[...] = reorder(r.resid[...] + inv_a * scaled - rows_x * (inv_a * inv_a * inv_a * inner))
    gain_add(5, g_step)
    g_step = gain_send(6)
    back_y0.wait_recv()
    back_y1.wait_recv()

    @pl.when(role == 0)
    def _():
        r.mlp_sum[...] = sum_pair[...].astype(F32) + r.raw[0].astype(F32)

    @pl.when(role == 1)
    def _():
        r.mlp_sum[...] = r.mlp_x[...].astype(F32) + r.raw[0].astype(F32)

    mlp_back_c.start()

    @pl.when(lends == 0)
    def _():
        r.d_mlp[...] = r.mlp_sum[core]

    @pl.when(x_hi == 0)
    def _():
        r.d_attn[...] = r.attn_sum[...]

    attn_back.wait_recv()

    @pl.when(odd)
    def _():
        r.d_attn[...] = r.attn_x[...].astype(F32)

    mlp_back_c.wait_recv()

    @pl.when(lends == 1)
    def _():
        r.d_mlp[...] = r.mlp_c[...]

    gain_add(6, g_step)
    sums = r.gains[...]
    r.d_gain[...] = reorder(sums)
    r.d_gain[0:1] = reorder(sums[0:1] / attn_gain)
    r.d_gain[2:3] = sums[2:3]
    flush()


def unpack(*refs):
    layer_in, input_in, d_attn, d_mlp, d_gain = refs[:5]
    (
        layer_out,
        input_grad,
        attn_gain,
        w_query,
        w_key,
        w_value,
        query_gain,
        key_gain,
        w_out,
        mlp_gain,
        w_gate,
        w_up,
        w_down,
    ) = refs[5:18]
    layer_out[...] = layer_in[...]
    input_grad[...] = input_in[...]
    attn_gain[...] = d_gain[0]
    mlp_gain[...] = d_gain[1]
    query_gain[...] = d_gain[2, 0:HEAD]
    key_gain[...] = d_gain[2, HEAD : 2 * HEAD]
    w_query[...] = d_attn[:, 0:256]
    w_key[...] = d_attn[:, 256:384]
    w_value[...] = d_attn[:, 384:512]
    w_out[...] = d_attn[:, 512:768]
    w_gate[...] = d_mlp[:, 0:HID]
    w_up[...] = d_mlp[:, HID : 2 * HID]
    w_down[...] = d_mlp[:, 2 * HID : MW]


def rope_table():
    position = np.arange(SEQ, dtype=np.float32)[:, None]
    channel = np.arange(HEAD // 2, dtype=np.float32)[None, :]
    rate = np.exp(channel * np.float32(-2.0 * math.log(ROPE_BASE) / HEAD)).astype(np.float32)
    angle = (position * rate).astype(np.float32).astype(np.float64)
    cos = np.cos(angle).astype(np.float32)
    sin = np.sin(angle).astype(np.float32)
    return np.concatenate([cos, sin], axis=1).reshape(4, ROWS, HEAD)


def body(
    tokens,
    attn_gain,
    w_query,
    key_weight,
    value_weight,
    query_gain,
    key_gain,
    w_out,
    mlp_gain,
    w_gate,
    w_up,
    w_down,
    out_cotangent,
):
    vmem = pl.BlockSpec(memory_space=pltpu.VMEM)

    def out(*shape):
        return jax.ShapeDtypeStruct(shape, F32)

    packed = pl.pallas_call(
        kernel,
        out_shape=(
            jax.ShapeDtypeStruct((ROWS, WIDTH), BF16),
            out(ROWS, WIDTH),
            out(64, AW),
            out(64, MW),
            out(8, WIDTH),
        ),
        in_specs=[vmem] * len(INPUTS),
        out_specs=(vmem,) * len(OUTPUTS),
        scratch_shapes=[pltpu.VMEM(*SCRATCH[name]) for name in NAMES]
        + [pltpu.SemaphoreType.DMA((N_SEM,)), pltpu.SemaphoreType.DMA((N_SEM,))],
        compiler_params=pltpu.CompilerParams(
            collective_id=0, has_side_effects=True, vmem_limit_bytes=64 * 2**20 - 2**17
        ),
        name="layer",
    )(
        tokens,
        out_cotangent,
        w_query,
        key_weight,
        value_weight,
        w_out.T,
        w_gate,
        w_up,
        w_down.T,
        attn_gain,
        mlp_gain,
        query_gain,
        key_gain,
        jnp.asarray(rope_table()),
    )
    parts = list(pl.pallas_call(
        unpack,
        out_shape=[
            jax.ShapeDtypeStruct((ROWS, WIDTH), BF16),
            out(ROWS, WIDTH),
            out(WIDTH),
            out(64, 256),
            out(64, HEAD),
            out(64, HEAD),
            out(HEAD),
            out(HEAD),
            out(64, 256),
            out(WIDTH),
            out(64, HID),
            out(64, HID),
            out(64, HID),
        ],
        in_specs=[vmem] * 5,
        out_specs=[vmem] * 13,
        name="unpack",
    )(*packed))
    parts[8] = parts[8].T
    parts[12] = parts[12].T
    return tuple(parts)


def solution(mesh):
    rows = P(("dp", "tensor"), None)
    first = P("dp", "tensor")
    second = P("tensor", "dp")
    whole = P()
    return jax.shard_map(
        body,
        mesh=mesh,
        in_specs=(
            rows,
            whole,
            first,
            first,
            first,
            whole,
            whole,
            second,
            whole,
            first,
            first,
            second,
            rows,
        ),
        out_specs=(
            rows,
            rows,
            whole,
            first,
            first,
            first,
            whole,
            whole,
            second,
            whole,
            first,
            first,
            second,
        ),
        check_vma=False,
    )
```
